32 devices in a mesh: img: 8 (over z, y), rows: 4 (over x, core).
Axes of the slice: x: 2, y: 2, z: 4, core: 2. Of those that a mesh axis runs over, the one named last changes fastest.
Arguments:
- features: bfloat16 [128, 8, 8, 2048], P('img', 'rows'), may hold values from -6 to 6
- weight_in: bfloat16 [2048, 512], replicated, may hold values from -0.125 to 0.125
- gain_in: float32 [512], replicated, may hold values from 0.5 to 1.5
- bias_in: float32 [512], replicated, may hold values from -0.5 to 0.5
- weight_mid: bfloat16 [3, 3, 512, 512], replicated, may hold values from -0.09375 to 0.09375
- gain_mid: float32 [512], replicated, may hold values from 0.5 to 1.5
- bias_mid: float32 [512], replicated, may hold values from -0.5 to 0.5
- weight_out: bfloat16 [512, 2048], replicated, may hold values from -0.25 to 0.25
- gain_out: float32 [2048], replicated, may hold values from 0.5 to 1.5
- bias_out: float32 [2048], replicated, may hold values from -0.5 to 0.5
- map_size: int32 [128], P('img'), may hold values from 5 to 7
- out_grad: bfloat16 [128, 8, 8, 2048], P('img', 'rows'), may hold values from -6 to 6
- pool_grad: float32 [128, 2048], P('img'), may hold values from -24 to 24
Outputs:
- block_out: bfloat16 [128, 8, 8, 2048], P('img', 'rows')
- pooled: float32 [128, 2048], P('img')
- grad_features: float32 [128, 8, 8, 2048], P('img', 'rows')
- grad_weight_in: float32 [2048, 512], replicated
- grad_gain_in: float32 [512], replicated
- grad_bias_in: float32 [512], replicated
- grad_weight_mid: float32 [3, 3, 512, 512], replicated
- grad_gain_mid: float32 [512], replicated
- grad_bias_mid: float32 [512], replicated
- grad_weight_out: float32 [512, 2048], replicated
- grad_gain_out: float32 [2048], replicated
- grad_bias_out: float32 [2048], replicated
The draws below stay inside these ranges and needn't reach their ends.
Inputs may be any that keep to these rules, and one draw needn't show every extreme that they name: Each image's map fills the first map_size rows and columns of its 8 x 8 array; the rest is padding.
All inputs are finite; a program needn't handle non-finite values.
Results may differ from the reference program's by a relative error of at most 0.008.
Values may be sent and summed in bfloat16 or wider, within the bound.
No kernel may reach another device: no remote copies, remote signals or barrier semaphores. Data moves between devices by JAX's collectives and lax.ppermute only.
A program may use at most 128 MiB of HBM per device.

```python
import jax
import jax.numpy as jnp
from jax import lax

CIN = 2048
MID = 512
MAP = 8
IMAGES = 128


def place_ends(entries, rng, least, top_value):
    longest = entries.shape.index(max(entries.shape))
    spots = []
    for shift in (0, 1):
        where = [jax.random.randint(jax.random.fold_in(rng, axis), (), 0, length) for axis, length in enumerate(entries.shape)]
        where[longest] = (where[longest] + shift) % entries.shape[longest]
        spots.append(tuple(where))
    return entries.at[spots[0]].set(least).at[spots[1]].set(top_value)


def shard_levels(key, shape, shards, low, top_value):
    level, own = 1.0, jax.random.fold_in(key, 6)
    for dim, blocks in shards:
        steps = jnp.exp(jax.random.uniform(jax.random.fold_in(own, dim), (blocks,), jnp.float32, low / len(shards), top_value / len(shards)))
        level = level * jnp.repeat(steps, shape[dim] // blocks).reshape([-1 if axis == dim else 1 for axis in range(len(shape))])
    return level


def scatter_about(rng, dims, width, bound, shards=(), kind=jnp.bfloat16):
    drawn = jax.random.normal(rng, dims, jnp.float32) * width
    if len(shards) > 0:
        drawn = shard_levels(rng, dims, shards, -0.22, 0.18) * drawn
    return jnp.clip(drawn, min=-bound, max=bound).astype(kind)


def setup_inputs(seed: int = 0) -> dict:
    seeds = jax.random.split(jax.random.key(seed), 14)
    return {
        "features": scatter_about(seeds[0], (IMAGES, MAP, MAP, CIN), 1.0, 6.0, ((0, 8), (1, 4))),
        "weight_in": scatter_about(seeds[1], (CIN, MID), CIN ** -0.5, 0.125),
        "gain_in": jnp.clip(jax.random.uniform(seeds[2], (MID,), jnp.float32, 0.5, 1.5), 0.5, 1.5),
        "bias_in": jnp.clip(jax.random.uniform(seeds[3], (MID,), jnp.float32, -0.5, 0.5), -0.5, 0.5),
        "weight_mid": scatter_about(seeds[4], (3, 3, MID, MID), (9 * MID) ** -0.5, 0.09375),
        "gain_mid": jnp.clip(jax.random.uniform(seeds[5], (MID,), jnp.float32, 0.5, 1.5), 0.5, 1.5),
        "bias_mid": jnp.clip(jax.random.uniform(seeds[6], (MID,), jnp.float32, -0.5, 0.5), -0.5, 0.5),
        "weight_out": scatter_about(seeds[7], (MID, CIN), MID ** -0.5, 0.25),
        "gain_out": jnp.clip(jax.random.uniform(seeds[8], (CIN,), jnp.float32, 0.5, 1.5), 0.5, 1.5),
        "bias_out": jnp.clip(jax.random.uniform(seeds[9], (CIN,), jnp.float32, -0.5, 0.5), -0.5, 0.5),
        "map_size": place_ends(jax.random.randint(seeds[10], (IMAGES,), 5, MAP), jax.random.fold_in(seeds[10], 1), 5, MAP - 1).astype(jnp.int32),
        "out_grad": scatter_about(seeds[11], (IMAGES, MAP, MAP, CIN), 1.0, 6.0, ((0, 8), (1, 4))),
        "pool_grad": scatter_about(seeds[12], (IMAGES, CIN), 4.0, 24.0, ((0, 8),), jnp.float32),
    }


EPSILON = 1e-05

@jax.custom_vjp
def low(v):
    return lax.optimization_barrier(v.astype(jnp.bfloat16)).astype(jnp.float32)

@jax.custom_vjp
def low_back(v):
    return v

def low_keep(v):
    return (low(v), None)

def low_pass(kept, grad):
    return (grad,)

def back_keep(v):
    return (v, None)

def back_low(kept, grad):
    return (low(grad),)
low.defvjp(low_keep, low_pass)
low_back.defvjp(back_keep, back_low)

def smooth(values):
    return jax.nn.silu(values)

def reference(features, weight_in, gain_in, bias_in, weight_mid, gain_mid, bias_mid, weight_out, gain_out, bias_out, map_size, out_grad, pool_grad):
    position = jnp.arange(MAP)
    sizes_col = map_size[:, None, None]
    inside = ((position[None, :, None] < sizes_col) & (position[None, None, :] < sizes_col)).astype(jnp.float32)[..., None]
    map_area = (map_size * map_size).astype(jnp.float32)[:, None]
    pixel_count = jnp.sum(inside)
    highest = lax.Precision.HIGHEST

    def normalize(hidden, gain, shift):
        average = lax.optimization_barrier(jnp.sum(hidden * inside, axis=(0, 1, 2))) / pixel_count
        variance = lax.optimization_barrier(jnp.sum(hidden * hidden * inside, axis=(0, 1, 2))) / pixel_count - average * average
        return gain * ((hidden - average) * lax.rsqrt(variance + EPSILON)) + shift

    def forward(source, w_in, g_in, s_in, w_mid, g_mid, s_mid, w_out, g_out, s_out):
        first = low_back(jnp.einsum('nhwc,cd->nhwd', source, w_in, precision=highest))
        first_act = low(smooth(normalize(first, g_in, s_in)) * inside)
        second = low_back(lax.conv_general_dilated(first_act, w_mid, (1, 1), ((1, 1), (1, 1)), dimension_numbers=('NHWC', 'HWIO', 'NHWC'), precision=highest))
        second_act = low(smooth(normalize(second, g_mid, s_mid)) * inside)
        third = low_back(jnp.einsum('nhwc,cd->nhwd', second_act, w_out, precision=highest))
        result = smooth(normalize(third, g_out, s_out) + source) * inside
        pooled = lax.optimization_barrier(jnp.sum(result, axis=(1, 2))) / map_area
        return (result, pooled)
    outputs, pullback = jax.vjp(forward, features.astype(jnp.float32), weight_in.astype(jnp.float32), gain_in, bias_in, weight_mid.astype(jnp.float32), gain_mid, bias_mid, weight_out.astype(jnp.float32), gain_out, bias_out)
    gradients = pullback((out_grad.astype(jnp.float32), pool_grad))
    return (outputs[0].astype(jnp.bfloat16), outputs[1], gradients[0], gradients[1], gradients[2], gradients[3], gradients[4], gradients[5], gradients[6], gradients[7], gradients[8], gradients[9])
```

```python
import jax
import jax.numpy as jnp
from jax import lax
from jax.sharding import PartitionSpec as P

EPSILON = 1e-05

AXES = ("img", "rows")


def swap(value, flips):
    count = lax.axis_size(AXES)
    return lax.ppermute(value, AXES, [(i, i ^ flips[i & 1]) for i in range(count)])


def bits():
    count, found = lax.axis_size(AXES), []
    while (1 << len(found)) < count:
        found.append(1 << len(found))
    return found


def sum_all(value):
    for bit in bits():
        value = value + swap(value, (bit, bit))
    return value


def flat_index():
    return lax.axis_index("img") * lax.axis_size("rows") + lax.axis_index("rows")


def plan():
    order = bits()
    steps = [(bit, bit) for bit in order]
    if len(order) >= 3:
        steps[1], steps[2] = (order[1], order[2]), (order[2], order[1])
    index = flat_index()
    low = index % 2
    chosen = []
    for even, odd in steps:
        chosen.append(((even, odd), jnp.where(low == 0, index // even % 2, index // odd % 2)))
    return chosen


def sum_scatter(value):
    for flips, mine in plan():
        halves = value.reshape((2, value.shape[0] // 2) + value.shape[1:])
        sent = lax.dynamic_index_in_dim(halves, 1 - mine, 0, keepdims=False).astype(jnp.bfloat16)
        kept = lax.dynamic_index_in_dim(halves, mine, 0, keepdims=False)
        value = kept + swap(sent, flips).astype(jnp.float32)
    return value


def gather_back(value):
    value = value.astype(jnp.bfloat16)
    half = jnp.arange(2).reshape((2,) + (1,) * value.ndim)
    for flips, mine in reversed(plan()):
        other = swap(value, flips)
        value = jnp.where(half == mine, value[None], other[None]).reshape((-1,) + value.shape[1:])
    return value.astype(jnp.float32)


def sum_weights(value):
    return gather_back(sum_scatter(value))


def with_halo(block, sides, width):
    for axis, dim in sides:
        count = lax.axis_size(axis)
        forward = [(i, i + 1) for i in range(count - 1)]
        backward = [(target, source) for source, target in forward]
        low = lax.ppermute(
            lax.slice_in_dim(block, block.shape[dim] - width, None, axis=dim), axis, forward
        )
        high = lax.ppermute(lax.slice_in_dim(block, 0, width, axis=dim), axis, backward)
        block = jnp.concatenate([low, block, high], axis=dim)
    return block


def flatten(tensor):
    return tensor.reshape(-1, tensor.shape[-1])


def widen(tensor):
    return jnp.pad(tensor, ((0, 0), (0, 0), (1, 1), (0, 0)))


def patches(padded, height, width):
    pieces = []
    for row_off in range(3):
        for col_off in range(3):
            pieces.append(padded[:, row_off : row_off + height, col_off : col_off + width, :])
    return jnp.concatenate(pieces, axis=3)


def contract(left, right):
    return lax.dot_general(
        flatten(left), flatten(right), (((0,), (0,)), ((), ())), preferred_element_type=jnp.float32
    )


def times_transpose(left, weights):
    return lax.dot_general(
        flatten(left), weights, (((1,), (1,)), ((), ())), preferred_element_type=jnp.float32
    )


def smooth(values):
    return jax.nn.silu(values)


def smooth_slope(values):
    logistic = jax.nn.sigmoid(values)
    return logistic * (1.0 + values * (1.0 - logistic))


def batch_stats(hidden, inside, pixel_count):
    masked = hidden * inside
    sums = jnp.stack([jnp.sum(masked, axis=(0, 1, 2)), jnp.sum(masked * hidden, axis=(0, 1, 2))])
    total, squares = sum_all(sums)
    average = total / pixel_count
    inv_std = lax.rsqrt(squares / pixel_count - average * average + EPSILON)
    return ((hidden - average) * inv_std, inv_std)


def norm_back(grad_z, normed, gain, inv_std, pixel_count, inside):
    grad_shift, grad_gain = sum_all(
        jnp.stack([jnp.sum(grad_z, axis=(0, 1, 2)), jnp.sum(grad_z * normed, axis=(0, 1, 2))])
    )
    grad_hidden = (
        inside * (gain * inv_std) * (grad_z - (grad_shift + normed * grad_gain) / pixel_count)
    )
    return (grad_hidden, grad_gain, grad_shift)


def per_device(
    features,
    weight_in,
    gain_in,
    bias_in,
    weight_mid,
    gain_mid,
    bias_mid,
    weight_out,
    gain_out,
    bias_out,
    map_size,
    out_grad,
    pool_grad,
):
    images = features.shape[0]
    height = features.shape[1]
    width = features.shape[2]
    channels_mid = weight_mid.shape[3]
    row_pos = lax.axis_index("rows") * height + jnp.arange(height)
    col_pos = jnp.arange(width)
    sizes_col = map_size[:, None, None]
    inside = ((row_pos[None, :, None] < sizes_col) & (col_pos[None, None, :] < sizes_col)).astype(
        jnp.float32
    )[..., None]
    map_area = (map_size * map_size).astype(jnp.float32)[:, None]
    pixel_count = sum_all(jnp.sum(inside))
    first = jnp.dot(flatten(features), weight_in, preferred_element_type=jnp.float32).reshape(
        images, height, width, -1
    )
    first_normed, first_std = batch_stats(first, inside, pixel_count)
    first_pre = gain_in * first_normed + bias_in
    first_act = (smooth(first_pre) * inside).astype(jnp.bfloat16)
    first_rim = with_halo(first_act, (("rows", 1),), 1)
    first_cols = patches(widen(first_rim), height, width)
    second = jnp.dot(
        flatten(first_cols),
        weight_mid.reshape(-1, channels_mid),
        preferred_element_type=jnp.float32,
    ).reshape(images, height, width, channels_mid)
    second_normed, second_std = batch_stats(second, inside, pixel_count)
    second_pre = gain_mid * second_normed + bias_mid
    second_act = (smooth(second_pre) * inside).astype(jnp.bfloat16)
    third = jnp.dot(flatten(second_act), weight_out, preferred_element_type=jnp.float32).reshape(
        images, height, width, -1
    )
    third_normed, third_std = batch_stats(third, inside, pixel_count)
    summed = gain_out * third_normed + bias_out + features.astype(jnp.float32)
    result = smooth(summed) * inside
    pooled = (
        lax.psum(jnp.sum(result, axis=(1, 2)).astype(jnp.bfloat16), "rows").astype(jnp.float32)
        / map_area
    )
    total_grad = out_grad.astype(jnp.float32) + (pool_grad / map_area)[:, None, None, :]
    grad_summed = total_grad * inside * smooth_slope(summed)
    grad_third, grad_gain_out, grad_bias_out = norm_back(
        grad_summed, third_normed, gain_out, third_std, pixel_count, inside
    )
    grad_third_low = grad_third.astype(jnp.bfloat16)
    grad_weight_out = contract(second_act, grad_third_low)
    grad_second_act = times_transpose(grad_third_low, weight_out).reshape(
        images, height, width, channels_mid
    )
    grad_second_pre = grad_second_act * inside * smooth_slope(second_pre)
    grad_second, grad_gain_mid, grad_bias_mid = norm_back(
        grad_second_pre, second_normed, gain_mid, second_std, pixel_count, inside
    )
    grad_second_low = grad_second.astype(jnp.bfloat16)
    grad_weight_mid = contract(first_cols, grad_second_low).reshape(
        3, 3, channels_mid, channels_mid
    )
    grad_rim = with_halo(grad_second_low, (("rows", 1),), 1)
    grad_cols = patches(widen(grad_rim), height, width)
    flipped = weight_mid[::-1, ::-1].transpose(0, 1, 3, 2).reshape(-1, channels_mid)
    grad_first_act = jnp.dot(
        flatten(grad_cols), flipped, preferred_element_type=jnp.float32
    ).reshape(images, height, width, channels_mid)
    grad_first_pre = grad_first_act * inside * smooth_slope(first_pre)
    grad_first, grad_gain_in, grad_bias_in = norm_back(
        grad_first_pre, first_normed, gain_in, first_std, pixel_count, inside
    )
    grad_first_low = grad_first.astype(jnp.bfloat16)
    grad_weight_in = contract(features, grad_first_low)
    grad_features = grad_summed + times_transpose(grad_first_low, weight_in).reshape(
        images, height, width, -1
    )
    grad_weight_in = sum_weights(grad_weight_in)
    grad_weight_mid = sum_weights(grad_weight_mid.reshape(-1, channels_mid)).reshape(
        3, 3, channels_mid, channels_mid
    )
    grad_weight_out = sum_weights(grad_weight_out)
    return (
        result.astype(jnp.bfloat16),
        pooled,
        grad_features,
        grad_weight_in,
        grad_gain_in,
        grad_bias_in,
        grad_weight_mid,
        grad_gain_mid,
        grad_bias_mid,
        grad_weight_out,
        grad_gain_out,
        grad_bias_out,
    )


def solution(mesh):
    placed = (
        P("img", "rows", None, None),
        P(),
        P(),
        P(),
        P(),
        P(),
        P(),
        P(),
        P(),
        P(),
        P("img"),
        P("img", "rows", None, None),
        P("img", None),
    )
    return jax.shard_map(
        per_device,
        mesh=mesh,
        in_specs=placed,
        out_specs=(
            P("img", "rows", None, None),
            P("img", None),
            P("img", "rows", None, None),
            P(),
            P(),
            P(),
            P(),
            P(),
            P(),
            P(),
            P(),
            P(),
        ),
        check_vma=False,
    )
```

```python
import jax
import jax.numpy as jnp
from jax import lax
from jax.experimental import pallas as pl
from jax.experimental.pallas import tpu as pltpu
from jax.sharding import PartitionSpec as P

EPSILON = 1e-05
AXES = ("img", "rows")
MIB = 1 << 20
LOW = jnp.bfloat16
FULL = jnp.float32
GROUP = 16


def swap(value, flips):
    count = lax.axis_size(AXES)
    return lax.ppermute(value, AXES, [(i, i ^ flips[i & 1]) for i in range(count)])


def bits():
    count, found = lax.axis_size(AXES), []
    while (1 << len(found)) < count:
        found.append(1 << len(found))
    return found


def sum_all(value):
    for bit in bits():
        value = value + swap(value, (bit, bit))
    return value


def flat_index():
    return lax.axis_index("img") * lax.axis_size("rows") + lax.axis_index("rows")


def plan():
    order = bits()
    steps = [(bit, bit) for bit in order]
    if len(order) >= 3:
        steps[1], steps[2] = (order[1], order[2]), (order[2], order[1])
    index = flat_index()
    low = index % 2
    chosen = []
    for even, odd in steps:
        chosen.append(((even, odd), jnp.where(low == 0, index // even % 2, index // odd % 2)))
    return chosen


def half_of(value, which):
    size = value.shape[0] // 2
    return lax.dynamic_slice_in_dim(value, which * size, size, axis=0)


def sum_scatter(value):
    for flips, mine in plan():
        sent = half_of(value, 1 - mine).astype(LOW)
        value = half_of(value, mine) + swap(sent, flips).astype(FULL)
    return value


def gather_back(value):
    value = value.astype(LOW)
    half = jnp.arange(2).reshape(2, 1, 1)
    for flips, mine in reversed(plan()):
        other = swap(value, flips)
        value = jnp.where(half == mine, value[None], other[None]).reshape(-1, value.shape[1])
    return value


def sum_rows_axis(value):
    count, bit = lax.axis_size("rows"), 1
    while bit < count:
        value = value + lax.ppermute(value, "rows", [(i, i ^ bit) for i in range(count)])
        bit *= 2
    return value


def rim(block):
    count = lax.axis_size("rows")
    odd = lax.axis_index("rows") % 2 == 1
    top, bottom = block[:, :1], block[:, -1:]
    first = lax.ppermute(jnp.where(odd, top, bottom), "rows", [(i, i ^ 1) for i in range(count)])
    pairs = [(i, i + 1) for i in range(1, count - 1, 2)]
    second = lax.ppermute(
        jnp.where(odd, bottom, top), "rows", pairs + [(b, a) for a, b in pairs]
    )
    return jnp.where(odd, first, second), jnp.where(odd, second, first)


def call(kernel, outs, *args):
    vmem = pl.BlockSpec(memory_space=pltpu.VMEM)
    return pl.pallas_call(
        kernel,
        out_shape=[jax.ShapeDtypeStruct(shape, kind) for shape, kind in outs],
        in_specs=[vmem] * len(args),
        out_specs=[vmem] * len(outs),
        compiler_params=pltpu.CompilerParams(vmem_limit_bytes=48 * MIB),
    )(*args)


def logistic(values):
    return 1.0 / (1.0 + jnp.exp(-values))


def slope(values):
    s = logistic(values)
    return s * (1.0 + values * (1.0 - s))


def shifted(values, by):
    return pltpu.roll(values, (-by) % values.shape[0], 0)


def spread(images, height, width, main, above, below):
    channels = main.shape[-1]
    main = main.reshape(images, height, width, channels)
    above = above.reshape(images, 1, width, channels)
    below = below.reshape(images, 1, width, channels)
    flat = (images * height * width, channels)
    return (
        jnp.concatenate([above, main[:, :-1]], axis=1).reshape(flat),
        main.reshape(flat),
        jnp.concatenate([main[:, 1:], below], axis=1).reshape(flat),
    )


def mid_forward(dims, first, above, below, mask, mask_above, mask_below, scale, shift, weight, x3, second, sums):
    def act(hidden, inside):
        pre = hidden[...] * scale[...] + shift[...]
        return pre * logistic(pre) * inside[...]

    three = spread(*dims, act(first, mask), act(above, mask_above), act(below, mask_below))
    for i in range(3):
        x3[i] = three[i].astype(LOW)
    total = None
    for j in range(3):
        part = None
        for i in range(3):
            term = jnp.dot(x3[i], weight[i, j], preferred_element_type=FULL)
            part = term if part is None else part + term
        part = shifted(part, j - 1) if j != 1 else part
        total = part if total is None else total + part
    second[...] = total
    masked = total * mask[...]
    sums[0:1] = jnp.sum(masked, axis=0, keepdims=True)
    sums[1:2] = jnp.sum(masked * total, axis=0, keepdims=True)


def mid_weights(x3, grad, total):
    groups, _, size, channels = total.shape
    for j in range(3):
        turned = grad[...].astype(FULL)
        turned = shifted(turned, 1 - j) if j != 1 else turned
        turned = turned.astype(LOW)
        for i in range(3):
            part = lax.dot_general(
                x3[i], turned, (((0,), (0,)), ((), ())), preferred_element_type=FULL
            )
            total[:, 3 * i + j] = part.reshape(groups, size, channels)


def mid_backward(dims, grad, above, below, first, mask, scale, shift, average, inv_std, weight, pre_grad, sums):
    def flat(ref):
        return ref[...].astype(FULL)

    three = spread(*dims, flat(grad), flat(above), flat(below))
    low = [part.astype(LOW) for part in three]
    total = None
    for j in range(3):
        part = None
        for i in range(3):
            term = lax.dot_general(
                low[2 - i], weight[i, j], (((1,), (1,)), ((), ())), preferred_element_type=FULL
            )
            part = term if part is None else part + term
        part = shifted(part, 1 - j) if j != 1 else part
        total = part if total is None else total + part
    hidden = first[...]
    pre = hidden * scale[...] + shift[...]
    total = total * mask[...] * slope(pre)
    pre_grad[...] = total
    normed = (hidden - average[...]) * inv_std[...]
    sums[0:1] = jnp.sum(total, axis=0, keepdims=True)
    sums[1:2] = jnp.sum(total * normed, axis=0, keepdims=True)


def dot(left, right):
    return jnp.dot(left, right, preferred_element_type=FULL)


def contract(left, right):
    return lax.dot_general(left, right, (((0,), (0,)), ((), ())), preferred_element_type=FULL)


def times_transpose(left, weights):
    return lax.dot_general(left, weights, (((1,), (1,)), ((), ())), preferred_element_type=FULL)


def both(values, others):
    return jnp.stack([jnp.sum(values, axis=0), jnp.sum(values * others, axis=0)])


def moments(sums, pixel_count):
    average = sums[0] / pixel_count
    inv_std = lax.rsqrt(sums[1] / pixel_count - average * average + EPSILON)
    return average, inv_std


def norm_back(grad_z, normed, gain, inv_std, sums, pixel_count, mask):
    return mask * (gain * inv_std) * (grad_z - (sums[0] + normed * sums[1]) / pixel_count)


def per_device(
    features,
    weight_in,
    gain_in,
    bias_in,
    weight_mid,
    gain_mid,
    bias_mid,
    weight_out,
    gain_out,
    bias_out,
    map_size,
    out_grad,
    pool_grad,
):
    images, height, width, channels = features.shape
    middle = weight_mid.shape[3]
    dims = (images, height, width)
    pixels = images * height * width

    def inside_rows(start, count):
        rows = start + jnp.arange(count)
        sizes = map_size[:, None, None]
        inside = (rows[None, :, None] >= 0) & (rows[None, :, None] < sizes)
        inside = inside & (jnp.arange(width)[None, None, :] < sizes)
        return inside.astype(FULL).reshape(-1, 1)

    start = lax.axis_index("rows") * height
    mask = inside_rows(start, height)
    mask_above = inside_rows(start - 1, 1)
    mask_below = inside_rows(start + height, 1)
    area = (map_size * map_size).astype(FULL)[:, None]
    flat_features = features.reshape(pixels, channels)

    first = dot(flat_features, weight_in)
    sums = jnp.concatenate(
        [both(first * mask, first), jnp.broadcast_to(jnp.sum(mask), (1, middle))], axis=0
    )
    above, below = rim(first.reshape(images, height, width, middle))
    sums = sum_all(sums)
    pixel_count = sums[2, 0]
    first_avg, first_std = moments(sums, pixel_count)
    first_scale = first_std * gain_in
    first_shift = bias_in - first_avg * first_scale
    x3, second, sums = call(
        lambda *refs: mid_forward(dims, *refs),
        [((3, pixels, middle), LOW), ((pixels, middle), FULL), ((2, middle), FULL)],
        first,
        above.reshape(-1, middle),
        below.reshape(-1, middle),
        mask,
        mask_above,
        mask_below,
        first_scale[None],
        first_shift[None],
        weight_mid,
    )
    second_avg, second_std = moments(sum_all(sums), pixel_count)
    second_normed = (second - second_avg) * second_std
    second_pre = gain_mid * second_normed + bias_mid
    second_act = (second_pre * logistic(second_pre) * mask).astype(LOW)
    third = dot(second_act, weight_out)
    third_avg, third_std = moments(sum_all(both(third * mask, third)), pixel_count)
    third_normed = (third - third_avg) * third_std
    summed = gain_out * third_normed + bias_out + flat_features.astype(FULL)
    gate = logistic(summed)
    result = summed * gate * mask
    pooled = jnp.sum(result.reshape(images, height * width, channels), axis=1)
    pooled = sum_rows_axis(pooled.astype(LOW).astype(FULL)) / area

    total_grad = out_grad.astype(FULL) + (pool_grad / area)[:, None, None, :]
    grad_summed = total_grad.reshape(pixels, channels) * mask * (gate * (1.0 + summed * (1.0 - gate)))
    sums_out = sum_all(both(grad_summed, third_normed))
    grad_third = norm_back(
        grad_summed, third_normed, gain_out, third_std, sums_out, pixel_count, mask
    ).astype(LOW)
    grad_second_act = times_transpose(grad_third, weight_out)
    grad_second_pre = grad_second_act * mask * slope(second_pre)
    sums_mid = sum_all(both(grad_second_pre, second_normed))
    grad_second = norm_back(
        grad_second_pre, second_normed, gain_mid, second_std, sums_mid, pixel_count, mask
    ).astype(LOW)
    above, below = rim(grad_second.reshape(images, height, width, middle))
    grad_first_pre, sums_in = call(
        lambda *refs: mid_backward(dims, *refs),
        [((pixels, middle), FULL), ((2, middle), FULL)],
        grad_second,
        above.reshape(-1, middle),
        below.reshape(-1, middle),
        first,
        mask,
        first_scale[None],
        first_shift[None],
        first_avg[None],
        first_std[None],
        weight_mid,
    )
    sums_in = sum_all(sums_in)
    first_normed = (first - first_avg) * first_std
    grad_first = norm_back(
        grad_first_pre, first_normed, gain_in, first_std, sums_in, pixel_count, mask
    ).astype(LOW)
    grad_features = grad_summed + times_transpose(grad_first, weight_in)

    grad_weight_out = contract(second_act, grad_third)
    (grad_weight_mid,) = call(
        mid_weights,
        [((middle // GROUP, 9, GROUP, middle), FULL)],
        x3,
        grad_second,
    )
    grad_weight_mid = grad_weight_mid.reshape(-1, middle)
    grad_weight_in = contract(flat_features, grad_first)
    grad_weight_out = gather_back(sum_scatter(grad_weight_out)).astype(FULL)
    grad_weight_mid = gather_back(sum_scatter(grad_weight_mid)).astype(FULL)
    grad_weight_mid = grad_weight_mid.reshape(-1, 9, GROUP, middle).transpose(1, 0, 2, 3)
    grad_weight_mid = grad_weight_mid.reshape(weight_mid.shape)
    grad_weight_in = gather_back(sum_scatter(grad_weight_in)).astype(FULL)
    whole = (images, height, width, channels)
    return (
        result.astype(LOW).reshape(whole),
        pooled,
        grad_features.reshape(whole),
        grad_weight_in,
        sums_in[1],
        sums_in[0],
        grad_weight_mid,
        sums_mid[1],
        sums_mid[0],
        grad_weight_out,
        sums_out[1],
        sums_out[0],
    )


def solution(mesh):
    tiles, single = P("img", "rows", None, None), P()
    return jax.shard_map(
        per_device,
        mesh=mesh,
        in_specs=(tiles,) + (single,) * 9 + (P("img"), tiles, P("img", None)),
        out_specs=(tiles, P("img", None), tiles) + (single,) * 9,
        check_vma=False,
    )
```

```python
import jax
import jax.numpy as jnp
from jax import lax
from jax.experimental import pallas as pl
from jax.experimental.pallas import tpu as pltpu
from jax.sharding import PartitionSpec as P

EPSILON = 1e-05
AXES = ("img", "rows")
MIB = 1 << 20
LOW = jnp.bfloat16
FULL = jnp.float32
GROUP = 16
LANES = 128


def swap(value, flips):
    count = lax.axis_size(AXES)
    return lax.ppermute(value, AXES, [(i, i ^ flips[i & 1]) for i in range(count)])


def bits():
    count, found = lax.axis_size(AXES), []
    while (1 << len(found)) < count:
        found.append(1 << len(found))
    return found


def everyone(copies):
    return lax.all_to_all(copies, AXES, 0, 0)


def sum_wide(value, *beside):
    order = bits()
    value = value + swap(value, order[:1] * 2)
    arrived = []
    for at in range(1, len(order) - 1, 2):
        p, q = order[at : at + 2]
        one, two, three = swap(value, (p, p)), swap(value, (q, q)), swap(value, (p ^ q, p ^ q))
        value = (value + one) + (two + three)
        travels = beside[len(arrived)] if len(arrived) < len(beside) else ()
        value, *came = tie(value, *(swap(*pair) for pair in travels))
        arrived.append(came)
    if len(order) % 2 == 0:
        value = value + swap(value, order[-1:] * 2)
    return value, *arrived[: len(beside)]


def tie(*values):
    return lax.optimization_barrier(values)


def flat_index():
    return lax.axis_index("img") * lax.axis_size("rows") + lax.axis_index("rows")


def plan():
    order = bits()
    steps = [(bit, bit) for bit in order]
    if len(order) >= 3:
        steps[1], steps[2] = (order[1], order[2]), (order[2], order[1])
    index = flat_index()
    low = index % 2
    chosen = []
    for even, odd in steps:
        chosen.append(((even, odd), jnp.where(low == 0, index // even % 2, index // odd % 2)))
    return chosen


def half_of(value, which, axis=0):
    size = value.shape[axis] // 2
    return lax.dynamic_slice_in_dim(value, which * size, size, axis=axis)


def stack(mine, value, other):
    low = mine == 0
    return jnp.stack([jnp.where(low, value, other), jnp.where(low, other, value)])


def scatter_step(value, step):
    _, mine = step
    return half_of(value, 1 - mine).astype(LOW), half_of(value, mine)


def merge(value, other, step):
    return stack(step[1], value, other).reshape((-1,) + value.shape[1:])


def reduce_chain(value, steps):
    for step in steps:
        sent, kept = scatter_step(value, step)
        came = yield sent, step[0]
        value = kept + came.astype(FULL)
    return value


def gather_chain(value, steps):
    for step in steps:
        came = yield value, step[0]
        value = merge(value, came, step)
    return value


def advance(chains, state, slots, extra=()):
    names = [name for name in slots if name in chains]
    came = [swap(*state[name]) for name in names]
    done = tie(*came, *extra)
    for name, value in zip(names, done):
        try:
            state[name] = chains[name].send(value)
        except StopIteration as end:
            state[name] = end.value
            del chains[name]
    return done[len(names) :]


def sum_rows_axis(value):
    count, bit = lax.axis_size("rows"), 1
    while bit < count:
        value = value + lax.ppermute(value, "rows", [(i, i ^ bit) for i in range(count)])
        bit *= 2
    return value


def rim(block):
    count = lax.axis_size("rows")
    odd = lax.axis_index("rows") % 2 == 1
    top, bottom = block[:, :1], block[:, -1:]
    near = lax.ppermute(jnp.where(odd, top, bottom), "rows", [(i, i ^ 1) for i in range(count)])
    pairs = [(i, i + 1) for i in range(1, count - 1, 2)]
    far = lax.ppermute(jnp.where(odd, bottom, top), "rows", pairs + [(b, a) for a, b in pairs])
    return near.reshape(-1, near.shape[-1]), far.reshape(-1, far.shape[-1])


def call(kernel, outs, *args, scratch=(), left=(), limit=48):
    def place(at, arg):
        if at in left:
            return pl.BlockSpec(memory_space=pltpu.HBM)
        whole = arg.dtype == jnp.int32
        return pl.BlockSpec(memory_space=pltpu.SMEM if whole else pltpu.VMEM)

    return pl.pallas_call(
        kernel,
        out_shape=[jax.ShapeDtypeStruct(shape, kind) for shape, kind in outs],
        in_specs=[place(at, arg) for at, arg in enumerate(args)],
        out_specs=[pl.BlockSpec(memory_space=pltpu.VMEM)] * len(outs),
        scratch_shapes=list(scratch),
        compiler_params=pltpu.CompilerParams(vmem_limit_bytes=limit * MIB),
    )(*args)


def logistic(values):
    return 1.0 / (1.0 + jnp.exp(-values))


def slope(values):
    s = logistic(values)
    return s * (1.0 + values * (1.0 - s))


def shifted(values, by):
    return pltpu.roll(values, (-by) % values.shape[0], 0)


def spread(images, height, width, main, above, below):
    channels = main.shape[-1]
    main = main.reshape(images, height, width, channels)
    above = above.reshape(images, 1, width, channels)
    below = below.reshape(images, 1, width, channels)
    flat = (images * height * width, channels)
    return (
        jnp.concatenate([above, main[:, :-1]], axis=1).reshape(flat),
        main.reshape(flat),
        jnp.concatenate([main[:, 1:], below], axis=1).reshape(flat),
    )


def wide(mask, like):
    return jnp.concatenate([mask] * (like.shape[1] // mask.shape[1]), axis=1)


def first_forward(
    dims, place, map_size, gain, bias, gain_mid, bias_mid, features, weight,
    first, sums, params, params_mid, areas, mask, mask_above, mask_below,
    sizes, rows, left, right, few, sems,
):
    images, height, width = dims
    lanes = mask.shape[1]
    parts = sems.shape[1]
    deep = left.shape[1] // parts
    small = [pltpu.make_async_copy(map_size, sizes, few.at[0])]
    for k, source in enumerate((gain, bias, gain_mid, bias_mid)):
        small.append(pltpu.make_async_copy(source, rows.at[k], few.at[k + 1]))
    for copy in small:
        copy.start()

    def load(k):
        span = pl.ds(k * deep, deep)
        return (
            pltpu.make_async_copy(features.at[:, span], left.at[:, span], sems.at[0, k]),
            pltpu.make_async_copy(weight.at[span, :], right.at[span, :], sems.at[1, k]),
        )

    for k in range(parts):
        for copy in load(k):
            copy.start()
    for copy in small:
        copy.wait()

    def inside(start, count):
        spot = lax.broadcasted_iota(jnp.int32, (count * width, lanes), 0)
        row, column = start + spot // width, spot % width
        parts = []
        for n in range(images):
            size = sizes[0, n]
            here = (row >= 0) & (row < size) & (column < size)
            parts.append(jnp.where(here, 1.0, 0.0))
        return jnp.concatenate(parts, axis=0)

    start = place[0, 0] * height
    kept = inside(start, height)
    mask[...] = kept
    mask_above[...] = inside(start - 1, 1)
    mask_below[...] = inside(start + height, 1)
    params[0:1], params[1:2] = rows[0], rows[1]
    params_mid[0:1], params_mid[1:2] = rows[2], rows[3]
    spot = lax.broadcasted_iota(jnp.int32, areas.shape, 0)
    area = jnp.zeros(areas.shape, FULL)
    for n in range(images):
        area = jnp.where(spot == n, (sizes[0, n] * sizes[0, n]).astype(FULL), area)
    areas[...] = area
    total = None
    for k in range(parts):
        for copy in load(k):
            copy.wait()
        span = pl.ds(k * deep, deep)
        part = jnp.dot(left[:, span], right[span, :], preferred_element_type=FULL)
        total = part if total is None else total + part
    first[...] = total
    masked = total * wide(kept, total)
    middle = total.shape[1]
    sums[:, 0, 0:middle] = spread_sum(sums, masked)
    sums[:, 1, 0:middle] = spread_sum(sums, masked * total)
    sums[:, 0, middle:] = spread_sum(sums, kept)
    sums[:, 1, middle:] = spread_sum(sums, kept)


def spread_sum(copies, values):
    total = jnp.sum(values, axis=0, keepdims=True)
    return jnp.broadcast_to(total, (copies.shape[0], total.shape[1]))


def fetch(weight, held, sems):
    def load(i, j):
        return pltpu.make_async_copy(weight.at[i, j], held.at[i, j], sems.at[i, j])

    for j in range(3):
        for i in range(3):
            load(i, j).start()

    def tap(i, j):
        load(i, j).wait()
        return held[i, j]

    return tap


def affine(sums, count, gain, bias):
    average = sums[0:1] / count
    inv_std = lax.rsqrt(sums[1:2] / count - average * average + EPSILON)
    scale = inv_std * gain
    return average, inv_std, scale, bias - average * scale


def mid_forward(
    dims, place, came, params, first, near, far, mask, mask_above, mask_below, weight,
    split, second, sums, sums_first, held, sems, edges, edge_sems,
):
    near_in = pltpu.make_async_copy(near, edges.at[0], edge_sems.at[0])
    far_in = pltpu.make_async_copy(far, edges.at[1], edge_sems.at[1])
    near_in.start()
    far_in.start()
    tap = fetch(weight, held, sems)
    middle = first.shape[1]
    totals = jnp.sum(came[...], axis=0)
    sums_first[...] = totals
    count = totals[0:1, middle : middle + 1]
    _, _, scale, shift = affine(totals[:, 0:middle], count, params[0:1], params[1:2])

    def act(hidden, inside):
        pre = hidden * scale + shift
        return pre * logistic(pre) * wide(inside[...], pre)

    odd = place[0, 0] % 2 == 1
    centre = act(first[...], mask)
    near_in.wait()
    far_in.wait()
    above = act(jnp.where(odd, edges[0], edges[1]), mask_above)
    below = act(jnp.where(odd, edges[1], edges[0]), mask_below)
    three = spread(*dims, centre, above, below)
    x3 = [part.astype(LOW) for part in three]
    flat_rows(dims, centre, split)
    total = None
    for j in range(3):
        part = None
        for i in range(3):
            term = jnp.dot(x3[i], tap(i, j), preferred_element_type=FULL)
            part = term if part is None else part + term
        part = shifted(part, j - 1) if j != 1 else part
        total = part if total is None else total + part
    second[...] = total
    masked = total * wide(mask[...], total)
    sums[:, 0] = spread_sum(sums, masked)
    sums[:, 1] = spread_sum(sums, masked * total)


def flat_rows(dims, value, out):
    images, height, width = dims
    value = value.reshape(images, height, width, -1)
    for r in range(height):
        out[r] = value[:, r].reshape(images * width, -1).astype(LOW)


def out_forward(dims, sums_first, came, params_mid, second, mask, weight, act, normed_rows, third, sums, sums_second):
    middle = second.shape[1]
    totals = jnp.sum(came[...], axis=0)
    sums_second[...] = totals
    count = sums_first[0:1, middle : middle + 1]
    average, inv_std, scale, shift = affine(totals, count, params_mid[0:1], params_mid[1:2])
    hidden = second[...]
    pre = hidden * scale + shift
    act[...] = (pre * logistic(pre) * wide(mask[...], pre)).astype(LOW)
    flat_rows(dims, (hidden - average) * inv_std, normed_rows)
    inside = wide(mask[...], hidden)
    for at in range(0, third.shape[1], middle):
        span = pl.ds(at, middle)
        total = jnp.dot(act[...], weight[:, span], preferred_element_type=FULL)
        third[:, span] = total
        masked = total * inside
        sums[0:1, span] = jnp.sum(masked, axis=0, keepdims=True)
        sums[1:2, span] = jnp.sum(masked * total, axis=0, keepdims=True)


def out_result(
    dims, sums_first, sums_third, params_out, third, features, out_grad, pool_grad, areas, mask,
    result, pooled, grad, sums,
):
    images, height, width = dims
    chunk = sums_first.shape[1] - mask.shape[1]
    count = sums_first[0:1, chunk : chunk + 1]
    inside = jnp.concatenate([mask[...]] * (chunk // mask.shape[1]), axis=1)
    area = jnp.concatenate([areas[...]] * (chunk // mask.shape[1]), axis=1)
    for at in range(0, third.shape[1], chunk):
        span = pl.ds(at, chunk)
        average, inv_std, _, _ = affine(sums_third[:, span], count, 1.0, 0.0)
        normed = (third[:, span] - average) * inv_std
        summed = params_out[0:1, span] * normed + params_out[1:2, span] + features[:, span].astype(FULL)
        gate = logistic(summed)
        value = summed * gate * inside
        result[:, span] = value.astype(LOW)
        pooled[:, span] = jnp.sum(value.reshape(images, height * width, chunk), axis=1)
        share = (pool_grad[:, span] / area)[:, None]
        total = out_grad[:, span].astype(FULL).reshape(images, height * width, chunk) + share
        total = total.reshape(inside.shape) * inside * (gate * (1.0 + summed * (1.0 - gate)))
        grad[:, span] = total
        sums[0:1, span] = jnp.sum(total, axis=0, keepdims=True)
        sums[1:2, span] = jnp.sum(total * normed, axis=0, keepdims=True)


def out_backward(
    dims, sums_first, sums_second, sums_third, sums_out, params_mid, params_out, third, grad, second, mask, weight,
    grad_third, pre_grad, rows, sums,
):
    chunk = second.shape[1]
    count = sums_first[0:1, chunk : chunk + 1]
    inside = wide(mask[...], second)
    back = None
    for at in range(0, third.shape[1], chunk):
        span = pl.ds(at, chunk)
        average, inv_std, scale, _ = affine(sums_third[:, span], count, params_out[0:1, span], 0.0)
        normed = (third[:, span] - average) * inv_std
        mean = (sums_out[0:1, span] + normed * sums_out[1:2, span]) / count
        low = (inside * scale * (grad[:, span] - mean)).astype(LOW)
        grad_third[:, span] = low
        part = lax.dot_general(
            low, weight[:, span], (((1,), (1,)), ((), ())), preferred_element_type=FULL
        )
        back = part if back is None else back + part
    average, inv_std, scale, shift = affine(sums_second[...], count, params_mid[0:1], params_mid[1:2])
    hidden = second[...]
    back = back * inside * slope(hidden * scale + shift)
    pre_grad[...] = back
    flat_rows(dims, back, rows)
    sums[:, 0] = spread_sum(sums, back)
    sums[:, 1] = spread_sum(sums, back * ((hidden - average) * inv_std))


def mid_weights(
    place, sizes, sums_first, sums_second, sums_grad, params_mid, acts, normed, grads, total, left, right
):
    groups, _, size, channels = total.shape
    pixels = acts.shape[2]
    images = sizes.shape[1]
    width = pixels // images
    swapped = place[0, 0] == 1
    middle = sums_grad.shape[1]
    count = sums_first[0:1, middle : middle + 1]
    span = pl.ds(pl.multiple_of(place[0, 1] * channels, channels), channels)
    average = sums_second[0:1, span] / count
    inv_std = lax.rsqrt(sums_second[1:2, span] / count - average * average + EPSILON)
    scale = inv_std * params_mid[0:1, span]
    mean_grad, mean_gain = sums_grad[0:1, span] / count, sums_grad[1:2, span] / count
    column = lax.broadcasted_iota(jnp.int32, (width, channels), 0)
    for y in range(2):
        for x in range(2):
            for c in range(2):
                spot = jnp.where(swapped, 4 * x + 2 * y + c, 4 * y + 2 * x + c)
                rows = pl.ds(((2 * y + x) * 2 + c) * pixels, pixels)
                for r in range(2):
                    left[r, rows, :] = acts[spot, r]
                    row = (2 * x + c) * 2 + r
                    inside = []
                    for n in range(images):
                        extent = jnp.where(row < sizes[y, n], sizes[y, n], 0)
                        inside.append(jnp.where(column < extent, 1.0, 0.0))
                    value = grads[spot, r].astype(FULL)
                    value = value - (mean_grad + normed[spot, r].astype(FULL) * mean_gain)
                    value = value * scale * jnp.concatenate(inside, axis=0)
                    right[r, rows, 0:channels] = value.astype(LOW)
    for r in range(2):
        grad = right[r, :, 0:channels].astype(FULL)
        right[r, :, channels : 2 * channels] = shifted(grad, 1).astype(LOW)
        right[r, :, 2 * channels :] = shifted(grad, -1).astype(LOW)
    span, image = 3 * pixels, 4 * pixels

    def product(r_left, at_left, r_right, at_right, count):
        return lax.dot_general(
            left[r_left, pl.ds(at_left, count), :],
            right[r_right, pl.ds(at_right, count), :],
            (((0,), (0,)), ((), ())),
            preferred_element_type=FULL,
        )

    def crossed(r_left, r_right, skip_left, skip_right):
        part = product(r_left, 0, r_right, 0, 2 * image)
        for y in range(2):
            part = part + product(
                r_right, y * image + skip_left, r_left, y * image + skip_right, span
            )
        return part

    taps = (
        crossed(0, 1, 0, pixels),
        product(0, 0, 0, 0, 2 * image) + product(1, 0, 1, 0, 2 * image),
        crossed(1, 0, pixels, 0),
    )
    for i in range(3):
        for j, place in ((1, 0), (0, 1), (2, 2)):
            part = taps[i][:, place * channels : (place + 1) * channels]
            total[:, 3 * i + j] = part.reshape(groups, size, channels)


def mid_assemble(odd, mine, other, total):
    quarters, groups, _, size, lanes = mine.shape
    half = groups * size
    swapped = odd[0, 0] == 1
    for q in range(quarters):
        a = mine[q, :, 0].astype(FULL).reshape(half, lanes)
        b = other[q, :, 0].astype(FULL).reshape(half, lanes)
        total[0, 0:half, q * lanes : (q + 1) * lanes] = jnp.where(swapped, b, a)
        total[0, half:, q * lanes : (q + 1) * lanes] = jnp.where(swapped, a, b)


def mid_backward(
    dims, place, sums_first, sums_second, came, params, params_mid, grad, near, far,
    second, second_near, second_far, first, mask, mask_above, mask_below, weight,
    pre_grad, sums, sums_mid, held, sems, edges, edge_sems,
):
    copies = []
    for k, source in enumerate((near, far, second_near, second_far)):
        copies.append(pltpu.make_async_copy(source, edges.at[k], edge_sems.at[k]))
        copies[-1].start()
    tap = fetch(weight, held, sems)
    middle = first.shape[1]
    count = sums_first[0:1, middle : middle + 1]
    totals = jnp.sum(came[...], axis=0)
    sums_mid[...] = totals
    average, inv_std, scale, shift = affine(sums_second[...], count, params_mid[0:1], params_mid[1:2])
    mean_grad, mean_gain = totals[0:1] / count, totals[1:2] / count

    def normed_grad(value, hidden, inside):
        normed = (hidden - average) * inv_std
        return wide(inside[...], value) * scale * (value - (mean_grad + normed * mean_gain))

    odd = place[0, 0] % 2 == 1

    def beside(one, other, inside):
        value = jnp.where(odd, edges[one], edges[other])
        return normed_grad(value, jnp.where(odd, edges[one + 2], edges[other + 2]), inside)

    centre = normed_grad(grad[...], second[...], mask)
    for copy in copies:
        copy.wait()
    above = beside(0, 1, mask_above)
    below = beside(1, 0, mask_below)
    three = spread(*dims, centre, above, below)
    average, inv_std, scale, shift = affine(sums_first[:, 0:middle], count, params[0:1], params[1:2])
    low = [part.astype(LOW) for part in three]
    total = None
    for j in range(3):
        part = None
        for i in range(3):
            term = lax.dot_general(
                low[2 - i], tap(i, j), (((1,), (1,)), ((), ())), preferred_element_type=FULL
            )
            part = term if part is None else part + term
        part = shifted(part, 1 - j) if j != 1 else part
        total = part if total is None else total + part
    hidden = first[...]
    total = total * wide(mask[...], total) * slope(hidden * scale + shift)
    pre_grad[...] = total
    sums[:, 0] = spread_sum(sums, total)
    sums[:, 1] = spread_sum(sums, total * ((hidden - average) * inv_std))


def first_backward(sums_first, came, params, first, grad, mask, low, sums_in):
    middle = first.shape[1]
    count = sums_first[0:1, middle : middle + 1]
    totals = jnp.sum(came[...], axis=0)
    sums_in[...] = totals
    average, inv_std, scale, _ = affine(sums_first[:, 0:middle], count, params[0:1], 0.0)
    normed = (first[...] - average) * inv_std
    value = grad[...] - (totals[0:1] + normed * totals[1:2]) / count
    low[...] = (wide(mask[...], value) * scale * value).astype(LOW)


def assemble(odd, mine, other, shape):
    groups, taps, size, lanes = shape
    quarters = mine.shape[0] // (groups * taps * size)
    channels = quarters * lanes
    pieces = pl.BlockSpec((quarters, groups, 1, size, lanes), lambda t: (0, 0, t, 0, 0))
    return pl.pallas_call(
        mid_assemble,
        grid=(taps,),
        out_shape=jax.ShapeDtypeStruct((taps, channels, channels), FULL),
        in_specs=[pl.BlockSpec(memory_space=pltpu.SMEM), pieces, pieces],
        out_specs=pl.BlockSpec((1, channels, channels), lambda t: (t, 0, 0)),
        compiler_params=pltpu.CompilerParams(vmem_limit_bytes=48 * MIB),
    )(
        odd,
        mine.reshape(quarters, groups, taps, size, lanes),
        other.reshape(quarters, groups, taps, size, lanes),
    )


def halves(value, step):
    _, mine = step
    return half_of(value, 1 - mine, 3), half_of(value, mine, 3)


def contract(left, right):
    return lax.dot_general(left, right, (((0,), (0,)), ((), ())), preferred_element_type=FULL)


def times_transpose(left, weights):
    return lax.dot_general(left, weights, (((1,), (1,)), ((), ())), preferred_element_type=FULL)


def per_device(
    features,
    weight_in,
    gain_in,
    bias_in,
    weight_mid,
    gain_mid,
    bias_mid,
    weight_out,
    gain_out,
    bias_out,
    map_size,
    out_grad,
    pool_grad,
):
    images, height, width, channels = features.shape
    middle = weight_mid.shape[3]
    dims = (images, height, width)
    pixels = images * height * width

    count = lax.axis_size(AXES)
    place = lax.axis_index("rows").astype(jnp.int32).reshape(1, 1)
    index = flat_index()
    flat_features = features.reshape(pixels, channels)
    params_out = jnp.stack([gain_out, bias_out])
    steps = plan()
    core, mine, far_steps = steps[0], steps[0][1], steps[3:]
    plane, narrow, broad = (pixels, middle), (2, middle), (2, channels)
    edge = (images * width, middle)

    def sides(value):
        return rim(value.reshape(images, height, width, middle))

    first, sums, params, params_mid, areas, mask, mask_above, mask_below = call(
        lambda *refs: first_forward(dims, *refs),
        [
            (plane, FULL),
            ((count, 2, middle + LANES), FULL),
            (narrow, FULL),
            (narrow, FULL),
            ((images, LANES), FULL),
            ((pixels, LANES), FULL),
            ((images * width, LANES), FULL),
            ((images * width, LANES), FULL),
        ],
        place,
        map_size[None],
        gain_in[None],
        bias_in[None],
        gain_mid[None],
        bias_mid[None],
        flat_features,
        weight_in,
        scratch=[
            pltpu.SMEM((1, images), jnp.int32),
            pltpu.VMEM((4, 1, middle), FULL),
            pltpu.VMEM((pixels, channels), LOW),
            pltpu.VMEM((channels, middle), LOW),
            pltpu.SemaphoreType.DMA((5,)),
            pltpu.SemaphoreType.DMA((2, 4)),
        ],
        left=(1, 2, 3, 4, 5, 6, 7),
        limit=56,
    )
    taps = [pltpu.VMEM(weight_mid.shape, LOW), pltpu.SemaphoreType.DMA((3, 3))]
    near, far = sides(first)
    came, near, far = tie(everyone(sums), near, far)
    split, second, sums, sums_first = call(
        lambda *refs: mid_forward(dims, *refs),
        [
            ((height, images * width, middle), LOW),
            (plane, FULL),
            ((count, 2, middle), FULL),
            ((2, middle + LANES), FULL),
        ],
        place,
        came,
        params,
        first,
        near,
        far,
        mask,
        mask_above,
        mask_below,
        weight_mid,
        scratch=taps + [pltpu.VMEM((2, *edge), FULL), pltpu.SemaphoreType.DMA((2,))],
        left=(4, 5, 9),
    )
    second_near, second_far = sides(second)
    acts = swap(half_of(split, 1 - mine, 2), core[0])
    sizes = map_size.astype(FULL)[None]
    other_sizes = swap(sizes, (lax.axis_size("rows"),) * 2)
    came, acts, second_near, second_far, other_sizes = tie(
        everyone(sums), acts, second_near, second_far, other_sizes
    )
    sizes = stack(lax.axis_index("img") % 2, sizes, other_sizes)[:, 0].astype(jnp.int32)
    second_act, normed, third, sums, sums_second = call(
        lambda *refs: out_forward(dims, *refs),
        [
            (plane, LOW),
            ((height, images * width, middle), LOW),
            ((pixels, channels), FULL),
            (broad, FULL),
            (narrow, FULL),
        ],
        sums_first,
        came,
        params_mid,
        second,
        mask,
        weight_out,
    )
    acts = stack(mine, half_of(split, mine, 2), acts)
    sums, acts, normed = tie(sums, acts, normed)
    sums_third, (came,), (acts_came,) = sum_wide(sums, ((normed, core[0]),), ((acts, steps[1][0]),))
    result, pooled, grad_summed, sums = call(
        lambda *refs: out_result(dims, *refs),
        [
            ((pixels, channels), LOW),
            ((images, channels), FULL),
            ((pixels, channels), FULL),
            (broad, FULL),
        ],
        sums_first,
        sums_third,
        params_out,
        third,
        flat_features,
        out_grad.reshape(pixels, channels),
        pool_grad,
        areas,
        mask,
    )

    acts = merge(acts, acts_came, steps[1])
    sent, kept = halves(stack(mine, normed, came), steps[1])
    sums, acts, sent = tie(sums, acts, sent)
    sums_out, (came,), (acts_came,) = sum_wide(
        sums, ((sent, steps[1][0]),), ((acts, steps[2][0]),)
    )
    grad_third, grad_second_pre, grads, sums = call(
        lambda *refs: out_backward(dims, *refs),
        [
            ((pixels, channels), LOW),
            (plane, FULL),
            ((height, images * width, middle), LOW),
            ((count, 2, middle), FULL),
        ],
        sums_first,
        sums_second,
        sums_third,
        sums_out,
        params_mid,
        params_out,
        third,
        grad_summed,
        second,
        mask,
        weight_out,
    )

    normed_sent, normed_kept = halves(merge(kept, came, steps[1]), steps[2])
    out_sent = contract(half_of(second_act, 1 - mine, 1), grad_third).astype(LOW)
    sums, grads, out_sent, normed_sent = tie(sums, grads, out_sent, normed_sent)
    came, out_came = swap(grads, core[0]), swap(out_sent, core[0])
    near, far = sides(grad_second_pre)
    sums = everyone(sums)
    sent, kept = halves(stack(mine, grads, came), steps[1])
    came, normed_came = swap(sent, steps[1][0]), swap(normed_sent, steps[2][0])
    out_kept = contract(half_of(second_act, mine, 1), grad_third)
    acts = merge(acts, acts_came, steps[2])
    sums, came, normed_came, out_came, out_kept, acts, near, far = tie(
        sums, came, normed_came, out_came, out_kept, acts, near, far
    )
    sent, kept = halves(merge(kept, came, steps[1]), steps[2])
    sent, sums = tie(sent, sums)
    came = swap(sent, steps[2][0])
    grad_first_pre, sums, sums_mid = call(
        lambda *refs: mid_backward(dims, *refs),
        [(plane, FULL), ((count, 2, middle), FULL), (narrow, FULL)],
        place,
        sums_first,
        sums_second,
        sums,
        params,
        params_mid,
        grad_second_pre,
        near,
        far,
        second,
        second_near,
        second_far,
        first,
        mask,
        mask_above,
        mask_below,
        weight_mid,
        scratch=taps + [pltpu.VMEM((4, *edge), FULL), pltpu.SemaphoreType.DMA((4,))],
        left=(7, 8, 10, 11, 16),
    )
    sums, came, out_came, out_kept = tie(sums, came, out_came, out_kept)
    grads = merge(kept, came, steps[2])
    normed = merge(normed_kept, normed_came, steps[2])

    odd = (index % 2).astype(jnp.int32).reshape(1, 1)
    chains, state = {}, {}

    def begin(name, chain):
        chains[name] = chain
        state[name] = next(chain)

    def out_chain():
        value = out_kept + out_came.astype(FULL)
        value = yield from reduce_chain(value, steps[1:])
        value = yield from gather_chain(value.astype(LOW), steps[:0:-1])
        other = yield value, core[0]
        return stack(mine, value, other).reshape(-1, channels).astype(FULL)

    def mid_chain():
        chunk = 2 * steps[1][1] + steps[2][1]
        lanes, deep = grads.shape[-1], acts.shape[-1]
        span = acts.shape[0] * images * width
        (block,) = call(
            mid_weights,
            [((deep // GROUP, 9, GROUP, lanes), FULL)],
            jnp.stack([index % 2, chunk]).astype(jnp.int32)[None],
            sizes,
            sums_first,
            sums_second,
            sums_mid,
            params_mid,
            acts,
            normed,
            grads,
            scratch=[pltpu.VMEM((2, span, deep), LOW), pltpu.VMEM((2, span, 3 * lanes), LOW)],
        )
        value = yield from reduce_chain(block.reshape(-1, lanes), far_steps)
        value = yield from gather_chain(value.astype(LOW), steps[:0:-1])
        other = yield value, core[0]
        return assemble(odd, value, other, block.shape)

    def in_chain():
        sent = contract(half_of(flat_features, 1 - mine, 1), grad_first).astype(LOW)
        kept = contract(half_of(flat_features, mine, 1), grad_first)
        came = yield sent, core[0]
        value = kept + came.astype(FULL)
        value = yield from reduce_chain(value, steps[1:])
        value = yield from gather_chain(value.astype(LOW), steps[:0:-1])
        other = yield value, core[0]
        return stack(mine, value, other).reshape(-1, middle).astype(FULL)

    begin("out", out_chain())
    begin("mid", mid_chain())
    (came,) = advance(chains, state, ("mid", "out"), (everyone(sums),))
    grad_first, sums_in = call(
        first_backward,
        [(plane, LOW), (narrow, FULL)],
        sums_first,
        came,
        params,
        first,
        grad_first_pre,
        mask,
    )
    begin("in", in_chain())
    advance(chains, state, ("in", "mid", "out"))
    grad_features = grad_summed + times_transpose(grad_first, weight_in)
    grad_features, pooled = advance(chains, state, ("in", "mid", "out"), (grad_features, pooled))
    pooled = sum_rows_axis(pooled.astype(LOW).astype(FULL)) / areas[:, :1]
    while chains:
        (pooled,) = advance(chains, state, ("in", "mid", "out"), (pooled,))
    grad_weight_in, grad_weight_mid, grad_weight_out = state["in"], state["mid"], state["out"]
    whole = (images, height, width, channels)
    return (
        result.astype(LOW).reshape(whole),
        pooled,
        grad_features.reshape(whole),
        grad_weight_in,
        sums_in[1],
        sums_in[0],
        grad_weight_mid.reshape(weight_mid.shape),
        sums_mid[1],
        sums_mid[0],
        grad_weight_out,
        sums_out[1],
        sums_out[0],
    )


def solution(mesh):
    tiles, single = P("img", "rows", None, None), P()
    return jax.shard_map(
        per_device,
        mesh=mesh,
        in_specs=(tiles,) + (single,) * 9 + (P("img"), tiles, P("img", None)),
        out_specs=(tiles, P("img", None), tiles) + (single,) * 9,
        check_vma=False,
    )
```

```python
import jax
import jax.numpy as jnp
from jax import lax
from jax.experimental import pallas as pl
from jax.experimental.pallas import tpu as pltpu
from jax.sharding import Mesh
from jax.sharding import PartitionSpec as P

EPSILON = 1e-05
ROWS = ("half", "low")
AXES = ("img", *ROWS)
MIB = 1 << 20
LOW = jnp.bfloat16
FULL = jnp.float32
GROUP = 16
LANES = 128


def swap(value, flips):
    count = lax.axis_size(AXES)
    return lax.ppermute(value, AXES, [(i, i ^ flips[i & 1]) for i in range(count)])


def bits():
    count, found = lax.axis_size(AXES), []
    while (1 << len(found)) < count:
        found.append(1 << len(found))
    return found


def everyone(copies):
    return lax.all_to_all(copies, AXES, 0, 0)


def everyone_wide(sent, kept, low_step):
    value = kept + swap(sent, low_step[0])
    count = lax.axis_size(AXES[:2])
    mine = lax.all_to_all(jnp.broadcast_to(value[None], (count, *value.shape)), AXES[:2], 0, 0)
    return mine, swap(mine, low_step[0])


def tie(*values):
    return lax.optimization_barrier(values)


def flat_index():
    return lax.axis_index("img") * lax.axis_size(ROWS) + lax.axis_index(ROWS)


def plan():
    order = bits()
    steps = [(bit, bit) for bit in order]
    if len(order) >= 3:
        steps[1], steps[2] = (order[1], order[2]), (order[2], order[1])
    index = flat_index()
    low = index % 2
    chosen = []
    for even, odd in steps:
        chosen.append(((even, odd), jnp.where(low == 0, index // even % 2, index // odd % 2)))
    return chosen


def half_of(value, which, axis=0):
    size = value.shape[axis] // 2
    return lax.dynamic_slice_in_dim(value, which * size, size, axis=axis)


def stack(mine, value, other):
    low = mine == 0
    return jnp.stack([jnp.where(low, value, other), jnp.where(low, other, value)])


def scatter_step(value, step):
    _, mine = step
    return half_of(value, 1 - mine).astype(LOW), half_of(value, mine)


def merge(value, other, step):
    return stack(step[1], value, other).reshape((-1,) + value.shape[1:])


def reduce_chain(value, steps):
    for step in steps:
        sent, kept = scatter_step(value, step)
        came = yield sent, step[0]
        value = kept + came.astype(FULL)
    return value


def gather_chain(value, steps):
    for step in steps:
        came = yield value, step[0]
        value = merge(value, came, step)
    return value


class Chains:
    def __init__(self):
        self.running, self.flying, self.results = {}, {}, {}

    def begin(self, name, chain, spans, sent=None):
        self.running[name] = (chain, list(spans))
        self.load(name, next(chain) if sent is None else sent)

    def load(self, name, sent):
        spans = self.running[name][1]
        self.flying[name] = [sent, None, spans.pop(0) if spans else 1]

    def slot(self, *extra):
        due = []
        for name, flight in self.flying.items():
            if flight[1] is None:
                flight[1] = swap(*flight[0])
            flight[2] -= 1
            if flight[2] <= 0:
                due.append(name)
        done = tie(*(self.flying[name][1] for name in due), *extra) if due or extra else ()
        for name, value in zip(due, done):
            try:
                self.load(name, self.running[name][0].send(value))
            except StopIteration as end:
                self.results[name] = end.value
                del self.running[name], self.flying[name]
        return done[len(due) :]


def sum_rows_axis(value):
    count, bit = lax.axis_size(ROWS), 1
    while bit < count:
        value = value + lax.ppermute(value, ROWS, [(i, i ^ bit) for i in range(count)])
        bit *= 2
    return value


def trade(near, far):
    count = lax.axis_size(ROWS)
    pairs = [(i, i + 1) for i in range(1, count - 1, 2)]
    return (
        lax.ppermute(near, ROWS, [(i, i ^ 1) for i in range(count)]),
        lax.ppermute(far, ROWS, pairs + [(b, a) for a, b in pairs]),
    )


def call(kernel, outs, *args, scratch=(), left=(), limit=60):
    def place(at, arg):
        if at in left:
            return pl.BlockSpec(memory_space=pltpu.HBM)
        return pl.BlockSpec(memory_space=pltpu.SMEM if arg.dtype == jnp.int32 else pltpu.VMEM)

    return pl.pallas_call(
        kernel,
        out_shape=[jax.ShapeDtypeStruct(shape, kind) for shape, kind in outs],
        in_specs=[place(at, arg) for at, arg in enumerate(args)],
        out_specs=[pl.BlockSpec(memory_space=pltpu.VMEM)] * len(outs),
        scratch_shapes=list(scratch),
        compiler_params=pltpu.CompilerParams(vmem_limit_bytes=limit * MIB),
    )(*args)


def logistic(values):
    return 0.5 * jnp.tanh(0.5 * values) + 0.5


def slope(values):
    s = logistic(values)
    return s * (1.0 + values * (1.0 - s))


def shifted(values, by):
    return pltpu.roll(values, (-by) % values.shape[0], 0)


def spread(images, height, width, main, above, below):
    channels = main.shape[-1]
    main = main.reshape(images, height, width, channels)
    above = above.reshape(images, 1, width, channels)
    below = below.reshape(images, 1, width, channels)
    flat = (images * height * width, channels)
    return (
        jnp.concatenate([above, main[:, :-1]], axis=1).reshape(flat),
        main.reshape(flat),
        jnp.concatenate([main[:, 1:], below], axis=1).reshape(flat),
    )


def wide(mask, like):
    return jnp.concatenate([mask] * (like.shape[1] // mask.shape[1]), axis=1)


def edges_of(dims, place, value, near, far):
    images, height, width = dims
    value = value.reshape(images, height, width, -1)
    top = value[:, 0].reshape(images * width, -1)
    bottom = value[:, height - 1].reshape(images * width, -1)
    odd = place[0, 0] % 2 == 1
    near[...] = jnp.where(odd, top, bottom)
    far[...] = jnp.where(odd, bottom, top)


def first_forward(
    dims, place, map_size, gain, bias, gain_mid, bias_mid, features, weight,
    first, near, far, sums, params, params_mid, areas, mask, mask_other, mask_above, mask_below,
    sizes, few, left, right, few_sems, sems,
):
    images, height, width = dims
    lanes = mask.shape[1]
    parts = sems.shape[1]
    deep = left.shape[1] // parts
    small = [pltpu.make_async_copy(map_size, sizes, few_sems.at[0])]
    for k, source in enumerate((gain, bias, gain_mid, bias_mid)):
        small.append(pltpu.make_async_copy(source, few.at[k], few_sems.at[k + 1]))
    for copy in small:
        copy.start()

    def load(k):
        span = pl.ds(k * deep, deep)
        return (
            pltpu.make_async_copy(features.at[:, span], left.at[:, span], sems.at[0, k]),
            pltpu.make_async_copy(weight.at[span, :], right.at[span, :], sems.at[1, k]),
        )

    for k in range(parts):
        for copy in load(k):
            copy.start()
    for copy in small:
        copy.wait()

    def inside(start, count):
        spot = lax.broadcasted_iota(jnp.int32, (count * width, lanes), 0)
        row, column = start + spot // width, spot % width
        parts = []
        for n in range(images):
            size = sizes[0, n]
            here = (row >= 0) & (row < size) & (column < size)
            parts.append(jnp.where(here, 1.0, 0.0))
        return jnp.concatenate(parts, axis=0)

    start = place[0, 0] * height
    kept = inside(start, height)
    mask[...] = kept
    mask_other[...] = inside((place[0, 0] + 1 - 2 * (place[0, 0] % 2)) * height, height)
    mask_above[...] = inside(start - 1, 1)
    mask_below[...] = inside(start + height, 1)
    params[0:1], params[1:2] = few[0], few[1]
    params_mid[0:1], params_mid[1:2] = few[2], few[3]
    spot = lax.broadcasted_iota(jnp.int32, areas.shape, 0)
    area = jnp.zeros(areas.shape, FULL)
    for n in range(images):
        area = jnp.where(spot == n, (sizes[0, n] * sizes[0, n]).astype(FULL), area)
    areas[...] = area
    total = None
    for k in range(parts):
        for copy in load(k):
            copy.wait()
        span = pl.ds(k * deep, deep)
        part = jnp.dot(left[:, span], right[span, :], preferred_element_type=FULL)
        total = part if total is None else total + part
    first[...] = total
    masked = total * wide(kept, total)
    middle = total.shape[1]
    sums[:, 0, 0:middle] = spread_sum(sums, masked)
    sums[:, 1, 0:middle] = spread_sum(sums, masked * total)
    sums[:, 0, middle:] = spread_sum(sums, kept)
    lane = lax.broadcasted_iota(jnp.int32, (1, lanes), 1)
    told = jnp.zeros((1, lanes), FULL)
    for n in range(images):
        told = jnp.where(lane == n, sizes[0, n].astype(FULL), told)
    sums[:, 1, middle:] = jnp.broadcast_to(told, (sums.shape[0], lanes))
    edges_of(dims, place, total, near, far)


def spread_sum(copies, values):
    total = jnp.sum(values, axis=0, keepdims=True)
    return jnp.broadcast_to(total, (copies.shape[0], total.shape[1]))


def fetch(weight, held, sems):
    def load(i, j):
        return pltpu.make_async_copy(weight.at[i, j], held.at[i, j], sems.at[i, j])

    for j in range(3):
        for i in range(3):
            load(i, j).start()

    def tap(i, j):
        load(i, j).wait()
        return held[i, j]

    return tap


def put_sums(dims, place, at, values, others, sent, kept):
    chunk, half = values.shape[1], sent.shape[1]
    span = pl.ds(at % half, chunk)
    mine = (place[0, 0] % 2 == 1) == (at >= half)
    for k, value in enumerate((values, others)):
        total = jnp.sum(value, axis=0, keepdims=True)
        kept[k : k + 1, span] = jnp.where(mine, total, kept[k : k + 1, span])
        sent[k : k + 1, span] = jnp.where(mine, sent[k : k + 1, span], total)


def take_sums(place, at, chunk, mine, other):
    half = mine.shape[2]
    span = pl.ds(at % half, chunk)
    here = (place[0, 0] % 2 == 1) == (at >= half)
    return jnp.where(here, jnp.sum(mine[:, :, span], axis=0), jnp.sum(other[:, :, span], axis=0))


def affine(sums, count, gain, bias):
    average = sums[0:1] / count
    inv_std = lax.rsqrt(sums[1:2] / count - average * average + EPSILON)
    scale = inv_std * gain
    return average, inv_std, scale, bias - average * scale


def mid_forward(
    dims, place, came, params, first, near, far, mask, mask_above, mask_below, weight,
    split, second, sums, sums_first, sizes, held, sems,
):
    tap = fetch(weight, held, sems)
    middle = first.shape[1]
    totals = jnp.sum(came[...], axis=0)
    sums_first[...] = totals
    for y in range(2):
        sizes[y : y + 1] = came[place[0, 1] + y * place[0, 2], 1:2, middle:]
    count = totals[0:1, middle : middle + 1]
    _, _, scale, shift = affine(totals[:, 0:middle], count, params[0:1], params[1:2])

    def act(hidden, inside):
        pre = hidden * scale + shift
        return pre * logistic(pre) * wide(inside[...], pre)

    odd = place[0, 0] % 2 == 1
    centre = act(first[...], mask)
    above = act(jnp.where(odd, near[...], far[...]), mask_above)
    below = act(jnp.where(odd, far[...], near[...]), mask_below)
    three = spread(*dims, centre, above, below)
    x3 = [part.astype(LOW) for part in three]
    flat_rows(dims, centre, split)
    total = None
    for j in range(3):
        part = None
        for i in range(3):
            term = jnp.dot(x3[i], tap(i, j), preferred_element_type=FULL)
            part = term if part is None else part + term
        part = shifted(part, j - 1) if j != 1 else part
        total = part if total is None else total + part
    second[...] = total
    masked = total * wide(mask[...], total)
    sums[:, 0] = spread_sum(sums, masked)
    sums[:, 1] = spread_sum(sums, masked * total)


def flat_rows(dims, value, out):
    images, height, width = dims
    value = value.reshape(images, height, width, -1)
    for r in range(height):
        out[r] = value[:, r].reshape(images * width, -1).astype(LOW)


def flat_halves(dims, place, value, sent, kept):
    quarter = value.shape[1] // 4
    odd, high = place[0, 0] % 2 == 1, place[0, 3] == 1
    parts = [value[:, k * quarter : (k + 1) * quarter] for k in range(4)]
    parts[1], parts[2] = jnp.where(odd, parts[2], parts[1]), jnp.where(odd, parts[1], parts[2])
    one, two = jnp.concatenate(parts[:2], axis=1), jnp.concatenate(parts[2:], axis=1)
    flat_rows(dims, jnp.where(high, one, two), sent)
    flat_rows(dims, jnp.where(high, two, one), kept)


def out_forward(
    dims, place, sums_first, came, params_mid, second, mask, weight,
    act, normed_sent, normed_kept, third, sums_sent, sums_kept, sums_second,
):
    middle = second.shape[1]
    totals = jnp.sum(came[...], axis=0)
    sums_second[...] = totals
    count = sums_first[0:1, middle : middle + 1]
    average, inv_std, scale, shift = affine(totals, count, params_mid[0:1], params_mid[1:2])
    hidden = second[...]
    pre = hidden * scale + shift
    inside = wide(mask[...], hidden)
    act[...] = (pre * logistic(pre) * inside).astype(LOW)
    flat_halves(dims, place, (hidden - average) * inv_std, normed_sent, normed_kept)
    for at in range(0, third.shape[1], middle):
        span = pl.ds(at, middle)
        total = jnp.dot(act[...], weight[:, span], preferred_element_type=FULL)
        third[:, span] = total
        masked = total * inside
        put_sums(dims, place, at, masked, masked * total, sums_sent, sums_kept)


def out_result(
    dims, place, sums_first, came, other, params_out, third, features, out_grad, pool_grad, areas, mask,
    result, pooled, grad, sums_sent, sums_kept, sums_third,
):
    images, height, width = dims
    chunk = sums_first.shape[1] - mask.shape[1]
    count = sums_first[0:1, chunk : chunk + 1]
    inside = jnp.concatenate([mask[...]] * (chunk // mask.shape[1]), axis=1)
    area = jnp.concatenate([areas[...]] * (chunk // mask.shape[1]), axis=1)
    for at in range(0, third.shape[1], chunk):
        span = pl.ds(at, chunk)
        totals = take_sums(place, at, chunk, came, other)
        sums_third[:, span] = totals
        average, inv_std, _, _ = affine(totals, count, 1.0, 0.0)
        normed = (third[:, span] - average) * inv_std
        summed = params_out[0:1, span] * normed + params_out[1:2, span] + features[:, span].astype(FULL)
        gate = logistic(summed)
        value = summed * gate * inside
        result[:, span] = value.astype(LOW)
        pooled[:, span] = jnp.sum(value.reshape(images, height * width, chunk), axis=1)
        share = (pool_grad[:, span] / area)[:, None]
        total = out_grad[:, span].astype(FULL).reshape(images, height * width, chunk) + share
        total = total.reshape(inside.shape) * inside * (gate * (1.0 + summed * (1.0 - gate)))
        grad[:, span] = total
        put_sums(dims, place, at, total, total * normed, sums_sent, sums_kept)


def out_backward(
    dims, place, sums_first, sums_second, sums_third, came, other, params_mid, params_out, third, grad, second,
    mask, weight, third_sent, third_kept, pre_grad, rows_sent, rows_kept, near, far, sums, sums_out, lows,
):
    chunk = second.shape[1]
    count = sums_first[0:1, chunk : chunk + 1]
    inside = wide(mask[...], second)
    back = None
    for at in range(0, third.shape[1], chunk):
        span = pl.ds(at, chunk)
        average, inv_std, scale, _ = affine(sums_third[:, span], count, params_out[0:1, span], 0.0)
        normed = (third[:, span] - average) * inv_std
        totals = take_sums(place, at, chunk, came, other)
        sums_out[:, span] = totals
        mean = (totals[0:1] + normed * totals[1:2]) / count
        low = (inside * scale * (grad[:, span] - mean)).astype(LOW)
        lows[:, span] = low
        part = lax.dot_general(
            low, weight[:, span], (((1,), (1,)), ((), ())), preferred_element_type=FULL
        )
        back = part if back is None else back + part
    average, inv_std, scale, shift = affine(sums_second[...], count, params_mid[0:1], params_mid[1:2])
    hidden = second[...]
    back = back * inside * slope(hidden * scale + shift)
    pre_grad[...] = back
    flat_halves(dims, place, back, rows_sent, rows_kept)
    odd, half = place[0, 0] % 2 == 1, third.shape[1] // 2
    one, two = lows[:, 0:half], lows[:, half:]
    third_sent[...] = jnp.where(odd, one, two)
    third_kept[...] = jnp.where(odd, two, one)
    sums[:, 0] = spread_sum(sums, back)
    sums[:, 1] = spread_sum(sums, back * ((hidden - average) * inv_std))
    edges_of(dims, place, jnp.concatenate([back, hidden], axis=1), near, far)


def mid_weights(
    place, sizes, sums_first, sums_second, sums_grad, params_mid,
    acts_mine, acts_came, normed_mine, normed_came, grads_mine, grads_came, sent, kept, left, right,
):
    groups, _, size, channels = kept.shape
    pixels = acts_mine.shape[2]
    images = sizes.shape[1]
    width = pixels // images
    swapped, high = place[0, 0] == 1, place[0, 3] == 1
    middle = sums_grad.shape[1]
    count = sums_first[0:1, middle : middle + 1]
    span = pl.ds(pl.multiple_of(place[0, 1] * channels, channels), channels)
    average = sums_second[0:1, span] / count
    inv_std = lax.rsqrt(sums_second[1:2, span] / count - average * average + EPSILON)
    scale = inv_std * params_mid[0:1, span]
    mean_grad, mean_gain = sums_grad[0:1, span] / count, sums_grad[1:2, span] / count
    column = lax.broadcasted_iota(jnp.int32, (width, channels), 0)
    for y in range(2):
        for x in range(2):
            for c in range(2):
                spot = jnp.where(swapped, 2 * y + c, 2 * x + c)
                here = jnp.where(swapped, x, y) == place[0, 2]
                four = 2 * x + y if c else 2 * y + x
                own = place[0, 0] == c
                rows = pl.ds(((2 * y + x) * 2 + c) * pixels, pixels)
                for r in range(2):
                    left[r, rows, :] = jnp.where(here, acts_mine[spot, r], acts_came[spot, r])
                    row = (2 * x + c) * 2 + r
                    inside = []
                    for n in range(images):
                        extent = jnp.where(row < sizes[y, n], sizes[y, n], 0)
                        inside.append(jnp.where(column < extent, 1.0, 0.0))
                    value = jnp.where(own, grads_mine[four, r], grads_came[four, r]).astype(FULL)
                    normed = jnp.where(own, normed_mine[four, r], normed_came[four, r])
                    value = value - (mean_grad + normed.astype(FULL) * mean_gain)
                    value = value * scale * jnp.concatenate(inside, axis=0)
                    right[r, rows, 0:channels] = value.astype(LOW)
    for r in range(2):
        grad = right[r, :, 0:channels].astype(FULL)
        right[r, :, channels : 2 * channels] = shifted(grad, 1).astype(LOW)
        right[r, :, 2 * channels :] = shifted(grad, -1).astype(LOW)
    span, image = 3 * pixels, 4 * pixels

    def product(r_left, at_left, r_right, at_right, count):
        return lax.dot_general(
            left[r_left, pl.ds(at_left, count), :],
            right[r_right, pl.ds(at_right, count), :],
            (((0,), (0,)), ((), ())),
            preferred_element_type=FULL,
        )

    def crossed(r_left, r_right, skip_left, skip_right):
        part = product(r_left, 0, r_right, 0, 2 * image)
        for y in range(2):
            part = part + product(
                r_right, y * image + skip_left, r_left, y * image + skip_right, span
            )
        return part

    taps = (
        crossed(0, 1, 0, pixels),
        product(0, 0, 0, 0, 2 * image) + product(1, 0, 1, 0, 2 * image),
        crossed(1, 0, pixels, 0),
    )
    for i in range(3):
        for j, place in ((1, 0), (0, 1), (2, 2)):
            part = taps[i][:, place * channels : (place + 1) * channels]
            one = part[0 : groups * size].reshape(groups, size, channels)
            two = part[groups * size :].reshape(groups, size, channels)
            sent[:, 3 * i + j] = jnp.where(high, one, two).astype(LOW)
            kept[:, 3 * i + j] = jnp.where(high, two, one)


def mid_assemble(odd, mine, other, total):
    quarters, groups, _, size, lanes = mine.shape
    half = groups * size
    swapped = odd[0, 0] == 1
    for q, turned in enumerate((0, 2, 1, 3)):
        span = pl.ds(q * lanes, lanes)
        even = jnp.where(swapped, other[q, :, 0], mine[q, :, 0])
        total[0, 0:half, span] = even.astype(FULL).reshape(half, lanes)
        uneven = jnp.where(swapped, mine[turned, :, 0], other[turned, :, 0])
        total[0, half:, span] = uneven.astype(FULL).reshape(half, lanes)


def mid_backward(
    dims, place, sums_first, sums_second, came, params, params_mid, grad, near, far,
    second, first, mask, mask_above, mask_below, weight, pre_grad, low_grad, sums, sums_mid, held, sems,
):
    tap = fetch(weight, held, sems)
    middle = first.shape[1]
    count = sums_first[0:1, middle : middle + 1]
    totals = jnp.sum(came[...], axis=0)
    sums_mid[...] = totals
    average, inv_std, scale, shift = affine(sums_second[...], count, params_mid[0:1], params_mid[1:2])
    mean_grad, mean_gain = totals[0:1] / count, totals[1:2] / count

    def normed_grad(value, hidden, inside):
        normed = (hidden - average) * inv_std
        return wide(inside[...], value) * scale * (value - (mean_grad + normed * mean_gain))

    odd = place[0, 0] % 2 == 1

    def beside(one, other, inside):
        value = jnp.where(odd, one[:, 0:middle], other[:, 0:middle])
        return normed_grad(value, jnp.where(odd, one[:, middle:], other[:, middle:]), inside)

    centre = normed_grad(grad[...], second[...], mask)
    above = beside(near, far, mask_above)
    below = beside(far, near, mask_below)
    three = spread(*dims, centre, above, below)
    average, inv_std, scale, shift = affine(sums_first[:, 0:middle], count, params[0:1], params[1:2])
    low = [part.astype(LOW) for part in three]
    total = None
    for j in range(3):
        part = None
        for i in range(3):
            term = lax.dot_general(
                low[2 - i], tap(i, j), (((1,), (1,)), ((), ())), preferred_element_type=FULL
            )
            part = term if part is None else part + term
        part = shifted(part, 1 - j) if j != 1 else part
        total = part if total is None else total + part
    hidden = first[...]
    total = total * wide(mask[...], total) * slope(hidden * scale + shift)
    pre_grad[...] = total
    low_grad[...] = total.astype(LOW)
    sums[:, 0] = spread_sum(sums, total)
    sums[:, 1] = spread_sum(sums, total * ((hidden - average) * inv_std))


def first_backward(sums_first, came, params, first, grad, mask, first_other, grad_other, mask_other, low, sums_in):
    pixels, middle = first.shape
    count = sums_first[0:1, middle : middle + 1]
    totals = jnp.sum(came[...], axis=0)
    sums_in[...] = totals
    average, inv_std, scale, _ = affine(sums_first[:, 0:middle], count, params[0:1], 0.0)
    pairs = ((first, grad, mask), (first_other, grad_other, mask_other))
    for k, (hidden, source, inside) in enumerate(pairs):
        normed = (hidden[...] - average) * inv_std
        value = source[...].astype(FULL) - (totals[0:1] + normed * totals[1:2]) / count
        low[k * pixels : (k + 1) * pixels] = (wide(inside[...], value) * scale * value).astype(LOW)


def assemble(odd, mine, other, shape):
    groups, taps, size, lanes = shape
    quarters = mine.shape[0] // (groups * taps * size)
    channels = quarters * lanes
    pieces = pl.BlockSpec((quarters, groups, 1, size, lanes), lambda t: (0, 0, t, 0, 0))
    return pl.pallas_call(
        mid_assemble,
        grid=(taps,),
        out_shape=jax.ShapeDtypeStruct((taps, channels, channels), FULL),
        in_specs=[pl.BlockSpec(memory_space=pltpu.SMEM), pieces, pieces],
        out_specs=pl.BlockSpec((1, channels, channels), lambda t: (t, 0, 0)),
        compiler_params=pltpu.CompilerParams(vmem_limit_bytes=48 * MIB),
    )(
        odd,
        mine.reshape(quarters, groups, taps, size, lanes),
        other.reshape(quarters, groups, taps, size, lanes),
    )


def halves(value, step):
    _, mine = step
    return half_of(value, 1 - mine, 3), half_of(value, mine, 3)


def contract(left, right):
    return lax.dot_general(left, right, (((0,), (0,)), ((), ())), preferred_element_type=FULL)


def times_transpose(left, weights):
    return lax.dot_general(left, weights, (((1,), (1,)), ((), ())), preferred_element_type=FULL)


def per_device(
    features,
    weight_in,
    gain_in,
    bias_in,
    weight_mid,
    gain_mid,
    bias_mid,
    weight_out,
    gain_out,
    bias_out,
    map_size,
    out_grad,
    pool_grad,
):
    images, height, width, channels = features.shape
    middle = weight_mid.shape[3]
    dims = (images, height, width)
    pixels = images * height * width

    count = lax.axis_size(AXES)
    place = lax.axis_index(ROWS).astype(jnp.int32)
    index = flat_index()
    rows_count = lax.axis_size(ROWS)
    base = index - lax.axis_index("img") % 2 * rows_count

    count = lax.axis_size(AXES)
    flat_features = features.reshape(pixels, channels)
    params_out = jnp.stack([gain_out, bias_out])
    steps = plan()
    core, mine, far_steps = steps[0], steps[0][1], steps[3:]
    place = jnp.stack([place, base, jnp.int32(rows_count), steps[1][1]]).astype(jnp.int32)[None]
    plane, narrow, broad, large = (pixels, middle), (2, middle), (2, channels), (pixels, channels)
    edge, split_rows = (images * width, middle), (height, images * width, middle)
    half_broad = (2, channels // 2)
    half_rows = (height, images * width, middle // 2)
    taps = [pltpu.VMEM(weight_mid.shape, LOW), pltpu.SemaphoreType.DMA((3, 3))]

    first, near, far, sums, params, params_mid, areas, mask, mask_other, mask_above, mask_below = call(
        lambda *refs: first_forward(dims, *refs),
        [
            (plane, FULL),
            (edge, FULL),
            (edge, FULL),
            ((count, 2, middle + LANES), FULL),
            (narrow, FULL),
            (narrow, FULL),
            ((images, LANES), FULL),
            ((pixels, LANES), FULL),
            ((pixels, LANES), FULL),
            ((images * width, LANES), FULL),
            ((images * width, LANES), FULL),
        ],
        place,
        map_size[None],
        gain_in[None],
        bias_in[None],
        gain_mid[None],
        bias_mid[None],
        flat_features,
        weight_in,
        scratch=[
            pltpu.SMEM((1, images), jnp.int32),
            pltpu.VMEM((4, 1, middle), FULL),
            pltpu.VMEM((pixels, channels), LOW),
            pltpu.VMEM((channels, middle), LOW),
            pltpu.SemaphoreType.DMA((5,)),
            pltpu.SemaphoreType.DMA((2, 4)),
        ],
        left=(1, 2, 3, 4, 5, 6, 7),
        limit=60,
    )
    near, far = trade(near, far)
    came, near, far = tie(everyone(sums), near, far)
    split, second, sums, sums_first, sizes = call(
        lambda *refs: mid_forward(dims, *refs),
        [
            (split_rows, LOW),
            (plane, FULL),
            ((count, 2, middle), FULL),
            ((2, middle + LANES), FULL),
            ((2, LANES), FULL),
        ],
        place,
        came,
        params,
        first,
        near,
        far,
        mask,
        mask_above,
        mask_below,
        weight_mid,
        scratch=taps,
        left=(9,),
    )
    acts = swap(half_of(split, 1 - mine, 2), core[0])
    came, acts, first_other = tie(everyone(sums), acts, swap(first, core[0]))
    second_act, normed_sent, normed_kept, third, sums_sent, sums_kept, sums_second = call(
        lambda *refs: out_forward(dims, *refs),
        [
            (plane, LOW),
            (half_rows, LOW),
            (half_rows, LOW),
            (large, FULL),
            (half_broad, FULL),
            (half_broad, FULL),
            (narrow, FULL),
        ],
        place,
        sums_first,
        came,
        params_mid,
        second,
        mask,
        weight_out,
    )
    acts = stack(mine, half_of(split, mine, 2), acts)
    features_came = swap(half_of(flat_features, 1 - mine, 1), core[0])
    came, came_other, acts_came, normed_came, act_other, features_came = tie(
        *everyone_wide(sums_sent, sums_kept, core),
        swap(acts, steps[1][0]),
        swap(normed_sent[None], steps[1][0]),
        swap(second_act, core[0]),
        features_came,
    )
    result, pooled, grad_summed, sums_sent, sums_kept, sums_third = call(
        lambda *refs: out_result(dims, *refs),
        [
            (large, LOW),
            ((images, channels), FULL),
            (large, FULL),
            (half_broad, FULL),
            (half_broad, FULL),
            (broad, FULL),
        ],
        place,
        sums_first,
        came,
        came_other,
        params_out,
        third,
        flat_features,
        out_grad.reshape(pixels, channels),
        pool_grad,
        areas,
        mask,
    )

    acts = merge(acts, acts_came, steps[1])
    normed_sent, normed_kept = halves(merge(normed_kept[None], normed_came, steps[1]), steps[2])
    sums_sent, acts, normed_sent = tie(sums_sent, acts, normed_sent)
    features_pair = jnp.concatenate([half_of(flat_features, mine, 1), features_came])
    features_sent = half_of(features_pair, 1 - steps[1][1], 1)
    features_kept = half_of(features_pair, steps[1][1], 1)
    normed = merge(normed_kept, swap(normed_sent, steps[2][0]), steps[2])
    came, came_other, acts_came, normed, features_sent, features_kept = tie(
        *everyone_wide(sums_sent, sums_kept, core),
        swap(acts, steps[2][0]),
        normed,
        features_sent,
        features_kept,
    )
    third_sent, third_kept, grad_second_pre, grads_sent, grads_kept, near, far, sums, sums_out = call(
        lambda *refs: out_backward(dims, *refs),
        [
            ((pixels, channels // 2), LOW),
            ((pixels, channels // 2), LOW),
            (plane, FULL),
            (half_rows, LOW),
            (half_rows, LOW),
            ((edge[0], 2 * middle), FULL),
            ((edge[0], 2 * middle), FULL),
            ((count, 2, middle), FULL),
            (broad, FULL),
        ],
        place,
        sums_first,
        sums_second,
        sums_third,
        came,
        came_other,
        params_mid,
        params_out,
        third,
        grad_summed,
        second,
        mask,
        weight_out,
        scratch=[pltpu.VMEM(large, LOW)],
    )

    near, far = trade(near, far)
    sums = everyone(sums)
    came = swap(grads_sent[None], steps[1][0])
    sent, kept = halves(merge(grads_kept[None], came, steps[1]), steps[2])
    came = swap(sent, steps[2][0])
    third_came = swap(third_sent, core[0])
    sums, came, third_came, near, far = tie(sums, came, third_came, near, far)
    grads = merge(kept, came, steps[2])
    grad_first_pre, low_grad, sums, sums_mid = call(
        lambda *refs: mid_backward(dims, *refs),
        [(plane, FULL), (plane, LOW), ((count, 2, middle), FULL), (narrow, FULL)],
        place,
        sums_first,
        sums_second,
        sums,
        params,
        params_mid,
        grad_second_pre,
        near,
        far,
        second,
        first,
        mask,
        mask_above,
        mask_below,
        weight_mid,
        scratch=taps,
        left=(14,),
    )
    sums = everyone(sums)
    grad_other = swap(low_grad, core[0])
    grads_came, normed_came = swap(grads, core[0]), swap(normed, core[0])

    def out_rows(which):
        one, two = (half_of(act, which, 1) for act in (second_act, act_other))
        return contract(one, third_kept) + contract(two, third_came)

    odd = (index % 2).astype(jnp.int32).reshape(1, 1)
    def out_chain():
        came = yield out_rows(1 - steps[1][1]).astype(LOW), steps[1][0]
        value = out_rows(steps[1][1]) + came.astype(FULL)
        value = yield from reduce_chain(value, steps[2:])
        value = yield from gather_chain(value.astype(LOW), steps[:0:-1])
        other = yield value, core[0]
        low = mine == 0
        parts = [jnp.where(low, value, other), jnp.where(low, other, value)]
        return jnp.concatenate(parts, axis=1).astype(FULL)

    def mid_chain():
        high, low = steps[1][1], steps[2][1]
        chunk = jnp.where(index % 2 == 0, 2 * high + low, 2 * low + high)
        lanes, deep = grads.shape[-1], acts.shape[-1]
        span = 2 * acts.shape[0] * images * width
        shape = (deep // GROUP // 2, 9, GROUP, lanes)
        sent, kept = call(
            mid_weights,
            [(shape, LOW), (shape, FULL)],
            jnp.stack([index % 2, chunk, steps[2][1], far_steps[0][1]]).astype(jnp.int32)[None],
            sizes[:, :images].astype(jnp.int32),
            sums_first,
            sums_second,
            sums_mid,
            params_mid,
            acts,
            acts_came,
            normed,
            normed_came,
            grads,
            grads_came,
            scratch=[pltpu.VMEM((2, span, deep), LOW), pltpu.VMEM((2, span, 3 * lanes), LOW)],
        )
        came = yield sent.reshape(-1, lanes), far_steps[0][0]
        value = kept.reshape(-1, lanes) + came.astype(FULL)
        value = yield from reduce_chain(value, far_steps[1:])
        value = yield from gather_chain(value.astype(LOW), steps[:0:-1])
        other = yield value, core[0]
        return assemble(odd, value, other, (2 * shape[0], *shape[1:]))

    def in_chain():
        came = yield contract(features_sent, grad_first).astype(LOW), steps[1][0]
        value = contract(features_kept, grad_first) + came.astype(FULL)
        value = yield from reduce_chain(value, steps[2:])
        value = yield from gather_chain(value.astype(LOW), steps[:0:-1])
        other = yield value, core[0]
        return stack(mine, value, other).reshape(-1, middle).astype(FULL)

    chains = Chains()
    mid = mid_chain()
    mid_sent, flips = next(mid)
    chains.begin("out", out_chain(), ())
    came, mid_sent, grad_other = chains.slot(sums, mid_sent, grad_other)
    chains.begin("mid", mid, (), (mid_sent, flips))
    pooled = sum_rows_axis(pooled)
    grad_first, sums_in = call(
        first_backward,
        [((2 * pixels, middle), LOW), (narrow, FULL)],
        sums_first,
        came,
        params,
        first,
        grad_first_pre,
        mask,
        first_other,
        grad_other,
        mask_other,
    )
    entry = in_chain()
    in_sent, in_flips = next(entry)
    in_sent, pooled = chains.slot(in_sent, pooled)
    chains.begin("in", entry, (), (in_sent, in_flips))
    pooled = pooled / areas[:, :1]
    grad_features = grad_summed + times_transpose(grad_first[:pixels], weight_in)
    (grad_features,) = chains.slot(grad_features)
    while chains.running:
        chains.slot()
    grad_weight_in, grad_weight_mid, grad_weight_out = (
        chains.results[name] for name in ("in", "mid", "out")
    )
    whole = (images, height, width, channels)
    return (
        result.astype(LOW).reshape(whole),
        pooled,
        grad_features.reshape(whole),
        grad_weight_in,
        sums_in[1],
        sums_in[0],
        grad_weight_mid.reshape(weight_mid.shape),
        sums_mid[1],
        sums_mid[0],
        grad_weight_out,
        sums_out[1],
        sums_out[0],
    )


def solution(mesh):
    images, rows = mesh.devices.shape
    mesh = Mesh(mesh.devices.reshape(images, rows // 2, 2), AXES)
    tiles, single = P("img", ROWS, None, None), P()
    return jax.shard_map(
        per_device,
        mesh=mesh,
        in_specs=(tiles,) + (single,) * 9 + (P("img"), tiles, P("img", None)),
        out_specs=(tiles, P("img", None), tiles) + (single,) * 9,
        check_vma=False,
    )
```

```python
import jax
import jax.numpy as jnp
from jax import lax
from jax.experimental import pallas as pl
from jax.experimental.pallas import tpu as pltpu
from jax.sharding import Mesh
from jax.sharding import PartitionSpec as P

EPSILON = 1e-05
ROWS = ("half", "low")
AXES = ("img", *ROWS)
MIB = 1 << 20
LOW = jnp.bfloat16
FULL = jnp.float32
GROUP = 16
LANES = 128


def swap(value, flips):
    count = lax.axis_size(AXES)
    return lax.ppermute(value, AXES, [(i, i ^ flips[i & 1]) for i in range(count)])


def bits():
    count, found = lax.axis_size(AXES), []
    while (1 << len(found)) < count:
        found.append(1 << len(found))
    return found


def everyone(copies):
    return lax.all_to_all(copies, AXES, 0, 0)


def everyone_wide(sent, kept, low_step):
    value = kept + swap(sent, low_step[0])
    count = lax.axis_size(AXES[:2])
    mine = lax.all_to_all(jnp.broadcast_to(value[None], (count, *value.shape)), AXES[:2], 0, 0)
    return mine, swap(mine, low_step[0])


def tie(*values):
    return lax.optimization_barrier(values)


def flat_index():
    return lax.axis_index("img") * lax.axis_size(ROWS) + lax.axis_index(ROWS)


def plan():
    order = bits()
    steps = [(bit, bit) for bit in order]
    if len(order) >= 3:
        steps[1], steps[2] = (order[1], order[2]), (order[2], order[1])
    index = flat_index()
    low = index % 2
    chosen = []
    for even, odd in steps:
        chosen.append(((even, odd), jnp.where(low == 0, index // even % 2, index // odd % 2)))
    return chosen


def half_of(value, which, axis=0):
    size = value.shape[axis] // 2
    return lax.dynamic_slice_in_dim(value, which * size, size, axis=axis)


def stack(mine, value, other):
    low = mine == 0
    return jnp.stack([jnp.where(low, value, other), jnp.where(low, other, value)])


def scatter_step(value, step):
    _, mine = step
    return half_of(value, 1 - mine).astype(LOW), half_of(value, mine)


def merge(value, other, step):
    return stack(step[1], value, other).reshape((-1,) + value.shape[1:])


def reduce_chain(value, steps):
    for step in steps:
        sent, kept = scatter_step(value, step)
        came = yield sent, step[0]
        value = kept + came.astype(FULL)
    return value


def gather_chain(value, steps):
    for step in steps:
        came = yield value, step[0]
        value = merge(value, came, step)
    return value


class Chains:
    def __init__(self):
        self.running, self.flying, self.results, self.fresh = {}, {}, {}, []

    def begin(self, name, chain, spans, sent=None):
        self.running[name] = (chain, list(spans))
        self.load(name, next(chain) if sent is None else sent)

    def load(self, name, sent):
        spans = self.running[name][1]
        self.flying[name] = [sent, None, spans.pop(0) if spans else 1]

    def slot(self, *extra, held=True):
        due, fresh = [], list(self.fresh)
        for name, flight in self.flying.items():
            if flight[1] is None:
                flight[1] = swap(*flight[0])
            flight[2] -= 1
            if flight[2] <= 0:
                due.append(name)
        done = [self.flying[name][1] for name in due] + list(extra)
        if held:
            done = tie(*done, *(self.results[name] for name in fresh))
            for name, value in zip(fresh, done[len(due) + len(extra) :]):
                self.results[name] = value
            self.fresh = []
        for name, value in zip(due, done):
            try:
                self.load(name, self.running[name][0].send(value))
            except StopIteration as end:
                self.results[name] = end.value
                self.fresh.append(name)
                del self.running[name], self.flying[name]
        return done[len(due) : len(due) + len(extra)]


def sum_rows_axis(value):
    count, bit = lax.axis_size(ROWS), 1
    while bit < count:
        value = value + lax.ppermute(value, ROWS, [(i, i ^ bit) for i in range(count)])
        bit *= 2
    return value


def trade(near, far):
    count = lax.axis_size(ROWS)
    pairs = [(i, i + 1) for i in range(1, count - 1, 2)]
    return (
        lax.ppermute(near, ROWS, [(i, i ^ 1) for i in range(count)]),
        lax.ppermute(far, ROWS, pairs + [(b, a) for a, b in pairs]),
    )


def call(kernel, outs, *args, scratch=(), left=(), limit=60):
    def place(at, arg):
        if at in left:
            return pl.BlockSpec(memory_space=pltpu.HBM)
        return pl.BlockSpec(memory_space=pltpu.SMEM if arg.dtype == jnp.int32 else pltpu.VMEM)

    return pl.pallas_call(
        kernel,
        out_shape=[jax.ShapeDtypeStruct(shape, kind) for shape, kind in outs],
        in_specs=[place(at, arg) for at, arg in enumerate(args)],
        out_specs=[pl.BlockSpec(memory_space=pltpu.VMEM)] * len(outs),
        scratch_shapes=list(scratch),
        compiler_params=pltpu.CompilerParams(vmem_limit_bytes=limit * MIB),
    )(*args)


def logistic(values):
    return 0.5 * jnp.tanh(0.5 * values) + 0.5


def slope(values):
    s = logistic(values)
    return s * (1.0 + values * (1.0 - s))


def shifted(values, by):
    return pltpu.roll(values, (-by) % values.shape[0], 0)


def spread(images, height, width, main, above, below):
    channels = main.shape[-1]
    main = main.reshape(images, height, width, channels)
    above = above.reshape(images, 1, width, channels)
    below = below.reshape(images, 1, width, channels)
    flat = (images * height * width, channels)
    return (
        jnp.concatenate([above, main[:, :-1]], axis=1).reshape(flat),
        main.reshape(flat),
        jnp.concatenate([main[:, 1:], below], axis=1).reshape(flat),
    )


def wide(mask, like):
    return jnp.concatenate([mask] * (like.shape[1] // mask.shape[1]), axis=1)


def edges_of(dims, place, value, near, far):
    images, height, width = dims
    value = value.reshape(images, height, width, -1)
    top = value[:, 0].reshape(images * width, -1)
    bottom = value[:, height - 1].reshape(images * width, -1)
    odd = place[0, 0] % 2 == 1
    near[...] = jnp.where(odd, top, bottom).astype(near.dtype)
    far[...] = jnp.where(odd, bottom, top).astype(far.dtype)


def first_forward(
    dims, place, map_size, gain, bias, gain_mid, bias_mid, features, weight,
    first, near, far, sums, params, params_mid, areas, mask, mask_other, mask_above, mask_below,
    sizes, few, left, right, few_sems, sems,
):
    images, height, width = dims
    lanes = mask.shape[1]
    parts = sems.shape[1]
    deep = left.shape[1] // parts
    small = [pltpu.make_async_copy(map_size, sizes, few_sems.at[0])]
    for k, source in enumerate((gain, bias, gain_mid, bias_mid)):
        small.append(pltpu.make_async_copy(source, few.at[k], few_sems.at[k + 1]))
    for copy in small:
        copy.start()

    def load(k):
        span = pl.ds(k * deep, deep)
        return (
            pltpu.make_async_copy(features.at[:, span], left.at[:, span], sems.at[0, k]),
            pltpu.make_async_copy(weight.at[span, :], right.at[span, :], sems.at[1, k]),
        )

    for k in range(parts):
        for copy in load(k):
            copy.start()
    for copy in small:
        copy.wait()

    def inside(start, count):
        spot = lax.broadcasted_iota(jnp.int32, (count * width, lanes), 0)
        row, column = start + spot // width, spot % width
        parts = []
        for n in range(images):
            size = sizes[0, n]
            here = (row >= 0) & (row < size) & (column < size)
            parts.append(jnp.where(here, 1.0, 0.0))
        return jnp.concatenate(parts, axis=0)

    start = place[0, 0] * height
    kept = inside(start, height)
    mask[...] = kept
    mask_other[...] = inside((place[0, 0] + 1 - 2 * (place[0, 0] % 2)) * height, height)
    mask_above[...] = inside(start - 1, 1)
    mask_below[...] = inside(start + height, 1)
    params[0:1], params[1:2] = few[0], few[1]
    params_mid[0:1], params_mid[1:2] = few[2], few[3]
    spot = lax.broadcasted_iota(jnp.int32, areas.shape, 0)
    area = jnp.zeros(areas.shape, FULL)
    for n in range(images):
        area = jnp.where(spot == n, (sizes[0, n] * sizes[0, n]).astype(FULL), area)
    areas[...] = area
    total = None
    for k in range(parts):
        for copy in load(k):
            copy.wait()
        span = pl.ds(k * deep, deep)
        part = jnp.dot(left[:, span], right[span, :], preferred_element_type=FULL)
        total = part if total is None else total + part
    first[...] = total
    masked = total * wide(kept, total)
    middle = total.shape[1]
    sums[:, 0, 0:middle] = spread_sum(sums, masked)
    sums[:, 1, 0:middle] = spread_sum(sums, masked * total)
    sums[:, 0, middle:] = spread_sum(sums, kept)
    lane = lax.broadcasted_iota(jnp.int32, (1, lanes), 1)
    told = jnp.zeros((1, lanes), FULL)
    for n in range(images):
        told = jnp.where(lane == n, sizes[0, n].astype(FULL), told)
    sums[:, 1, middle:] = jnp.broadcast_to(told, (sums.shape[0], lanes))
    edges_of(dims, place, total, near, far)


def spread_sum(copies, values):
    total = jnp.sum(values, axis=0, keepdims=True)
    return jnp.broadcast_to(total, (copies.shape[0], total.shape[1]))


def fetch(weight, held, sems):
    def load(i, j):
        return pltpu.make_async_copy(weight.at[i, j], held.at[i, j], sems.at[i, j])

    for j in range(3):
        for i in range(3):
            load(i, j).start()

    def tap(i, j):
        load(i, j).wait()
        return held[i, j]

    return tap


def put_sums(dims, place, at, values, others, sent, kept):
    chunk, half = values.shape[1], sent.shape[1]
    span = pl.ds(at % half, chunk)
    mine = (place[0, 0] % 2 == 1) == (at >= half)
    for k, value in enumerate((values, others)):
        total = jnp.sum(value, axis=0, keepdims=True)
        kept[k : k + 1, span] = jnp.where(mine, total, kept[k : k + 1, span])
        sent[k : k + 1, span] = jnp.where(mine, sent[k : k + 1, span], total)


def take_sums(place, at, chunk, mine, other):
    half = mine.shape[2]
    span = pl.ds(at % half, chunk)
    here = (place[0, 0] % 2 == 1) == (at >= half)
    return jnp.where(here, jnp.sum(mine[:, :, span], axis=0), jnp.sum(other[:, :, span], axis=0))


def affine(sums, count, gain, bias):
    average = sums[0:1] / count
    inv_std = lax.rsqrt(sums[1:2] / count - average * average + EPSILON)
    scale = inv_std * gain
    return average, inv_std, scale, bias - average * scale


def mid_forward(
    dims, place, came, params, first, near, far, mask, mask_above, mask_below, weight,
    split, second, sums, sums_first, sizes, held, sems,
):
    tap = fetch(weight, held, sems)
    middle = first.shape[1]
    totals = jnp.sum(came[...], axis=0)
    sums_first[...] = totals
    for y in range(2):
        sizes[y : y + 1] = came[place[0, 1] + y * place[0, 2], 1:2, middle:]
    count = totals[0:1, middle : middle + 1]
    _, _, scale, shift = affine(totals[:, 0:middle], count, params[0:1], params[1:2])

    def act(hidden, inside):
        pre = hidden * scale + shift
        return pre * logistic(pre) * wide(inside[...], pre)

    odd = place[0, 0] % 2 == 1
    centre = act(first[...], mask)
    above = act(jnp.where(odd, near[...], far[...]), mask_above)
    below = act(jnp.where(odd, far[...], near[...]), mask_below)
    three = spread(*dims, centre, above, below)
    x3 = [part.astype(LOW) for part in three]
    flat_rows(dims, centre, split)
    total = None
    for j in range(3):
        part = None
        for i in range(3):
            term = jnp.dot(x3[i], tap(i, j), preferred_element_type=FULL)
            part = term if part is None else part + term
        part = shifted(part, j - 1) if j != 1 else part
        total = part if total is None else total + part
    second[...] = total
    masked = total * wide(mask[...], total)
    sums[:, 0] = spread_sum(sums, masked)
    sums[:, 1] = spread_sum(sums, masked * total)


def flat_rows(dims, value, out):
    images, height, width = dims
    value = value.reshape(images, height, width, -1)
    for r in range(height):
        out[r] = value[:, r].reshape(images * width, -1).astype(LOW)


def flat_halves(dims, place, value, sent, kept):
    quarter = value.shape[1] // 4
    odd, high = place[0, 0] % 2 == 1, place[0, 3] == 1
    parts = [value[:, k * quarter : (k + 1) * quarter] for k in range(4)]
    parts[1], parts[2] = jnp.where(odd, parts[2], parts[1]), jnp.where(odd, parts[1], parts[2])
    one, two = jnp.concatenate(parts[:2], axis=1), jnp.concatenate(parts[2:], axis=1)
    flat_rows(dims, jnp.where(high, one, two), sent)
    flat_rows(dims, jnp.where(high, two, one), kept)


def out_forward(
    dims, place, sums_first, came, params_mid, second, mask, weight,
    act, normed_sent, normed_kept, third, sums_sent, sums_kept, sums_second,
):
    middle = second.shape[1]
    totals = jnp.sum(came[...], axis=0)
    sums_second[...] = totals
    count = sums_first[0:1, middle : middle + 1]
    average, inv_std, scale, shift = affine(totals, count, params_mid[0:1], params_mid[1:2])
    hidden = second[...]
    pre = hidden * scale + shift
    inside = wide(mask[...], hidden)
    act[...] = (pre * logistic(pre) * inside).astype(LOW)
    flat_halves(dims, place, (hidden - average) * inv_std, normed_sent, normed_kept)
    for at in range(0, third.shape[1], middle):
        span = pl.ds(at, middle)
        total = jnp.dot(act[...], weight[:, span], preferred_element_type=FULL)
        third[:, span] = total
        masked = total * inside
        put_sums(dims, place, at, masked, masked * total, sums_sent, sums_kept)


def out_result(
    dims, place, sums_first, came, other, params_out, third, features, out_grad, pool_grad, areas, mask,
    result, pooled, grad, sums_sent, sums_kept, sums_third,
):
    images, height, width = dims
    chunk = sums_first.shape[1] - mask.shape[1]
    count = sums_first[0:1, chunk : chunk + 1]
    inside = jnp.concatenate([mask[...]] * (chunk // mask.shape[1]), axis=1)
    area = jnp.concatenate([areas[...]] * (chunk // mask.shape[1]), axis=1)
    for at in range(0, third.shape[1], chunk):
        span = pl.ds(at, chunk)
        totals = take_sums(place, at, chunk, came, other)
        sums_third[:, span] = totals
        average, inv_std, _, _ = affine(totals, count, 1.0, 0.0)
        normed = (third[:, span] - average) * inv_std
        summed = params_out[0:1, span] * normed + params_out[1:2, span] + features[:, span].astype(FULL)
        gate = logistic(summed)
        value = summed * gate * inside
        result[:, span] = value.astype(LOW)
        pooled[:, span] = jnp.sum(value.reshape(images, height * width, chunk), axis=1)
        share = (pool_grad[:, span] / area)[:, None]
        total = out_grad[:, span].astype(FULL).reshape(images, height * width, chunk) + share
        total = total.reshape(inside.shape) * inside * (gate * (1.0 + summed * (1.0 - gate)))
        grad[:, span] = total
        put_sums(dims, place, at, total, total * normed, sums_sent, sums_kept)


def out_backward(
    dims, place, sums_first, sums_second, sums_third, came, other, params_mid, params_out, third, grad, second,
    mask, weight, third_sent, third_kept, pre_grad, rows_sent, rows_kept, near, far, sums, sums_out, lows,
):
    chunk = second.shape[1]
    count = sums_first[0:1, chunk : chunk + 1]
    inside = wide(mask[...], second)
    back = None
    for at in range(0, third.shape[1], chunk):
        span = pl.ds(at, chunk)
        average, inv_std, scale, _ = affine(sums_third[:, span], count, params_out[0:1, span], 0.0)
        normed = (third[:, span] - average) * inv_std
        totals = take_sums(place, at, chunk, came, other)
        sums_out[:, span] = totals
        mean = (totals[0:1] + normed * totals[1:2]) / count
        low = (inside * scale * (grad[:, span] - mean)).astype(LOW)
        lows[:, span] = low
        part = lax.dot_general(
            low, weight[:, span], (((1,), (1,)), ((), ())), preferred_element_type=FULL
        )
        back = part if back is None else back + part
    average, inv_std, scale, shift = affine(sums_second[...], count, params_mid[0:1], params_mid[1:2])
    hidden = second[...]
    back = back * inside * slope(hidden * scale + shift)
    pre_grad[...] = back
    flat_halves(dims, place, back, rows_sent, rows_kept)
    odd, half = place[0, 0] % 2 == 1, third.shape[1] // 2
    one, two = lows[:, 0:half], lows[:, half:]
    third_sent[...] = jnp.where(odd, one, two)
    third_kept[...] = jnp.where(odd, two, one)
    sums[:, 0] = spread_sum(sums, back)
    normed = (hidden - average) * inv_std
    sums[:, 1] = spread_sum(sums, back * normed)
    edges_of(dims, place, jnp.concatenate([back, normed], axis=1), near, far)


def mid_weights(
    place, sizes, sums_first, sums_second, sums_grad, params_mid,
    acts_mine, acts_came, normed_mine, normed_came, grads_mine, grads_came, sent, kept, left, right,
):
    groups, _, size, channels = kept.shape
    pixels = acts_mine.shape[2]
    images = sizes.shape[1]
    width = pixels // images
    swapped, high = place[0, 0] == 1, place[0, 3] == 1
    middle = sums_grad.shape[1]
    count = sums_first[0:1, middle : middle + 1]
    span = pl.ds(pl.multiple_of(place[0, 1] * channels, channels), channels)
    average = sums_second[0:1, span] / count
    inv_std = lax.rsqrt(sums_second[1:2, span] / count - average * average + EPSILON)
    scale = inv_std * params_mid[0:1, span]
    mean_grad, mean_gain = sums_grad[0:1, span] / count, sums_grad[1:2, span] / count
    column = lax.broadcasted_iota(jnp.int32, (width, channels), 0)
    for y in range(2):
        for x in range(2):
            for c in range(2):
                spot = jnp.where(swapped, 2 * y + c, 2 * x + c)
                here = jnp.where(swapped, x, y) == place[0, 2]
                four = 2 * x + y if c else 2 * y + x
                own = place[0, 0] == c
                rows = pl.ds(((2 * y + x) * 2 + c) * pixels, pixels)
                for r in range(2):
                    left[r, rows, :] = jnp.where(here, acts_mine[spot, r], acts_came[spot, r])
                    row = (2 * x + c) * 2 + r
                    inside = []
                    for n in range(images):
                        extent = jnp.where(row < sizes[y, n], sizes[y, n], 0)
                        inside.append(jnp.where(column < extent, 1.0, 0.0))
                    value = jnp.where(own, grads_mine[four, r], grads_came[four, r]).astype(FULL)
                    normed = jnp.where(own, normed_mine[four, r], normed_came[four, r])
                    value = value - (mean_grad + normed.astype(FULL) * mean_gain)
                    value = value * scale * jnp.concatenate(inside, axis=0)
                    right[r, rows, 0:channels] = value.astype(LOW)
    for r in range(2):
        grad = right[r, :, 0:channels].astype(FULL)
        right[r, :, channels : 2 * channels] = shifted(grad, 1).astype(LOW)
        right[r, :, 2 * channels :] = shifted(grad, -1).astype(LOW)
    span, image = 3 * pixels, 4 * pixels

    def product(r_left, at_left, r_right, at_right, count):
        return lax.dot_general(
            left[r_left, pl.ds(at_left, count), :],
            right[r_right, pl.ds(at_right, count), :],
            (((0,), (0,)), ((), ())),
            preferred_element_type=FULL,
        )

    def crossed(r_left, r_right, skip_left, skip_right):
        part = product(r_left, 0, r_right, 0, 2 * image)
        for y in range(2):
            part = part + product(
                r_right, y * image + skip_left, r_left, y * image + skip_right, span
            )
        return part

    taps = (
        crossed(0, 1, 0, pixels),
        product(0, 0, 0, 0, 2 * image) + product(1, 0, 1, 0, 2 * image),
        crossed(1, 0, pixels, 0),
    )
    for i in range(3):
        for j, place in ((1, 0), (0, 1), (2, 2)):
            part = taps[i][:, place * channels : (place + 1) * channels]
            one = part[0 : groups * size].reshape(groups, size, channels)
            two = part[groups * size :].reshape(groups, size, channels)
            sent[:, 3 * i + j] = jnp.where(high, one, two).astype(LOW)
            kept[:, 3 * i + j] = jnp.where(high, two, one)


def mid_assemble(odd, mine, other, total):
    quarters, groups, _, size, lanes = mine.shape
    half = groups * size
    swapped = odd[0, 0] == 1
    for q, turned in enumerate((0, 2, 1, 3)):
        span = pl.ds(q * lanes, lanes)
        even = jnp.where(swapped, other[q, :, 0], mine[q, :, 0])
        total[0, 0:half, span] = even.astype(FULL).reshape(half, lanes)
        uneven = jnp.where(swapped, mine[turned, :, 0], other[turned, :, 0])
        total[0, half:, span] = uneven.astype(FULL).reshape(half, lanes)


def mid_backward(
    dims, place, sums_first, sums_second, came, params, params_mid, grad, near, far,
    second, first, mask, mask_above, mask_below, weight, pre_grad, low_grad, sums, sums_mid, held, sems,
):
    tap = fetch(weight, held, sems)
    middle = first.shape[1]
    count = sums_first[0:1, middle : middle + 1]
    totals = jnp.sum(came[...], axis=0)
    sums_mid[...] = totals
    average, inv_std, scale, shift = affine(sums_second[...], count, params_mid[0:1], params_mid[1:2])
    mean_grad, mean_gain = totals[0:1] / count, totals[1:2] / count

    def normed_grad(value, normed, inside):
        return wide(inside[...], value) * scale * (value - (mean_grad + normed * mean_gain))

    odd = place[0, 0] % 2 == 1

    def beside(one, other, inside):
        value = jnp.where(odd, one[...], other[...]).astype(FULL)
        return normed_grad(value[:, 0:middle], value[:, middle:], inside)

    centre = normed_grad(grad[...], (second[...] - average) * inv_std, mask)
    above = beside(near, far, mask_above)
    below = beside(far, near, mask_below)
    three = spread(*dims, centre, above, below)
    average, inv_std, scale, shift = affine(sums_first[:, 0:middle], count, params[0:1], params[1:2])
    low = [part.astype(LOW) for part in three]
    total = None
    for j in range(3):
        part = None
        for i in range(3):
            term = lax.dot_general(
                low[2 - i], tap(i, j), (((1,), (1,)), ((), ())), preferred_element_type=FULL
            )
            part = term if part is None else part + term
        part = shifted(part, 1 - j) if j != 1 else part
        total = part if total is None else total + part
    hidden = first[...]
    total = total * wide(mask[...], total) * slope(hidden * scale + shift)
    pre_grad[...] = total
    low_grad[...] = total.astype(LOW)
    sums[:, 0] = spread_sum(sums, total)
    sums[:, 1] = spread_sum(sums, total * ((hidden - average) * inv_std))


def contract_in(left, right):
    return lax.dot_general(left, right, (((0,), (0,)), ((), ())), preferred_element_type=FULL)


def put_halves(place, total, sent, kept):
    half = total.shape[0] // 2
    high = place[0, 3] == 1
    one, two = total[0:half], total[half:]
    sent[...] = jnp.where(high, one, two).astype(LOW)
    kept[...] = jnp.where(high, two, one)


def first_backward(
    place, sums_first, came, params, first, grad, mask, first_other, grad_other, mask_other, features,
    low, sums_in, sent, kept, both,
):
    pixels, middle = first.shape
    count = sums_first[0:1, middle : middle + 1]
    totals = jnp.sum(came[...], axis=0)
    sums_in[...] = totals
    average, inv_std, scale, _ = affine(sums_first[:, 0:middle], count, params[0:1], 0.0)
    pairs = ((first, grad, mask), (first_other, grad_other, mask_other))
    for k, (hidden, source, inside) in enumerate(pairs):
        normed = (hidden[...] - average) * inv_std
        value = source[...].astype(FULL) - (totals[0:1] + normed * totals[1:2]) / count
        both[k * pixels : (k + 1) * pixels] = (wide(inside[...], value) * scale * value).astype(LOW)
    low[...] = both[0:pixels]
    put_halves(place, contract_in(features[...], both[...]), sent, kept)


def out_weights(place, act, act_other, third, third_other, sent, kept):
    total = contract_in(act[...], third[...]) + contract_in(act_other[...], third_other[...])
    put_halves(place, total, sent, kept)


def assemble(odd, mine, other, shape):
    groups, taps, size, lanes = shape
    quarters = mine.shape[0] // (groups * taps * size)
    channels = quarters * lanes
    pieces = pl.BlockSpec((quarters, groups, 1, size, lanes), lambda t: (0, 0, t, 0, 0))
    return pl.pallas_call(
        mid_assemble,
        grid=(taps,),
        out_shape=jax.ShapeDtypeStruct((taps, channels, channels), FULL),
        in_specs=[pl.BlockSpec(memory_space=pltpu.SMEM), pieces, pieces],
        out_specs=pl.BlockSpec((1, channels, channels), lambda t: (t, 0, 0)),
        compiler_params=pltpu.CompilerParams(vmem_limit_bytes=48 * MIB),
    )(
        odd,
        mine.reshape(quarters, groups, taps, size, lanes),
        other.reshape(quarters, groups, taps, size, lanes),
    )


def halves(value, step):
    _, mine = step
    return half_of(value, 1 - mine, 3), half_of(value, mine, 3)


def contract(left, right):
    return lax.dot_general(left, right, (((0,), (0,)), ((), ())), preferred_element_type=FULL)


def times_transpose(left, weights):
    return lax.dot_general(left, weights, (((1,), (1,)), ((), ())), preferred_element_type=FULL)


def per_device(
    features,
    weight_in,
    gain_in,
    bias_in,
    weight_mid,
    gain_mid,
    bias_mid,
    weight_out,
    gain_out,
    bias_out,
    map_size,
    out_grad,
    pool_grad,
):
    images, height, width, channels = features.shape
    middle = weight_mid.shape[3]
    dims = (images, height, width)
    pixels = images * height * width

    count = lax.axis_size(AXES)
    place = lax.axis_index(ROWS).astype(jnp.int32)
    index = flat_index()
    rows_count = lax.axis_size(ROWS)
    base = index - lax.axis_index("img") % 2 * rows_count

    count = lax.axis_size(AXES)
    flat_features = features.reshape(pixels, channels)
    params_out = jnp.stack([gain_out, bias_out])
    steps = plan()
    core, mine, far_steps = steps[0], steps[0][1], steps[3:]
    place = jnp.stack([place, base, jnp.int32(rows_count), steps[1][1]]).astype(jnp.int32)[None]
    plane, narrow, broad, large = (pixels, middle), (2, middle), (2, channels), (pixels, channels)
    edge, split_rows = (images * width, middle), (height, images * width, middle)
    half_broad = (2, channels // 2)
    half_rows = (height, images * width, middle // 2)
    taps = [pltpu.VMEM(weight_mid.shape, LOW), pltpu.SemaphoreType.DMA((3, 3))]

    first, near, far, sums, params, params_mid, areas, mask, mask_other, mask_above, mask_below = call(
        lambda *refs: first_forward(dims, *refs),
        [
            (plane, FULL),
            (edge, FULL),
            (edge, FULL),
            ((count, 2, middle + LANES), FULL),
            (narrow, FULL),
            (narrow, FULL),
            ((images, LANES), FULL),
            ((pixels, LANES), FULL),
            ((pixels, LANES), FULL),
            ((images * width, LANES), FULL),
            ((images * width, LANES), FULL),
        ],
        place,
        map_size[None],
        gain_in[None],
        bias_in[None],
        gain_mid[None],
        bias_mid[None],
        flat_features,
        weight_in,
        scratch=[
            pltpu.SMEM((1, images), jnp.int32),
            pltpu.VMEM((4, 1, middle), FULL),
            pltpu.VMEM((pixels, channels), LOW),
            pltpu.VMEM((channels, middle), LOW),
            pltpu.SemaphoreType.DMA((5,)),
            pltpu.SemaphoreType.DMA((2, 4)),
        ],
        left=(1, 2, 3, 4, 5, 6, 7),
        limit=60,
    )
    near, far = trade(near, far)
    came, near, far = tie(everyone(sums), near, far)
    split, second, sums, sums_first, sizes = call(
        lambda *refs: mid_forward(dims, *refs),
        [
            (split_rows, LOW),
            (plane, FULL),
            ((count, 2, middle), FULL),
            ((2, middle + LANES), FULL),
            ((2, LANES), FULL),
        ],
        place,
        came,
        params,
        first,
        near,
        far,
        mask,
        mask_above,
        mask_below,
        weight_mid,
        scratch=taps,
        left=(9,),
    )
    acts = swap(half_of(split, 1 - mine, 2), core[0])
    came, acts, first_other = tie(everyone(sums), acts, swap(first, core[0]))
    second_act, normed_sent, normed_kept, third, sums_sent, sums_kept, sums_second = call(
        lambda *refs: out_forward(dims, *refs),
        [
            (plane, LOW),
            (half_rows, LOW),
            (half_rows, LOW),
            (large, FULL),
            (half_broad, FULL),
            (half_broad, FULL),
            (narrow, FULL),
        ],
        place,
        sums_first,
        came,
        params_mid,
        second,
        mask,
        weight_out,
    )
    acts = stack(mine, half_of(split, mine, 2), acts)
    features_came = swap(half_of(flat_features, 1 - mine, 1), core[0])
    came, came_other, acts_came, normed_came, act_other, features_came = tie(
        *everyone_wide(sums_sent, sums_kept, core),
        swap(acts, steps[1][0]),
        swap(normed_sent[None], steps[1][0]),
        swap(second_act, core[0]),
        features_came,
    )
    result, pooled, grad_summed, sums_sent, sums_kept, sums_third = call(
        lambda *refs: out_result(dims, *refs),
        [
            (large, LOW),
            ((images, channels), FULL),
            (large, FULL),
            (half_broad, FULL),
            (half_broad, FULL),
            (broad, FULL),
        ],
        place,
        sums_first,
        came,
        came_other,
        params_out,
        third,
        flat_features,
        out_grad.reshape(pixels, channels),
        pool_grad,
        areas,
        mask,
    )

    acts = merge(acts, acts_came, steps[1])
    normed_sent, normed_kept = halves(merge(normed_kept[None], normed_came, steps[1]), steps[2])
    sums_sent, acts, normed_sent = tie(sums_sent, acts, normed_sent)
    features_pair = jnp.concatenate([half_of(flat_features, mine, 1), features_came])
    came, came_other, acts_came, features_pair = tie(
        *everyone_wide(sums_sent, sums_kept, core),
        swap(acts, steps[2][0]),
        features_pair,
    )
    normed_came = swap(normed_sent, steps[2][0])
    third_sent, third_kept, grad_second_pre, grads_sent, grads_kept, near, far, sums, sums_out = call(
        lambda *refs: out_backward(dims, *refs),
        [
            ((pixels, channels // 2), LOW),
            ((pixels, channels // 2), LOW),
            (plane, FULL),
            (half_rows, LOW),
            (half_rows, LOW),
            ((edge[0], 2 * middle), LOW),
            ((edge[0], 2 * middle), LOW),
            ((count, 2, middle), FULL),
            (broad, FULL),
        ],
        place,
        sums_first,
        sums_second,
        sums_third,
        came,
        came_other,
        params_mid,
        params_out,
        third,
        grad_summed,
        second,
        mask,
        weight_out,
        scratch=[pltpu.VMEM(large, LOW)],
    )

    near, far = trade(near, far)
    sums = everyone(sums)
    came = swap(grads_sent[None], steps[1][0])
    sent, kept = halves(merge(grads_kept[None], came, steps[1]), steps[2])
    came = swap(sent, steps[2][0])
    third_came = swap(third_sent, core[0])
    out_sent, out_kept = call(
        out_weights,
        [((middle // 2, channels // 2), LOW), ((middle // 2, channels // 2), FULL)],
        place,
        second_act,
        act_other,
        third_kept,
        third_came,
    )
    sums, came, out_sent, near, far = tie(sums, came, out_sent, near, far)
    grads = merge(kept, came, steps[2])
    grad_first_pre, low_grad, sums, sums_mid = call(
        lambda *refs: mid_backward(dims, *refs),
        [(plane, FULL), (plane, LOW), ((count, 2, middle), FULL), (narrow, FULL)],
        place,
        sums_first,
        sums_second,
        sums,
        params,
        params_mid,
        grad_second_pre,
        near,
        far,
        second,
        first,
        mask,
        mask_above,
        mask_below,
        weight_mid,
        scratch=taps,
        left=(14,),
    )
    sums, normed_came = tie(sums, normed_came)
    normed = merge(normed_kept, normed_came, steps[2])
    sums = everyone(sums)
    grad_other = swap(low_grad, core[0])
    grads_came, normed_came = swap(grads, core[0]), swap(normed, core[0])

    odd = (index % 2).astype(jnp.int32).reshape(1, 1)

    def out_chain():
        came = yield out_sent, steps[1][0]
        value = out_kept + came.astype(FULL)
        value = yield from reduce_chain(value, steps[2:])
        value = yield from gather_chain(value.astype(LOW), steps[:0:-1])
        other = yield value, core[0]
        low = mine == 0
        parts = [jnp.where(low, value, other), jnp.where(low, other, value)]
        return jnp.concatenate(parts, axis=1).astype(FULL)

    def mid_chain():
        high, low = steps[1][1], steps[2][1]
        chunk = jnp.where(index % 2 == 0, 2 * high + low, 2 * low + high)
        lanes, deep = grads.shape[-1], acts.shape[-1]
        span = 2 * acts.shape[0] * images * width
        shape = (deep // GROUP // 2, 9, GROUP, lanes)
        sent, kept = call(
            mid_weights,
            [(shape, LOW), (shape, FULL)],
            jnp.stack([index % 2, chunk, steps[2][1], far_steps[0][1]]).astype(jnp.int32)[None],
            sizes[:, :images].astype(jnp.int32),
            sums_first,
            sums_second,
            sums_mid,
            params_mid,
            acts,
            acts_came,
            normed,
            normed_came,
            grads,
            grads_came,
            scratch=[pltpu.VMEM((2, span, deep), LOW), pltpu.VMEM((2, span, 3 * lanes), LOW)],
        )
        came = yield sent.reshape(-1, lanes), far_steps[0][0]
        value = kept.reshape(-1, lanes) + came.astype(FULL)
        value = yield from reduce_chain(value, far_steps[1:])
        value = yield from gather_chain(value.astype(LOW), steps[:0:-1])
        other = yield value, core[0]
        return assemble(odd, value, other, (2 * shape[0], *shape[1:]))

    def in_chain():
        came = yield in_sent, steps[1][0]
        value = in_kept + came.astype(FULL)
        value = yield from reduce_chain(value, steps[2:])
        value = yield from gather_chain(value.astype(LOW), steps[:0:-1])
        other = yield value, core[0]
        return stack(mine, value, other).reshape(-1, middle).astype(FULL)

    chains = Chains()
    mid = mid_chain()
    mid_sent, flips = next(mid)
    came, mid_sent, grad_other, out_sent = tie(sums, mid_sent, grad_other, out_sent)
    chains.begin("out", out_chain(), ())
    chains.begin("mid", mid, (), (mid_sent, flips))
    grad_first, sums_in, in_sent, in_kept = call(
        first_backward,
        [
            (plane, LOW),
            (narrow, FULL),
            ((channels // 4, middle), LOW),
            ((channels // 4, middle), FULL),
        ],
        place,
        sums_first,
        came,
        params,
        first,
        grad_first_pre,
        mask,
        first_other,
        grad_other,
        mask_other,
        features_pair,
        scratch=[pltpu.VMEM((2 * pixels, middle), LOW)],
    )
    chains.slot(held=False)
    chains.begin("in", in_chain(), ())
    grad_features = grad_summed + times_transpose(grad_first, weight_in)
    (grad_features,) = chains.slot(grad_features)
    chains.slot()
    (pooled,) = chains.slot(pooled)
    (pooled,) = chains.slot(sum_rows_axis(pooled) / areas[:, :1])
    while chains.running:
        chains.slot()
    grad_weight_in, grad_weight_mid, grad_weight_out = (
        chains.results[name] for name in ("in", "mid", "out")
    )
    whole = (images, height, width, channels)
    return (
        result.astype(LOW).reshape(whole),
        pooled,
        grad_features.reshape(whole),
        grad_weight_in,
        sums_in[1],
        sums_in[0],
        grad_weight_mid.reshape(weight_mid.shape),
        sums_mid[1],
        sums_mid[0],
        grad_weight_out,
        sums_out[1],
        sums_out[0],
    )


def solution(mesh):
    images, rows = mesh.devices.shape
    mesh = Mesh(mesh.devices.reshape(images, rows // 2, 2), AXES)
    tiles, single = P("img", ROWS, None, None), P()
    return jax.shard_map(
        per_device,
        mesh=mesh,
        in_specs=(tiles,) + (single,) * 9 + (P("img"), tiles, P("img", None)),
        out_specs=(tiles, P("img", None), tiles) + (single,) * 9,
        check_vma=False,
    )
```

```python
import jax
import jax.numpy as jnp
from jax import lax
from jax.experimental import pallas as pl
from jax.experimental.pallas import tpu as pltpu
from jax.sharding import Mesh
from jax.sharding import PartitionSpec as P

EPSILON = 1e-05
ROWS = ("half", "low")
AXES = ("img", *ROWS)
MIB = 1 << 20
LOW = jnp.bfloat16
FULL = jnp.float32
GROUP = 16
LANES = 128


def swap(value, flips):
    count = lax.axis_size(AXES)
    return lax.ppermute(value, AXES, [(i, i ^ flips[i & 1]) for i in range(count)])


def bits():
    count, found = lax.axis_size(AXES), []
    while (1 << len(found)) < count:
        found.append(1 << len(found))
    return found


def everyone(copies):
    return lax.all_to_all(copies, AXES, 0, 0)


def everyone_wide(sent, kept, low_step):
    value = kept + swap(sent, low_step[0])
    count = lax.axis_size(AXES[:2])
    mine = lax.all_to_all(jnp.broadcast_to(value[None], (count, *value.shape)), AXES[:2], 0, 0)
    return mine, swap(mine, low_step[0])


def tie(*values):
    return lax.optimization_barrier(values)


def flat_index():
    return lax.axis_index("img") * lax.axis_size(ROWS) + lax.axis_index(ROWS)


def plan():
    order = bits()
    steps = [(bit, bit) for bit in order]
    if len(order) >= 3:
        steps[1], steps[2] = (order[1], order[2]), (order[2], order[1])
    index = flat_index()
    low = index % 2
    chosen = []
    for even, odd in steps:
        chosen.append(((even, odd), jnp.where(low == 0, index // even % 2, index // odd % 2)))
    return chosen


def half_of(value, which, axis=0):
    size = value.shape[axis] // 2
    return lax.dynamic_slice_in_dim(value, which * size, size, axis=axis)


def stack(mine, value, other):
    low = mine == 0
    return jnp.stack([jnp.where(low, value, other), jnp.where(low, other, value)])


def scatter_step(value, step):
    _, mine = step
    return half_of(value, 1 - mine).astype(LOW), half_of(value, mine)


def merge(value, other, step):
    return stack(step[1], value, other).reshape((-1,) + value.shape[1:])


def reduce_chain(value, steps):
    for step in steps:
        sent, kept = scatter_step(value, step)
        came = yield sent, step[0]
        value = kept + came.astype(FULL)
    return value


def gather_chain(value, steps):
    for step in steps:
        came = yield value, step[0]
        value = merge(value, came, step)
    return value


class Chains:
    def __init__(self):
        self.running, self.flying, self.results, self.fresh = {}, {}, {}, []

    def begin(self, name, chain, spans, sent=None):
        self.running[name] = (chain, list(spans))
        self.load(name, next(chain) if sent is None else sent)

    def load(self, name, sent):
        spans = self.running[name][1]
        self.flying[name] = [sent, None, spans.pop(0) if spans else 1]

    def slot(self, *extra, held=True):
        due, fresh = [], list(self.fresh)
        for name, flight in self.flying.items():
            if flight[1] is None:
                flight[1] = swap(*flight[0])
            flight[2] -= 1
            if flight[2] <= 0:
                due.append(name)
        done = [self.flying[name][1] for name in due] + list(extra)
        if held:
            done = tie(*done, *(self.results[name] for name in fresh))
            for name, value in zip(fresh, done[len(due) + len(extra) :]):
                self.results[name] = value
            self.fresh = []
        for name, value in zip(due, done):
            try:
                self.load(name, self.running[name][0].send(value))
            except StopIteration as end:
                self.results[name] = end.value
                self.fresh.append(name)
                del self.running[name], self.flying[name]
        return done[len(due) : len(due) + len(extra)]


def sum_rows_axis(value):
    count, bit = lax.axis_size(ROWS), 1
    while bit < count:
        value = value + lax.ppermute(value, ROWS, [(i, i ^ bit) for i in range(count)])
        bit *= 2
    return value


def trade(near, far):
    count = lax.axis_size(ROWS)
    pairs = [(i, i + 1) for i in range(1, count - 1, 2)]
    return (
        lax.ppermute(near, ROWS, [(i, i ^ 1) for i in range(count)]),
        lax.ppermute(far, ROWS, pairs + [(b, a) for a, b in pairs]),
    )


def call(kernel, outs, *args, scratch=(), left=(), limit=60):
    def place(at, arg):
        if at in left:
            return pl.BlockSpec(memory_space=pltpu.HBM)
        return pl.BlockSpec(memory_space=pltpu.SMEM if arg.dtype == jnp.int32 else pltpu.VMEM)

    return pl.pallas_call(
        kernel,
        out_shape=[jax.ShapeDtypeStruct(shape, kind) for shape, kind in outs],
        in_specs=[place(at, arg) for at, arg in enumerate(args)],
        out_specs=[pl.BlockSpec(memory_space=pltpu.VMEM)] * len(outs),
        scratch_shapes=list(scratch),
        compiler_params=pltpu.CompilerParams(vmem_limit_bytes=limit * MIB),
    )(*args)


def logistic(values):
    return 0.5 * jnp.tanh(0.5 * values) + 0.5


def slope(values):
    s = logistic(values)
    return s * (1.0 + values * (1.0 - s))


def shifted(values, by):
    return pltpu.roll(values, (-by) % values.shape[0], 0)


def spread(images, height, width, main, above, below):
    channels = main.shape[-1]
    main = main.reshape(images, height, width, channels)
    above = above.reshape(images, 1, width, channels)
    below = below.reshape(images, 1, width, channels)
    flat = (images * height * width, channels)
    return (
        jnp.concatenate([above, main[:, :-1]], axis=1).reshape(flat),
        main.reshape(flat),
        jnp.concatenate([main[:, 1:], below], axis=1).reshape(flat),
    )


def wide(mask, like):
    return jnp.concatenate([mask] * (like.shape[1] // mask.shape[1]), axis=1)


def edges_of(dims, place, value, near, far):
    images, height, width = dims
    value = value.reshape(images, height, width, -1)
    top = value[:, 0].reshape(images * width, -1)
    bottom = value[:, height - 1].reshape(images * width, -1)
    odd = place[0, 0] % 2 == 1
    near[...] = jnp.where(odd, top, bottom).astype(near.dtype)
    far[...] = jnp.where(odd, bottom, top).astype(far.dtype)


def first_forward(
    dims, place, map_size, gain, bias, gain_mid, bias_mid, features, weight,
    first, near, far, sums, params, params_mid, areas, mask, mask_other, mask_above, mask_below,
    sizes, few, left, right, few_sems, sems,
):
    images, height, width = dims
    lanes = mask.shape[1]
    parts = sems.shape[1]
    deep = left.shape[1] // parts
    small = [pltpu.make_async_copy(map_size, sizes, few_sems.at[0])]
    for k, source in enumerate((gain, bias, gain_mid, bias_mid)):
        small.append(pltpu.make_async_copy(source, few.at[k], few_sems.at[k + 1]))
    for copy in small:
        copy.start()

    def load(k):
        span = pl.ds(k * deep, deep)
        return (
            pltpu.make_async_copy(features.at[:, span], left.at[:, span], sems.at[0, k]),
            pltpu.make_async_copy(weight.at[span, :], right.at[span, :], sems.at[1, k]),
        )

    for k in range(parts):
        for copy in load(k):
            copy.start()
    for copy in small:
        copy.wait()

    def inside(start, count):
        spot = lax.broadcasted_iota(jnp.int32, (count * width, lanes), 0)
        row, column = start + spot // width, spot % width
        parts = []
        for n in range(images):
            size = sizes[0, n]
            here = (row >= 0) & (row < size) & (column < size)
            parts.append(jnp.where(here, 1.0, 0.0))
        return jnp.concatenate(parts, axis=0)

    start = place[0, 0] * height
    kept = inside(start, height)
    mask[...] = kept
    mask_other[...] = inside((place[0, 0] + 1 - 2 * (place[0, 0] % 2)) * height, height)
    mask_above[...] = inside(start - 1, 1)
    mask_below[...] = inside(start + height, 1)
    params[0:1], params[1:2] = few[0], few[1]
    params_mid[0:1], params_mid[1:2] = few[2], few[3]
    spot = lax.broadcasted_iota(jnp.int32, areas.shape, 0)
    area = jnp.zeros(areas.shape, FULL)
    for n in range(images):
        area = jnp.where(spot == n, (sizes[0, n] * sizes[0, n]).astype(FULL), area)
    areas[...] = area
    total = None
    for k in range(parts):
        for copy in load(k):
            copy.wait()
        span = pl.ds(k * deep, deep)
        part = jnp.dot(left[:, span], right[span, :], preferred_element_type=FULL)
        total = part if total is None else total + part
    first[...] = total
    masked = total * wide(kept, total)
    middle = total.shape[1]
    sums[:, 0, 0:middle] = spread_sum(sums, masked)
    sums[:, 1, 0:middle] = spread_sum(sums, masked * total)
    sums[:, 0, middle:] = spread_sum(sums, kept)
    lane = lax.broadcasted_iota(jnp.int32, (1, lanes), 1)
    told = jnp.zeros((1, lanes), FULL)
    for n in range(images):
        told = jnp.where(lane == n, sizes[0, n].astype(FULL), told)
    sums[:, 1, middle:] = jnp.broadcast_to(told, (sums.shape[0], lanes))
    edges_of(dims, place, total, near, far)


def spread_sum(copies, values):
    total = jnp.sum(values, axis=0, keepdims=True)
    return jnp.broadcast_to(total, (copies.shape[0], total.shape[1]))


def fetch(weight, held, sems):
    def load(i, j):
        return pltpu.make_async_copy(weight.at[i, j], held.at[i, j], sems.at[i, j])

    for j in range(3):
        for i in range(3):
            load(i, j).start()

    def tap(i, j):
        load(i, j).wait()
        return held[i, j]

    return tap


def put_sums(dims, place, at, values, others, sent, kept):
    chunk, half = values.shape[1], sent.shape[1]
    span = pl.ds(at % half, chunk)
    mine = (place[0, 0] % 2 == 1) == (at >= half)
    for k, value in enumerate((values, others)):
        total = jnp.sum(value, axis=0, keepdims=True)
        kept[k : k + 1, span] = jnp.where(mine, total, kept[k : k + 1, span])
        sent[k : k + 1, span] = jnp.where(mine, sent[k : k + 1, span], total)


def take_sums(place, at, chunk, mine, other):
    half = mine.shape[2]
    span = pl.ds(at % half, chunk)
    here = (place[0, 0] % 2 == 1) == (at >= half)
    return jnp.where(here, jnp.sum(mine[:, :, span], axis=0), jnp.sum(other[:, :, span], axis=0))


def affine(sums, count, gain, bias):
    average = sums[0:1] / count
    inv_std = lax.rsqrt(sums[1:2] / count - average * average + EPSILON)
    scale = inv_std * gain
    return average, inv_std, scale, bias - average * scale


def mid_forward(
    dims, place, came, params, first, near, far, mask, mask_above, mask_below, weight,
    split, second, sums, sums_first, sizes, held, sems,
):
    tap = fetch(weight, held, sems)
    middle = first.shape[1]
    totals = jnp.sum(came[...], axis=0)
    sums_first[...] = totals
    for y in range(2):
        sizes[y : y + 1] = came[place[0, 1] + y * place[0, 2], 1:2, middle:]
    count = totals[0:1, middle : middle + 1]
    _, _, scale, shift = affine(totals[:, 0:middle], count, params[0:1], params[1:2])

    def act(hidden, inside):
        pre = hidden * scale + shift
        return pre * logistic(pre) * wide(inside[...], pre)

    odd = place[0, 0] % 2 == 1
    centre = act(first[...], mask)
    above = act(jnp.where(odd, near[...], far[...]), mask_above)
    below = act(jnp.where(odd, far[...], near[...]), mask_below)
    three = spread(*dims, centre, above, below)
    x3 = [part.astype(LOW) for part in three]
    flat_rows(dims, centre, split)
    total = None
    for j in range(3):
        part = None
        for i in range(3):
            term = jnp.dot(x3[i], tap(i, j), preferred_element_type=FULL)
            part = term if part is None else part + term
        part = shifted(part, j - 1) if j != 1 else part
        total = part if total is None else total + part
    second[...] = total
    masked = total * wide(mask[...], total)
    sums[:, 0] = spread_sum(sums, masked)
    sums[:, 1] = spread_sum(sums, masked * total)


def flat_rows(dims, value, out):
    images, height, width = dims
    value = value.reshape(images, height, width, -1)
    for r in range(height):
        out[r] = value[:, r].reshape(images * width, -1).astype(LOW)


def flat_halves(dims, place, value, sent, kept):
    quarter = value.shape[1] // 4
    odd, high = place[0, 0] % 2 == 1, place[0, 3] == 1
    parts = [value[:, k * quarter : (k + 1) * quarter] for k in range(4)]
    parts[1], parts[2] = jnp.where(odd, parts[2], parts[1]), jnp.where(odd, parts[1], parts[2])
    one, two = jnp.concatenate(parts[:2], axis=1), jnp.concatenate(parts[2:], axis=1)
    flat_rows(dims, jnp.where(high, one, two), sent)
    flat_rows(dims, jnp.where(high, two, one), kept)


def out_forward(
    dims, place, sums_first, came, params_mid, second, mask, weight,
    act, normed_sent, normed_kept, third, sums_sent, sums_kept, sums_second,
):
    middle = second.shape[1]
    totals = jnp.sum(came[...], axis=0)
    sums_second[...] = totals
    count = sums_first[0:1, middle : middle + 1]
    average, inv_std, scale, shift = affine(totals, count, params_mid[0:1], params_mid[1:2])
    hidden = second[...]
    pre = hidden * scale + shift
    inside = wide(mask[...], hidden)
    act[...] = (pre * logistic(pre) * inside).astype(LOW)
    flat_halves(dims, place, (hidden - average) * inv_std, normed_sent, normed_kept)
    for at in range(0, third.shape[1], middle):
        span = pl.ds(at, middle)
        total = jnp.dot(act[...], weight[:, span], preferred_element_type=FULL)
        third[:, span] = total
        masked = total * inside
        put_sums(dims, place, at, masked, masked * total, sums_sent, sums_kept)


def out_result(
    dims, place, sums_first, came, other, params_out, third, features, out_grad, pool_grad, areas, mask,
    result, pooled, grad, sums_sent, sums_kept, sums_third,
):
    images, height, width = dims
    chunk = sums_first.shape[1] - mask.shape[1]
    count = sums_first[0:1, chunk : chunk + 1]
    inside = jnp.concatenate([mask[...]] * (chunk // mask.shape[1]), axis=1)
    area = jnp.concatenate([areas[...]] * (chunk // mask.shape[1]), axis=1)
    for at in range(0, third.shape[1], chunk):
        span = pl.ds(at, chunk)
        totals = take_sums(place, at, chunk, came, other)
        sums_third[:, span] = totals
        average, inv_std, _, _ = affine(totals, count, 1.0, 0.0)
        normed = (third[:, span] - average) * inv_std
        summed = params_out[0:1, span] * normed + params_out[1:2, span] + features[:, span].astype(FULL)
        gate = logistic(summed)
        value = summed * gate * inside
        result[:, span] = value.astype(LOW)
        pooled[:, span] = jnp.sum(value.reshape(images, height * width, chunk), axis=1)
        share = (pool_grad[:, span] / area)[:, None]
        total = out_grad[:, span].astype(FULL).reshape(images, height * width, chunk) + share
        total = total.reshape(inside.shape) * inside * (gate * (1.0 + summed * (1.0 - gate)))
        grad[:, span] = total
        put_sums(dims, place, at, total, total * normed, sums_sent, sums_kept)


def out_backward(
    dims, place, sums_first, sums_second, sums_third, came, other, params_mid, params_out, third, grad, second,
    mask, weight, third_sent, third_kept, pre_grad, rows_sent, rows_kept, near, far, sums, sums_out, lows,
):
    chunk = second.shape[1]
    count = sums_first[0:1, chunk : chunk + 1]
    inside = wide(mask[...], second)
    back = None
    for at in range(0, third.shape[1], chunk):
        span = pl.ds(at, chunk)
        average, inv_std, scale, _ = affine(sums_third[:, span], count, params_out[0:1, span], 0.0)
        normed = (third[:, span] - average) * inv_std
        totals = take_sums(place, at, chunk, came, other)
        sums_out[:, span] = totals
        mean = (totals[0:1] + normed * totals[1:2]) / count
        low = (inside * scale * (grad[:, span] - mean)).astype(LOW)
        lows[:, span] = low
        part = lax.dot_general(
            low, weight[:, span], (((1,), (1,)), ((), ())), preferred_element_type=FULL
        )
        back = part if back is None else back + part
    average, inv_std, scale, shift = affine(sums_second[...], count, params_mid[0:1], params_mid[1:2])
    hidden = second[...]
    back = back * inside * slope(hidden * scale + shift)
    pre_grad[...] = back
    flat_halves(dims, place, back, rows_sent, rows_kept)
    odd, half = place[0, 0] % 2 == 1, third.shape[1] // 2
    one, two = lows[:, 0:half], lows[:, half:]
    third_sent[...] = jnp.where(odd, one, two)
    third_kept[...] = jnp.where(odd, two, one)
    sums[:, 0] = spread_sum(sums, back)
    normed = (hidden - average) * inv_std
    sums[:, 1] = spread_sum(sums, back * normed)
    edges_of(dims, place, jnp.concatenate([back, normed], axis=1), near, far)


def mid_weights(
    place, sizes, sums_first, sums_second, sums_grad, params_mid,
    acts_mine, acts_came, normed_mine, normed_came, grads_mine, grads_came, sent, kept, left, right,
):
    groups, _, size, channels = kept.shape
    pixels = acts_mine.shape[2]
    images = sizes.shape[1]
    width = pixels // images
    swapped, high = place[0, 0] == 1, place[0, 3] == 1
    middle = sums_grad.shape[1]
    count = sums_first[0:1, middle : middle + 1]
    span = pl.ds(pl.multiple_of(place[0, 1] * channels, channels), channels)
    average = sums_second[0:1, span] / count
    inv_std = lax.rsqrt(sums_second[1:2, span] / count - average * average + EPSILON)
    scale = inv_std * params_mid[0:1, span]
    mean_grad, mean_gain = sums_grad[0:1, span] / count, sums_grad[1:2, span] / count
    column = lax.broadcasted_iota(jnp.int32, (width, channels), 0)
    for y in range(2):
        for x in range(2):
            for c in range(2):
                spot = jnp.where(swapped, 2 * y + c, 2 * x + c)
                here = jnp.where(swapped, x, y) == place[0, 2]
                four = 2 * x + y if c else 2 * y + x
                own = place[0, 0] == c
                rows = pl.ds(((2 * y + x) * 2 + c) * pixels, pixels)
                for r in range(2):
                    left[r, rows, :] = jnp.where(here, acts_mine[spot, r], acts_came[spot, r])
                    row = (2 * x + c) * 2 + r
                    inside = []
                    for n in range(images):
                        extent = jnp.where(row < sizes[y, n], sizes[y, n], 0)
                        inside.append(jnp.where(column < extent, 1.0, 0.0))
                    value = jnp.where(own, grads_mine[four, r], grads_came[four, r]).astype(FULL)
                    normed = jnp.where(own, normed_mine[four, r], normed_came[four, r])
                    value = value - (mean_grad + normed.astype(FULL) * mean_gain)
                    value = value * scale * jnp.concatenate(inside, axis=0)
                    right[r, rows, 0:channels] = value.astype(LOW)
    for r in range(2):
        grad = right[r, :, 0:channels].astype(FULL)
        right[r, :, channels : 2 * channels] = shifted(grad, 1).astype(LOW)
        right[r, :, 2 * channels :] = shifted(grad, -1).astype(LOW)
    span, image = 3 * pixels, 4 * pixels

    def product(r_left, at_left, r_right, at_right, count):
        return lax.dot_general(
            left[r_left, pl.ds(at_left, count), :],
            right[r_right, pl.ds(at_right, count), :],
            (((0,), (0,)), ((), ())),
            preferred_element_type=FULL,
        )

    def crossed(r_left, r_right, skip_left, skip_right):
        part = product(r_left, 0, r_right, 0, 2 * image)
        for y in range(2):
            part = part + product(
                r_right, y * image + skip_left, r_left, y * image + skip_right, span
            )
        return part

    taps = (
        crossed(0, 1, 0, pixels),
        product(0, 0, 0, 0, 2 * image) + product(1, 0, 1, 0, 2 * image),
        crossed(1, 0, pixels, 0),
    )
    for i in range(3):
        for j, place in ((1, 0), (0, 1), (2, 2)):
            part = taps[i][:, place * channels : (place + 1) * channels]
            one = part[0 : groups * size].reshape(groups, size, channels)
            two = part[groups * size :].reshape(groups, size, channels)
            sent[:, 3 * i + j] = jnp.where(high, one, two).astype(LOW)
            kept[:, 3 * i + j] = jnp.where(high, two, one)


def mid_assemble(odd, mine, other, total):
    quarters, groups, _, size, lanes = mine.shape
    half = groups * size
    swapped = odd[0, 0] == 1
    for q, turned in enumerate((0, 2, 1, 3)):
        span = pl.ds(q * lanes, lanes)
        even = jnp.where(swapped, other[q, :, 0], mine[q, :, 0])
        total[0, 0:half, span] = even.astype(FULL).reshape(half, lanes)
        uneven = jnp.where(swapped, mine[turned, :, 0], other[turned, :, 0])
        total[0, half:, span] = uneven.astype(FULL).reshape(half, lanes)


def mid_backward(
    dims, place, sums_first, sums_second, came, params, params_mid, grad, near, far,
    second, first, mask, mask_above, mask_below, weight, pre_grad, low_grad, sums, sums_mid, held, sems,
):
    tap = fetch(weight, held, sems)
    middle = first.shape[1]
    count = sums_first[0:1, middle : middle + 1]
    totals = jnp.sum(came[...], axis=0)
    sums_mid[...] = totals
    average, inv_std, scale, shift = affine(sums_second[...], count, params_mid[0:1], params_mid[1:2])
    mean_grad, mean_gain = totals[0:1] / count, totals[1:2] / count

    def normed_grad(value, normed, inside):
        return wide(inside[...], value) * scale * (value - (mean_grad + normed * mean_gain))

    odd = place[0, 0] % 2 == 1

    def beside(one, other, inside):
        value = jnp.where(odd, one[...], other[...]).astype(FULL)
        return normed_grad(value[:, 0:middle], value[:, middle:], inside)

    centre = normed_grad(grad[...], (second[...] - average) * inv_std, mask)
    above = beside(near, far, mask_above)
    below = beside(far, near, mask_below)
    three = spread(*dims, centre, above, below)
    average, inv_std, scale, shift = affine(sums_first[:, 0:middle], count, params[0:1], params[1:2])
    low = [part.astype(LOW) for part in three]
    total = None
    for j in range(3):
        part = None
        for i in range(3):
            term = lax.dot_general(
                low[2 - i], tap(i, j), (((1,), (1,)), ((), ())), preferred_element_type=FULL
            )
            part = term if part is None else part + term
        part = shifted(part, 1 - j) if j != 1 else part
        total = part if total is None else total + part
    hidden = first[...]
    total = total * wide(mask[...], total) * slope(hidden * scale + shift)
    pre_grad[...] = total
    low_grad[...] = total.astype(LOW)
    sums[:, 0] = spread_sum(sums, total)
    sums[:, 1] = spread_sum(sums, total * ((hidden - average) * inv_std))


def contract_in(left, right):
    return lax.dot_general(left, right, (((0,), (0,)), ((), ())), preferred_element_type=FULL)


def put_halves(place, total, sent, kept):
    half = total.shape[0] // 2
    high = place[0, 3] == 1
    one, two = total[0:half], total[half:]
    sent[...] = jnp.where(high, one, two).astype(LOW)
    kept[...] = jnp.where(high, two, one)


def first_backward(
    place, sums_first, came, params, first, grad, mask, first_other, grad_other, mask_other, features,
    low, sums_in, sent, kept, both,
):
    pixels, middle = first.shape
    count = sums_first[0:1, middle : middle + 1]
    totals = jnp.sum(came[...], axis=0)
    sums_in[...] = totals
    average, inv_std, scale, _ = affine(sums_first[:, 0:middle], count, params[0:1], 0.0)
    pairs = ((first, grad, mask), (first_other, grad_other, mask_other))
    for k, (hidden, source, inside) in enumerate(pairs):
        normed = (hidden[...] - average) * inv_std
        value = source[...].astype(FULL) - (totals[0:1] + normed * totals[1:2]) / count
        both[k * pixels : (k + 1) * pixels] = (wide(inside[...], value) * scale * value).astype(LOW)
    low[...] = both[0:pixels]
    put_halves(place, contract_in(features[...], both[...]), sent, kept)


def out_weights(place, act, act_other, third, third_other, sent, kept):
    total = contract_in(act[...], third[...]) + contract_in(act_other[...], third_other[...])
    put_halves(place, total, sent, kept)


def assemble(odd, mine, other, shape):
    groups, taps, size, lanes = shape
    quarters = mine.shape[0] // (groups * taps * size)
    channels = quarters * lanes
    pieces = pl.BlockSpec((quarters, groups, 1, size, lanes), lambda t: (0, 0, t, 0, 0))
    return pl.pallas_call(
        mid_assemble,
        grid=(taps,),
        out_shape=jax.ShapeDtypeStruct((taps, channels, channels), FULL),
        in_specs=[pl.BlockSpec(memory_space=pltpu.SMEM), pieces, pieces],
        out_specs=pl.BlockSpec((1, channels, channels), lambda t: (t, 0, 0)),
        compiler_params=pltpu.CompilerParams(vmem_limit_bytes=48 * MIB),
    )(
        odd,
        mine.reshape(quarters, groups, taps, size, lanes),
        other.reshape(quarters, groups, taps, size, lanes),
    )


def halves(value, step):
    _, mine = step
    return half_of(value, 1 - mine, 3), half_of(value, mine, 3)


def contract(left, right):
    return lax.dot_general(left, right, (((0,), (0,)), ((), ())), preferred_element_type=FULL)


def times_transpose(left, weights):
    return lax.dot_general(left, weights, (((1,), (1,)), ((), ())), preferred_element_type=FULL)


def per_device(
    features,
    weight_in,
    gain_in,
    bias_in,
    weight_mid,
    gain_mid,
    bias_mid,
    weight_out,
    gain_out,
    bias_out,
    map_size,
    out_grad,
    pool_grad,
):
    images, height, width, channels = features.shape
    middle = weight_mid.shape[3]
    dims = (images, height, width)
    pixels = images * height * width

    count = lax.axis_size(AXES)
    place = lax.axis_index(ROWS).astype(jnp.int32)
    index = flat_index()
    rows_count = lax.axis_size(ROWS)
    base = index - lax.axis_index("img") % 2 * rows_count

    count = lax.axis_size(AXES)
    flat_features = features.reshape(pixels, channels)
    params_out = jnp.stack([gain_out, bias_out])
    steps = plan()
    core, mine, far_steps = steps[0], steps[0][1], steps[3:]
    place = jnp.stack([place, base, jnp.int32(rows_count), steps[1][1]]).astype(jnp.int32)[None]
    plane, narrow, broad, large = (pixels, middle), (2, middle), (2, channels), (pixels, channels)
    edge, split_rows = (images * width, middle), (height, images * width, middle)
    half_broad = (2, channels // 2)
    half_rows = (height, images * width, middle // 2)
    taps = [pltpu.VMEM(weight_mid.shape, LOW), pltpu.SemaphoreType.DMA((3, 3))]

    first, near, far, sums, params, params_mid, areas, mask, mask_other, mask_above, mask_below = call(
        lambda *refs: first_forward(dims, *refs),
        [
            (plane, FULL),
            (edge, FULL),
            (edge, FULL),
            ((count, 2, middle + LANES), FULL),
            (narrow, FULL),
            (narrow, FULL),
            ((images, LANES), FULL),
            ((pixels, LANES), FULL),
            ((pixels, LANES), FULL),
            ((images * width, LANES), FULL),
            ((images * width, LANES), FULL),
        ],
        place,
        map_size[None],
        gain_in[None],
        bias_in[None],
        gain_mid[None],
        bias_mid[None],
        flat_features,
        weight_in,
        scratch=[
            pltpu.SMEM((1, images), jnp.int32),
            pltpu.VMEM((4, 1, middle), FULL),
            pltpu.VMEM((pixels, channels), LOW),
            pltpu.VMEM((channels, middle), LOW),
            pltpu.SemaphoreType.DMA((5,)),
            pltpu.SemaphoreType.DMA((2, 4)),
        ],
        left=(1, 2, 3, 4, 5, 6, 7),
        limit=60,
    )
    near, far = trade(near, far)
    came, near, far = tie(everyone(sums), near, far)
    split, second, sums, sums_first, sizes = call(
        lambda *refs: mid_forward(dims, *refs),
        [
            (split_rows, LOW),
            (plane, FULL),
            ((count, 2, middle), FULL),
            ((2, middle + LANES), FULL),
            ((2, LANES), FULL),
        ],
        place,
        came,
        params,
        first,
        near,
        far,
        mask,
        mask_above,
        mask_below,
        weight_mid,
        scratch=taps,
        left=(9,),
    )
    acts = swap(half_of(split, 1 - mine, 2), core[0])
    came, acts, first_other = tie(everyone(sums), acts, swap(first, core[0]))
    second_act, normed_sent, normed_kept, third, sums_sent, sums_kept, sums_second = call(
        lambda *refs: out_forward(dims, *refs),
        [
            (plane, LOW),
            (half_rows, LOW),
            (half_rows, LOW),
            (large, FULL),
            (half_broad, FULL),
            (half_broad, FULL),
            (narrow, FULL),
        ],
        place,
        sums_first,
        came,
        params_mid,
        second,
        mask,
        weight_out,
    )
    acts = stack(mine, half_of(split, mine, 2), acts)
    features_came = swap(half_of(flat_features, 1 - mine, 1), core[0])
    came, came_other, acts_came, normed_came, act_other, features_came = tie(
        *everyone_wide(sums_sent, sums_kept, core),
        swap(acts, steps[1][0]),
        swap(normed_sent[None], steps[1][0]),
        swap(second_act, core[0]),
        features_came,
    )
    result, pooled, grad_summed, sums_sent, sums_kept, sums_third = call(
        lambda *refs: out_result(dims, *refs),
        [
            (large, LOW),
            ((images, channels), FULL),
            (large, FULL),
            (half_broad, FULL),
            (half_broad, FULL),
            (broad, FULL),
        ],
        place,
        sums_first,
        came,
        came_other,
        params_out,
        third,
        flat_features,
        out_grad.reshape(pixels, channels),
        pool_grad,
        areas,
        mask,
    )

    acts = merge(acts, acts_came, steps[1])
    normed_sent, normed_kept = halves(merge(normed_kept[None], normed_came, steps[1]), steps[2])
    sums_sent, acts, normed_sent = tie(sums_sent, acts, normed_sent)
    features_pair = jnp.concatenate([half_of(flat_features, mine, 1), features_came])
    came, came_other, acts_came, features_pair = tie(
        *everyone_wide(sums_sent, sums_kept, core),
        swap(acts, steps[2][0]),
        features_pair,
    )
    normed_came = swap(normed_sent, steps[2][0])
    third_sent, third_kept, grad_second_pre, grads_sent, grads_kept, near, far, sums, sums_out = call(
        lambda *refs: out_backward(dims, *refs),
        [
            ((pixels, channels // 2), LOW),
            ((pixels, channels // 2), LOW),
            (plane, FULL),
            (half_rows, LOW),
            (half_rows, LOW),
            ((edge[0], 2 * middle), LOW),
            ((edge[0], 2 * middle), LOW),
            ((count, 2, middle), FULL),
            (broad, FULL),
        ],
        place,
        sums_first,
        sums_second,
        sums_third,
        came,
        came_other,
        params_mid,
        params_out,
        third,
        grad_summed,
        second,
        mask,
        weight_out,
        scratch=[pltpu.VMEM(large, LOW)],
    )

    near, far = trade(near, far)
    sums = everyone(sums)
    came = swap(grads_sent[None], steps[1][0])
    sent, kept = halves(merge(grads_kept[None], came, steps[1]), steps[2])
    came = swap(sent, steps[2][0])
    third_came = swap(third_sent, core[0])
    out_sent, out_kept = call(
        out_weights,
        [((middle // 2, channels // 2), LOW), ((middle // 2, channels // 2), FULL)],
        place,
        second_act,
        act_other,
        third_kept,
        third_came,
    )
    sums, came, out_sent, near, far = tie(sums, came, out_sent, near, far)
    grads = merge(kept, came, steps[2])
    grad_first_pre, low_grad, sums, sums_mid = call(
        lambda *refs: mid_backward(dims, *refs),
        [(plane, FULL), (plane, LOW), ((count, 2, middle), FULL), (narrow, FULL)],
        place,
        sums_first,
        sums_second,
        sums,
        params,
        params_mid,
        grad_second_pre,
        near,
        far,
        second,
        first,
        mask,
        mask_above,
        mask_below,
        weight_mid,
        scratch=taps,
        left=(14,),
    )
    sums, normed_came = tie(sums, normed_came)
    normed = merge(normed_kept, normed_came, steps[2])
    sums = everyone(sums)
    grad_other = swap(low_grad, core[0])
    grads_came, normed_came = swap(grads, core[0]), swap(normed, core[0])

    odd = (index % 2).astype(jnp.int32).reshape(1, 1)

    def out_chain():
        came = yield out_sent, steps[1][0]
        value = out_kept + came.astype(FULL)
        value = yield from reduce_chain(value, steps[2:])
        value = yield from gather_chain(value.astype(LOW), steps[:0:-1])
        other = yield value, core[0]
        low = mine == 0
        parts = [jnp.where(low, value, other), jnp.where(low, other, value)]
        return jnp.concatenate(parts, axis=1).astype(FULL)

    def mid_chain():
        high, low = steps[1][1], steps[2][1]
        chunk = jnp.where(index % 2 == 0, 2 * high + low, 2 * low + high)
        lanes, deep = grads.shape[-1], acts.shape[-1]
        span = 2 * acts.shape[0] * images * width
        shape = (deep // GROUP // 2, 9, GROUP, lanes)
        sent, kept = call(
            mid_weights,
            [(shape, LOW), (shape, FULL)],
            jnp.stack([index % 2, chunk, steps[2][1], far_steps[0][1]]).astype(jnp.int32)[None],
            sizes[:, :images].astype(jnp.int32),
            sums_first,
            sums_second,
            sums_mid,
            params_mid,
            acts,
            acts_came,
            normed,
            normed_came,
            grads,
            grads_came,
            scratch=[pltpu.VMEM((2, span, deep), LOW), pltpu.VMEM((2, span, 3 * lanes), LOW)],
        )
        came = yield sent.reshape(-1, lanes), far_steps[0][0]
        value = kept.reshape(-1, lanes) + came.astype(FULL)
        value = yield from reduce_chain(value, far_steps[1:])
        value = yield from gather_chain(value.astype(LOW), steps[:0:-1])
        other = yield value, core[0]
        return assemble(odd, value, other, (2 * shape[0], *shape[1:]))

    def in_chain():
        came = yield in_sent, steps[1][0]
        value = in_kept + came.astype(FULL)
        value = yield from reduce_chain(value, steps[2:])
        value = yield from gather_chain(value.astype(LOW), steps[:0:-1])
        other = yield value, core[0]
        return stack(mine, value, other).reshape(-1, middle).astype(FULL)

    chains = Chains()
    mid = mid_chain()
    mid_sent, flips = next(mid)
    came, mid_sent, grad_other, out_sent = tie(sums, mid_sent, grad_other, out_sent)
    chains.begin("out", out_chain(), ())
    chains.begin("mid", mid, (), (mid_sent, flips))
    grad_first, sums_in, in_sent, in_kept = call(
        first_backward,
        [
            (plane, LOW),
            (narrow, FULL),
            ((channels // 4, middle), LOW),
            ((channels // 4, middle), FULL),
        ],
        place,
        sums_first,
        came,
        params,
        first,
        grad_first_pre,
        mask,
        first_other,
        grad_other,
        mask_other,
        features_pair,
        scratch=[pltpu.VMEM((2 * pixels, middle), LOW)],
    )
    chains.slot(held=False)
    chains.begin("in", in_chain(), ())
    grad_features = grad_summed + times_transpose(grad_first, weight_in)
    (grad_features,) = chains.slot(grad_features)
    chains.slot()
    (pooled,) = chains.slot(pooled)
    (pooled,) = chains.slot(sum_rows_axis(pooled))
    pooled = pooled / areas[:, :1]
    for _ in range(0):
        chains.slot()
    while chains.running:
        chains.slot(held=False)
    grad_weight_in, grad_weight_mid, grad_weight_out = (
        chains.results[name] for name in ("in", "mid", "out")
    )
    whole = (images, height, width, channels)
    return (
        result.astype(LOW).reshape(whole),
        pooled,
        grad_features.reshape(whole),
        grad_weight_in,
        sums_in[1],
        sums_in[0],
        grad_weight_mid.reshape(weight_mid.shape),
        sums_mid[1],
        sums_mid[0],
        grad_weight_out,
        sums_out[1],
        sums_out[0],
    )


def solution(mesh):
    images, rows = mesh.devices.shape
    mesh = Mesh(mesh.devices.reshape(images, rows // 2, 2), AXES)
    tiles, single = P("img", ROWS, None, None), P()
    return jax.shard_map(
        per_device,
        mesh=mesh,
        in_specs=(tiles,) + (single,) * 9 + (P("img"), tiles, P("img", None)),
        out_specs=(tiles, P("img", None), tiles) + (single,) * 9,
        check_vma=False,
    )
```

```python
import jax
import jax.numpy as jnp
from jax import lax
from jax.experimental import pallas as pl
from jax.experimental.pallas import tpu as pltpu
from jax.sharding import Mesh
from jax.sharding import PartitionSpec as P

EPSILON = 1e-05
ROWS = ("half", "low")
AXES = ("img", *ROWS)
MIB = 1 << 20
LOW = jnp.bfloat16
FULL = jnp.float32
GROUP = 16
LANES = 128


def swap(value, flips):
    count = lax.axis_size(AXES)
    return lax.ppermute(value, AXES, [(i, i ^ flips[i & 1]) for i in range(count)])


def bits():
    count, found = lax.axis_size(AXES), []
    while (1 << len(found)) < count:
        found.append(1 << len(found))
    return found


def everyone(copies):
    return lax.all_to_all(copies, AXES, 0, 0)


def everyone_wide(sent, kept, low_step):
    value = kept + swap(sent, low_step[0])
    count = lax.axis_size(AXES[:2])
    mine = lax.all_to_all(jnp.broadcast_to(value[None], (count, *value.shape)), AXES[:2], 0, 0)
    return mine, swap(mine, low_step[0])


def tie(*values):
    return lax.optimization_barrier(values)


def flat_index():
    return lax.axis_index("img") * lax.axis_size(ROWS) + lax.axis_index(ROWS)


def plan():
    order = bits()
    steps = [(bit, bit) for bit in order]
    if len(order) >= 3:
        steps[1], steps[2] = (order[1], order[2]), (order[2], order[1])
    index = flat_index()
    low = index % 2
    chosen = []
    for even, odd in steps:
        chosen.append(((even, odd), jnp.where(low == 0, index // even % 2, index // odd % 2)))
    return chosen


def half_of(value, which, axis=0):
    size = value.shape[axis] // 2
    return lax.dynamic_slice_in_dim(value, which * size, size, axis=axis)


def stack(mine, value, other):
    low = mine == 0
    return jnp.stack([jnp.where(low, value, other), jnp.where(low, other, value)])


def scatter_step(value, step):
    _, mine = step
    return half_of(value, 1 - mine).astype(LOW), half_of(value, mine)


def merge(value, other, step):
    return stack(step[1], value, other).reshape((-1,) + value.shape[1:])


def reduce_chain(value, steps):
    for step in steps:
        sent, kept = scatter_step(value, step)
        came = yield sent, step[0]
        value = kept + came.astype(FULL)
    return value


def gather_chain(value, steps):
    for step in steps:
        came = yield value, step[0]
        value = merge(value, came, step)
    return value


class Chains:
    def __init__(self):
        self.running, self.flying, self.results, self.fresh = {}, {}, {}, []

    def begin(self, name, chain, spans, sent=None):
        self.running[name] = (chain, list(spans))
        self.load(name, next(chain) if sent is None else sent)

    def load(self, name, sent):
        spans = self.running[name][1]
        self.flying[name] = [sent, None, spans.pop(0) if spans else 1]

    def slot(self, *extra, held=True):
        due, fresh = [], list(self.fresh)
        for name, flight in self.flying.items():
            if flight[1] is None:
                flight[1] = swap(*flight[0])
            flight[2] -= 1
            if flight[2] <= 0:
                due.append(name)
        done = [self.flying[name][1] for name in due] + list(extra)
        if held:
            done = tie(*done, *(self.results[name] for name in fresh))
            for name, value in zip(fresh, done[len(due) + len(extra) :]):
                self.results[name] = value
            self.fresh = []
        for name, value in zip(due, done):
            try:
                self.load(name, self.running[name][0].send(value))
            except StopIteration as end:
                self.results[name] = end.value
                self.fresh.append(name)
                del self.running[name], self.flying[name]
        return done[len(due) : len(due) + len(extra)]


def sum_rows_axis(value):
    count, bit = lax.axis_size(ROWS), 1
    while bit < count:
        value = value + lax.ppermute(value, ROWS, [(i, i ^ bit) for i in range(count)])
        bit *= 2
    return value


def trade(near, far):
    count = lax.axis_size(ROWS)
    pairs = [(i, i + 1) for i in range(1, count - 1, 2)]
    return (
        lax.ppermute(near, ROWS, [(i, i ^ 1) for i in range(count)]),
        lax.ppermute(far, ROWS, pairs + [(b, a) for a, b in pairs]),
    )


def call(kernel, outs, *args, scratch=(), left=(), limit=60):
    def place(at, arg):
        if at in left:
            return pl.BlockSpec(memory_space=pltpu.HBM)
        return pl.BlockSpec(memory_space=pltpu.SMEM if arg.dtype == jnp.int32 else pltpu.VMEM)

    return pl.pallas_call(
        kernel,
        out_shape=[jax.ShapeDtypeStruct(shape, kind) for shape, kind in outs],
        in_specs=[place(at, arg) for at, arg in enumerate(args)],
        out_specs=[pl.BlockSpec(memory_space=pltpu.VMEM)] * len(outs),
        scratch_shapes=list(scratch),
        compiler_params=pltpu.CompilerParams(vmem_limit_bytes=limit * MIB),
    )(*args)


def logistic(values):
    return 0.5 * jnp.tanh(0.5 * values) + 0.5


def slope(values):
    s = logistic(values)
    return s * (1.0 + values * (1.0 - s))


def shifted(values, by):
    return pltpu.roll(values, (-by) % values.shape[0], 0)


def spread(images, height, width, main, above, below):
    channels = main.shape[-1]
    main = main.reshape(images, height, width, channels)
    above = above.reshape(images, 1, width, channels)
    below = below.reshape(images, 1, width, channels)
    flat = (images * height * width, channels)
    return (
        jnp.concatenate([above, main[:, :-1]], axis=1).reshape(flat),
        main.reshape(flat),
        jnp.concatenate([main[:, 1:], below], axis=1).reshape(flat),
    )


def wide(mask, like):
    return jnp.concatenate([mask] * (like.shape[1] // mask.shape[1]), axis=1)


def edges_of(dims, place, value, near, far):
    images, height, width = dims
    value = value.reshape(images, height, width, -1)
    top = value[:, 0].reshape(images * width, -1)
    bottom = value[:, height - 1].reshape(images * width, -1)
    odd = place[0, 0] % 2 == 1
    near[...] = jnp.where(odd, top, bottom).astype(near.dtype)
    far[...] = jnp.where(odd, bottom, top).astype(far.dtype)


def first_forward(
    dims, place, map_size, gain, bias, gain_mid, bias_mid, features, weight,
    first, near, far, sums, params, params_mid, areas, mask, mask_other, mask_above, mask_below,
    sizes, few, left, right, few_sems, sems,
):
    images, height, width = dims
    lanes = mask.shape[1]
    parts = sems.shape[1]
    deep = left.shape[1] // parts
    small = [pltpu.make_async_copy(map_size, sizes, few_sems.at[0])]
    for k, source in enumerate((gain, bias, gain_mid, bias_mid)):
        small.append(pltpu.make_async_copy(source, few.at[k], few_sems.at[k + 1]))
    for copy in small:
        copy.start()

    def load(k):
        span = pl.ds(k * deep, deep)
        return (
            pltpu.make_async_copy(features.at[:, span], left.at[:, span], sems.at[0, k]),
            pltpu.make_async_copy(weight.at[span, :], right.at[span, :], sems.at[1, k]),
        )

    for k in range(parts):
        for copy in load(k):
            copy.start()
    for copy in small:
        copy.wait()

    def inside(start, count):
        spot = lax.broadcasted_iota(jnp.int32, (count * width, lanes), 0)
        row, column = start + spot // width, spot % width
        parts = []
        for n in range(images):
            size = sizes[0, n]
            here = (row >= 0) & (row < size) & (column < size)
            parts.append(jnp.where(here, 1.0, 0.0))
        return jnp.concatenate(parts, axis=0)

    start = place[0, 0] * height
    kept = inside(start, height)
    mask[...] = kept
    mask_other[...] = inside((place[0, 0] + 1 - 2 * (place[0, 0] % 2)) * height, height)
    mask_above[...] = inside(start - 1, 1)
    mask_below[...] = inside(start + height, 1)
    params[0:1], params[1:2] = few[0], few[1]
    params_mid[0:1], params_mid[1:2] = few[2], few[3]
    spot = lax.broadcasted_iota(jnp.int32, areas.shape, 0)
    area = jnp.zeros(areas.shape, FULL)
    for n in range(images):
        area = jnp.where(spot == n, (sizes[0, n] * sizes[0, n]).astype(FULL), area)
    areas[...] = area
    total = None
    for k in range(parts):
        for copy in load(k):
            copy.wait()
        span = pl.ds(k * deep, deep)
        part = jnp.dot(left[:, span], right[span, :], preferred_element_type=FULL)
        total = part if total is None else total + part
    first[...] = total
    masked = total * wide(kept, total)
    middle = total.shape[1]
    sums[:, 0, 0:middle] = spread_sum(sums, masked)
    sums[:, 1, 0:middle] = spread_sum(sums, masked * total)
    sums[:, 0, middle:] = spread_sum(sums, kept)
    lane = lax.broadcasted_iota(jnp.int32, (1, lanes), 1)
    told = jnp.zeros((1, lanes), FULL)
    for n in range(images):
        told = jnp.where(lane == n, sizes[0, n].astype(FULL), told)
    sums[:, 1, middle:] = jnp.broadcast_to(told, (sums.shape[0], lanes))
    edges_of(dims, place, total, near, far)


def spread_sum(copies, values):
    total = jnp.sum(values, axis=0, keepdims=True)
    return jnp.broadcast_to(total, (copies.shape[0], total.shape[1]))


def fetch(weight, held, sems):
    def load(i, j):
        return pltpu.make_async_copy(weight.at[i, j], held.at[i, j], sems.at[i, j])

    for j in range(3):
        for i in range(3):
            load(i, j).start()

    def tap(i, j):
        load(i, j).wait()
        return held[i, j]

    return tap


def put_sums(dims, place, at, values, others, sent, kept):
    chunk, half = values.shape[1], sent.shape[1]
    span = pl.ds(at % half, chunk)
    mine = (place[0, 0] % 2 == 1) == (at >= half)
    for k, value in enumerate((values, others)):
        total = jnp.sum(value, axis=0, keepdims=True)
        kept[k : k + 1, span] = jnp.where(mine, total, kept[k : k + 1, span])
        sent[k : k + 1, span] = jnp.where(mine, sent[k : k + 1, span], total)


def take_sums(place, at, chunk, mine, other):
    half = mine.shape[2]
    span = pl.ds(at % half, chunk)
    here = (place[0, 0] % 2 == 1) == (at >= half)
    return jnp.where(here, jnp.sum(mine[:, :, span], axis=0), jnp.sum(other[:, :, span], axis=0))


def affine(sums, count, gain, bias):
    average = sums[0:1] / count
    inv_std = lax.rsqrt(sums[1:2] / count - average * average + EPSILON)
    scale = inv_std * gain
    return average, inv_std, scale, bias - average * scale


def mid_forward(
    dims, place, came, params, first, near, far, mask, mask_above, mask_below, weight,
    split, second, sums, sums_first, sizes, held, sems,
):
    tap = fetch(weight, held, sems)
    middle = first.shape[1]
    totals = jnp.sum(came[...], axis=0)
    sums_first[...] = totals
    for y in range(2):
        sizes[y : y + 1] = came[place[0, 1] + y * place[0, 2], 1:2, middle:]
    count = totals[0:1, middle : middle + 1]
    _, _, scale, shift = affine(totals[:, 0:middle], count, params[0:1], params[1:2])

    def act(hidden, inside):
        pre = hidden * scale + shift
        return pre * logistic(pre) * wide(inside[...], pre)

    odd = place[0, 0] % 2 == 1
    centre = act(first[...], mask)
    above = act(jnp.where(odd, near[...], far[...]), mask_above)
    below = act(jnp.where(odd, far[...], near[...]), mask_below)
    three = spread(*dims, centre, above, below)
    x3 = [part.astype(LOW) for part in three]
    flat_rows(dims, centre, split)
    total = None
    for j in range(3):
        part = None
        for i in range(3):
            term = jnp.dot(x3[i], tap(i, j), preferred_element_type=FULL)
            part = term if part is None else part + term
        part = shifted(part, j - 1) if j != 1 else part
        total = part if total is None else total + part
    second[...] = total
    masked = total * wide(mask[...], total)
    sums[:, 0] = spread_sum(sums, masked)
    sums[:, 1] = spread_sum(sums, masked * total)


def flat_rows(dims, value, out):
    images, height, width = dims
    value = value.reshape(images, height, width, -1)
    for r in range(height):
        out[r] = value[:, r].reshape(images * width, -1).astype(LOW)


def flat_halves(dims, place, value, sent, kept):
    quarter = value.shape[1] // 4
    odd, high = place[0, 0] % 2 == 1, place[0, 3] == 1
    parts = [value[:, k * quarter : (k + 1) * quarter] for k in range(4)]
    parts[1], parts[2] = jnp.where(odd, parts[2], parts[1]), jnp.where(odd, parts[1], parts[2])
    one, two = jnp.concatenate(parts[:2], axis=1), jnp.concatenate(parts[2:], axis=1)
    flat_rows(dims, jnp.where(high, one, two), sent)
    flat_rows(dims, jnp.where(high, two, one), kept)


def out_forward(
    dims, place, sums_first, came, params_mid, second, mask, weight,
    act, normed_sent, normed_kept, third, sums_sent, sums_kept, sums_second,
):
    middle = second.shape[1]
    totals = jnp.sum(came[...], axis=0)
    sums_second[...] = totals
    count = sums_first[0:1, middle : middle + 1]
    average, inv_std, scale, shift = affine(totals, count, params_mid[0:1], params_mid[1:2])
    hidden = second[...]
    pre = hidden * scale + shift
    inside = wide(mask[...], hidden)
    act[...] = (pre * logistic(pre) * inside).astype(LOW)
    flat_halves(dims, place, (hidden - average) * inv_std, normed_sent, normed_kept)
    for at in range(0, third.shape[1], middle):
        span = pl.ds(at, middle)
        total = jnp.dot(act[...], weight[:, span], preferred_element_type=FULL)
        third[:, span] = total
        masked = total * inside
        put_sums(dims, place, at, masked, masked * total, sums_sent, sums_kept)


def out_result(
    dims, place, sums_first, came, other, params_out, third, features, out_grad, pool_grad, areas, mask,
    result, pooled, grad, sums_sent, sums_kept, sums_third,
):
    images, height, width = dims
    chunk = sums_first.shape[1] - mask.shape[1]
    count = sums_first[0:1, chunk : chunk + 1]
    inside = jnp.concatenate([mask[...]] * (chunk // mask.shape[1]), axis=1)
    area = jnp.concatenate([areas[...]] * (chunk // mask.shape[1]), axis=1)
    for at in range(0, third.shape[1], chunk):
        span = pl.ds(at, chunk)
        totals = take_sums(place, at, chunk, came, other)
        sums_third[:, span] = totals
        average, inv_std, _, _ = affine(totals, count, 1.0, 0.0)
        normed = (third[:, span] - average) * inv_std
        summed = params_out[0:1, span] * normed + params_out[1:2, span] + features[:, span].astype(FULL)
        gate = logistic(summed)
        value = summed * gate * inside
        result[:, span] = value.astype(LOW)
        pooled[:, span] = jnp.sum(value.reshape(images, height * width, chunk), axis=1)
        share = (pool_grad[:, span] / area)[:, None]
        total = out_grad[:, span].astype(FULL).reshape(images, height * width, chunk) + share
        total = total.reshape(inside.shape) * inside * (gate * (1.0 + summed * (1.0 - gate)))
        grad[:, span] = total
        put_sums(dims, place, at, total, total * normed, sums_sent, sums_kept)


def out_backward(
    dims, place, sums_first, sums_second, sums_third, came, other, params_mid, params_out, third, grad, second,
    mask, weight, third_sent, third_kept, pre_grad, rows_sent, rows_kept, near, far, sums, sums_out, lows,
):
    chunk = second.shape[1]
    count = sums_first[0:1, chunk : chunk + 1]
    inside = wide(mask[...], second)
    back = None
    for at in range(0, third.shape[1], chunk):
        span = pl.ds(at, chunk)
        average, inv_std, scale, _ = affine(sums_third[:, span], count, params_out[0:1, span], 0.0)
        normed = (third[:, span] - average) * inv_std
        totals = take_sums(place, at, chunk, came, other)
        sums_out[:, span] = totals
        mean = (totals[0:1] + normed * totals[1:2]) / count
        low = (inside * scale * (grad[:, span] - mean)).astype(LOW)
        lows[:, span] = low
        part = lax.dot_general(
            low, weight[:, span], (((1,), (1,)), ((), ())), preferred_element_type=FULL
        )
        back = part if back is None else back + part
    average, inv_std, scale, shift = affine(sums_second[...], count, params_mid[0:1], params_mid[1:2])
    hidden = second[...]
    back = back * inside * slope(hidden * scale + shift)
    pre_grad[...] = back
    flat_halves(dims, place, back, rows_sent, rows_kept)
    odd, half = place[0, 0] % 2 == 1, third.shape[1] // 2
    one, two = lows[:, 0:half], lows[:, half:]
    third_sent[...] = jnp.where(odd, one, two)
    third_kept[...] = jnp.where(odd, two, one)
    sums[:, 0] = spread_sum(sums, back)
    normed = (hidden - average) * inv_std
    sums[:, 1] = spread_sum(sums, back * normed)
    edges_of(dims, place, jnp.concatenate([back, normed], axis=1), near, far)


def mid_weights(
    place, sizes, sums_first, sums_second, sums_grad, params_mid,
    acts_mine, acts_came, normed_mine, normed_came, grads_mine, grads_came, sent, kept, left, right,
):
    groups, _, size, channels = kept.shape
    pixels = acts_mine.shape[2]
    images = sizes.shape[1]
    width = pixels // images
    swapped, high = place[0, 0] == 1, place[0, 3] == 1
    middle = sums_grad.shape[1]
    count = sums_first[0:1, middle : middle + 1]
    span = pl.ds(pl.multiple_of(place[0, 1] * channels, channels), channels)
    average = sums_second[0:1, span] / count
    inv_std = lax.rsqrt(sums_second[1:2, span] / count - average * average + EPSILON)
    scale = inv_std * params_mid[0:1, span]
    mean_grad, mean_gain = sums_grad[0:1, span] / count, sums_grad[1:2, span] / count
    column = lax.broadcasted_iota(jnp.int32, (width, channels), 0)
    for y in range(2):
        for x in range(2):
            for c in range(2):
                spot = jnp.where(swapped, 2 * y + c, 2 * x + c)
                here = jnp.where(swapped, x, y) == place[0, 2]
                four = 2 * x + y if c else 2 * y + x
                own = place[0, 0] == c
                rows = pl.ds(((2 * y + x) * 2 + c) * pixels, pixels)
                for r in range(2):
                    left[r, rows, :] = jnp.where(here, acts_mine[spot, r], acts_came[spot, r])
                    row = (2 * x + c) * 2 + r
                    inside = []
                    for n in range(images):
                        extent = jnp.where(row < sizes[y, n], sizes[y, n], 0)
                        inside.append(jnp.where(column < extent, 1.0, 0.0))
                    value = jnp.where(own, grads_mine[four, r], grads_came[four, r]).astype(FULL)
                    normed = jnp.where(own, normed_mine[four, r], normed_came[four, r])
                    value = value - (mean_grad + normed.astype(FULL) * mean_gain)
                    value = value * scale * jnp.concatenate(inside, axis=0)
                    right[r, rows, 0:channels] = value.astype(LOW)
    for r in range(2):
        grad = right[r, :, 0:channels].astype(FULL)
        right[r, :, channels : 2 * channels] = shifted(grad, 1).astype(LOW)
        right[r, :, 2 * channels :] = shifted(grad, -1).astype(LOW)
    span, image = 3 * pixels, 4 * pixels

    def product(r_left, at_left, r_right, at_right, count):
        return lax.dot_general(
            left[r_left, pl.ds(at_left, count), :],
            right[r_right, pl.ds(at_right, count), :],
            (((0,), (0,)), ((), ())),
            preferred_element_type=FULL,
        )

    def crossed(r_left, r_right, skip_left, skip_right):
        part = product(r_left, 0, r_right, 0, 2 * image)
        for y in range(2):
            part = part + product(
                r_right, y * image + skip_left, r_left, y * image + skip_right, span
            )
        return part

    taps = (
        crossed(0, 1, 0, pixels),
        product(0, 0, 0, 0, 2 * image) + product(1, 0, 1, 0, 2 * image),
        crossed(1, 0, pixels, 0),
    )
    for i in range(3):
        for j, place in ((1, 0), (0, 1), (2, 2)):
            part = taps[i][:, place * channels : (place + 1) * channels]
            one = part[0 : groups * size].reshape(groups, size, channels)
            two = part[groups * size :].reshape(groups, size, channels)
            sent[:, 3 * i + j] = jnp.where(high, one, two).astype(LOW)
            kept[:, 3 * i + j] = jnp.where(high, two, one)


def mid_assemble(odd, mine, other, total):
    quarters, groups, taps, size, lanes = mine.shape
    half = groups * size
    swapped = odd[0, 0] == 1
    for t in range(taps):
        for q, turned in enumerate((0, 2, 1, 3)):
            span = pl.ds(q * lanes, lanes)
            even = jnp.where(swapped, other[q, :, t], mine[q, :, t])
            total[t, 0:half, span] = even.astype(FULL).reshape(half, lanes)
            uneven = jnp.where(swapped, mine[turned, :, t], other[turned, :, t])
            total[t, half:, span] = uneven.astype(FULL).reshape(half, lanes)


def mid_backward(
    dims, place, sums_first, sums_second, came, params, params_mid, grad, near, far,
    second, first, mask, mask_above, mask_below, weight, pre_grad, low_grad, sums, sums_mid, held, sems,
):
    tap = fetch(weight, held, sems)
    middle = first.shape[1]
    count = sums_first[0:1, middle : middle + 1]
    totals = jnp.sum(came[...], axis=0)
    sums_mid[...] = totals
    average, inv_std, scale, shift = affine(sums_second[...], count, params_mid[0:1], params_mid[1:2])
    mean_grad, mean_gain = totals[0:1] / count, totals[1:2] / count

    def normed_grad(value, normed, inside):
        return wide(inside[...], value) * scale * (value - (mean_grad + normed * mean_gain))

    odd = place[0, 0] % 2 == 1

    def beside(one, other, inside):
        value = jnp.where(odd, one[...], other[...]).astype(FULL)
        return normed_grad(value[:, 0:middle], value[:, middle:], inside)

    centre = normed_grad(grad[...], (second[...] - average) * inv_std, mask)
    above = beside(near, far, mask_above)
    below = beside(far, near, mask_below)
    three = spread(*dims, centre, above, below)
    average, inv_std, scale, shift = affine(sums_first[:, 0:middle], count, params[0:1], params[1:2])
    low = [part.astype(LOW) for part in three]
    total = None
    for j in range(3):
        part = None
        for i in range(3):
            term = lax.dot_general(
                low[2 - i], tap(i, j), (((1,), (1,)), ((), ())), preferred_element_type=FULL
            )
            part = term if part is None else part + term
        part = shifted(part, 1 - j) if j != 1 else part
        total = part if total is None else total + part
    hidden = first[...]
    total = total * wide(mask[...], total) * slope(hidden * scale + shift)
    pre_grad[...] = total
    low_grad[...] = total.astype(LOW)
    sums[:, 0] = spread_sum(sums, total)
    sums[:, 1] = spread_sum(sums, total * ((hidden - average) * inv_std))


def contract_in(left, right):
    return lax.dot_general(left, right, (((0,), (0,)), ((), ())), preferred_element_type=FULL)


def put_halves(place, total, sent, kept):
    half = total.shape[0] // 2
    high = place[0, 3] == 1
    one, two = total[0:half], total[half:]
    sent[...] = jnp.where(high, one, two).astype(LOW)
    kept[...] = jnp.where(high, two, one)


def first_backward(
    place, sums_first, came, params, first, grad, mask, first_other, grad_other, mask_other, features,
    low, sums_in, sent, kept, both,
):
    pixels, middle = first.shape
    count = sums_first[0:1, middle : middle + 1]
    totals = jnp.sum(came[...], axis=0)
    sums_in[...] = totals
    average, inv_std, scale, _ = affine(sums_first[:, 0:middle], count, params[0:1], 0.0)
    pairs = ((first, grad, mask), (first_other, grad_other, mask_other))
    for k, (hidden, source, inside) in enumerate(pairs):
        normed = (hidden[...] - average) * inv_std
        value = source[...].astype(FULL) - (totals[0:1] + normed * totals[1:2]) / count
        both[k * pixels : (k + 1) * pixels] = (wide(inside[...], value) * scale * value).astype(LOW)
    low[...] = both[0:pixels]
    put_halves(place, contract_in(features[...], both[...]), sent, kept)


def out_weights(place, act, act_other, third, third_other, sent, kept):
    total = contract_in(act[...], third[...]) + contract_in(act_other[...], third_other[...])
    put_halves(place, total, sent, kept)


def assemble(odd, mine, other, shape):
    groups, taps, size, lanes = shape
    quarters = mine.shape[0] // (groups * taps * size)
    channels = quarters * lanes
    step = 3
    pieces = pl.BlockSpec((quarters, groups, step, size, lanes), lambda t: (0, 0, t, 0, 0))
    return pl.pallas_call(
        mid_assemble,
        grid=(taps // step,),
        out_shape=jax.ShapeDtypeStruct((taps, channels, channels), FULL),
        in_specs=[pl.BlockSpec(memory_space=pltpu.SMEM), pieces, pieces],
        out_specs=pl.BlockSpec((step, channels, channels), lambda t: (t, 0, 0)),
        compiler_params=pltpu.CompilerParams(vmem_limit_bytes=48 * MIB),
    )(
        odd,
        mine.reshape(quarters, groups, taps, size, lanes),
        other.reshape(quarters, groups, taps, size, lanes),
    )


def halves(value, step):
    _, mine = step
    return half_of(value, 1 - mine, 3), half_of(value, mine, 3)


def contract(left, right):
    return lax.dot_general(left, right, (((0,), (0,)), ((), ())), preferred_element_type=FULL)


def times_transpose(left, weights):
    return lax.dot_general(left, weights, (((1,), (1,)), ((), ())), preferred_element_type=FULL)


def per_device(
    features,
    weight_in,
    gain_in,
    bias_in,
    weight_mid,
    gain_mid,
    bias_mid,
    weight_out,
    gain_out,
    bias_out,
    map_size,
    out_grad,
    pool_grad,
):
    images, height, width, channels = features.shape
    middle = weight_mid.shape[3]
    dims = (images, height, width)
    pixels = images * height * width

    count = lax.axis_size(AXES)
    place = lax.axis_index(ROWS).astype(jnp.int32)
    index = flat_index()
    rows_count = lax.axis_size(ROWS)
    base = index - lax.axis_index("img") % 2 * rows_count

    count = lax.axis_size(AXES)
    flat_features = features.reshape(pixels, channels)
    params_out = jnp.stack([gain_out, bias_out])
    steps = plan()
    core, mine, far_steps = steps[0], steps[0][1], steps[3:]
    place = jnp.stack([place, base, jnp.int32(rows_count), steps[1][1]]).astype(jnp.int32)[None]
    plane, narrow, broad, large = (pixels, middle), (2, middle), (2, channels), (pixels, channels)
    edge, split_rows = (images * width, middle), (height, images * width, middle)
    half_broad = (2, channels // 2)
    half_rows = (height, images * width, middle // 2)
    taps = [pltpu.VMEM(weight_mid.shape, LOW), pltpu.SemaphoreType.DMA((3, 3))]

    first, near, far, sums, params, params_mid, areas, mask, mask_other, mask_above, mask_below = call(
        lambda *refs: first_forward(dims, *refs),
        [
            (plane, FULL),
            (edge, FULL),
            (edge, FULL),
            ((count, 2, middle + LANES), FULL),
            (narrow, FULL),
            (narrow, FULL),
            ((images, LANES), FULL),
            ((pixels, LANES), FULL),
            ((pixels, LANES), FULL),
            ((images * width, LANES), FULL),
            ((images * width, LANES), FULL),
        ],
        place,
        map_size[None],
        gain_in[None],
        bias_in[None],
        gain_mid[None],
        bias_mid[None],
        flat_features,
        weight_in,
        scratch=[
            pltpu.SMEM((1, images), jnp.int32),
            pltpu.VMEM((4, 1, middle), FULL),
            pltpu.VMEM((pixels, channels), LOW),
            pltpu.VMEM((channels, middle), LOW),
            pltpu.SemaphoreType.DMA((5,)),
            pltpu.SemaphoreType.DMA((2, 4)),
        ],
        left=(1, 2, 3, 4, 5, 6, 7),
        limit=60,
    )
    near, far = trade(near, far)
    came, near, far = tie(everyone(sums), near, far)
    split, second, sums, sums_first, sizes = call(
        lambda *refs: mid_forward(dims, *refs),
        [
            (split_rows, LOW),
            (plane, FULL),
            ((count, 2, middle), FULL),
            ((2, middle + LANES), FULL),
            ((2, LANES), FULL),
        ],
        place,
        came,
        params,
        first,
        near,
        far,
        mask,
        mask_above,
        mask_below,
        weight_mid,
        scratch=taps,
        left=(9,),
    )
    acts = swap(half_of(split, 1 - mine, 2), core[0])
    came, acts, first_other = tie(everyone(sums), acts, swap(first, core[0]))
    second_act, normed_sent, normed_kept, third, sums_sent, sums_kept, sums_second = call(
        lambda *refs: out_forward(dims, *refs),
        [
            (plane, LOW),
            (half_rows, LOW),
            (half_rows, LOW),
            (large, FULL),
            (half_broad, FULL),
            (half_broad, FULL),
            (narrow, FULL),
        ],
        place,
        sums_first,
        came,
        params_mid,
        second,
        mask,
        weight_out,
    )
    acts = stack(mine, half_of(split, mine, 2), acts)
    features_came = swap(half_of(flat_features, 1 - mine, 1), core[0])
    came, came_other, acts_came, normed_came, act_other, features_came = tie(
        *everyone_wide(sums_sent, sums_kept, core),
        swap(acts, steps[1][0]),
        swap(normed_sent[None], steps[1][0]),
        swap(second_act, core[0]),
        features_came,
    )
    result, pooled, grad_summed, sums_sent, sums_kept, sums_third = call(
        lambda *refs: out_result(dims, *refs),
        [
            (large, LOW),
            ((images, channels), FULL),
            (large, FULL),
            (half_broad, FULL),
            (half_broad, FULL),
            (broad, FULL),
        ],
        place,
        sums_first,
        came,
        came_other,
        params_out,
        third,
        flat_features,
        out_grad.reshape(pixels, channels),
        pool_grad,
        areas,
        mask,
    )

    acts = merge(acts, acts_came, steps[1])
    normed_sent, normed_kept = halves(merge(normed_kept[None], normed_came, steps[1]), steps[2])
    sums_sent, acts, normed_sent = tie(sums_sent, acts, normed_sent)
    features_pair = jnp.concatenate([half_of(flat_features, mine, 1), features_came])
    came, came_other, acts_came, features_pair = tie(
        *everyone_wide(sums_sent, sums_kept, core),
        swap(acts, steps[2][0]),
        features_pair,
    )
    normed_came = swap(normed_sent, steps[2][0])
    third_sent, third_kept, grad_second_pre, grads_sent, grads_kept, near, far, sums, sums_out = call(
        lambda *refs: out_backward(dims, *refs),
        [
            ((pixels, channels // 2), LOW),
            ((pixels, channels // 2), LOW),
            (plane, FULL),
            (half_rows, LOW),
            (half_rows, LOW),
            ((edge[0], 2 * middle), LOW),
            ((edge[0], 2 * middle), LOW),
            ((count, 2, middle), FULL),
            (broad, FULL),
        ],
        place,
        sums_first,
        sums_second,
        sums_third,
        came,
        came_other,
        params_mid,
        params_out,
        third,
        grad_summed,
        second,
        mask,
        weight_out,
        scratch=[pltpu.VMEM(large, LOW)],
    )

    near, far = trade(near, far)
    sums = everyone(sums)
    came = swap(grads_sent[None], steps[1][0])
    sent, kept = halves(merge(grads_kept[None], came, steps[1]), steps[2])
    came = swap(sent, steps[2][0])
    third_came = swap(third_sent, core[0])
    out_sent, out_kept = call(
        out_weights,
        [((middle // 2, channels // 2), LOW), ((middle // 2, channels // 2), FULL)],
        place,
        second_act,
        act_other,
        third_kept,
        third_came,
    )
    sums, came, out_sent, near, far = tie(sums, came, out_sent, near, far)
    grads = merge(kept, came, steps[2])
    grad_first_pre, low_grad, sums, sums_mid = call(
        lambda *refs: mid_backward(dims, *refs),
        [(plane, FULL), (plane, LOW), ((count, 2, middle), FULL), (narrow, FULL)],
        place,
        sums_first,
        sums_second,
        sums,
        params,
        params_mid,
        grad_second_pre,
        near,
        far,
        second,
        first,
        mask,
        mask_above,
        mask_below,
        weight_mid,
        scratch=taps,
        left=(14,),
    )
    sums, normed_came = tie(sums, normed_came)
    normed = merge(normed_kept, normed_came, steps[2])
    sums = everyone(sums)
    grad_other = swap(low_grad, core[0])
    grads_came, normed_came = swap(grads, core[0]), swap(normed, core[0])

    odd = (index % 2).astype(jnp.int32).reshape(1, 1)

    def out_chain():
        came = yield out_sent, steps[1][0]
        value = out_kept + came.astype(FULL)
        value = yield from reduce_chain(value, steps[2:])
        value = yield from gather_chain(value.astype(LOW), steps[:0:-1])
        other = yield value, core[0]
        low = mine == 0
        parts = [jnp.where(low, value, other), jnp.where(low, other, value)]
        return jnp.concatenate(parts, axis=1).astype(FULL)

    def mid_chain():
        high, low = steps[1][1], steps[2][1]
        chunk = jnp.where(index % 2 == 0, 2 * high + low, 2 * low + high)
        lanes, deep = grads.shape[-1], acts.shape[-1]
        span = 2 * acts.shape[0] * images * width
        shape = (deep // GROUP // 2, 9, GROUP, lanes)
        sent, kept = call(
            mid_weights,
            [(shape, LOW), (shape, FULL)],
            jnp.stack([index % 2, chunk, steps[2][1], far_steps[0][1]]).astype(jnp.int32)[None],
            sizes[:, :images].astype(jnp.int32),
            sums_first,
            sums_second,
            sums_mid,
            params_mid,
            acts,
            acts_came,
            normed,
            normed_came,
            grads,
            grads_came,
            scratch=[pltpu.VMEM((2, span, deep), LOW), pltpu.VMEM((2, span, 3 * lanes), LOW)],
        )
        came = yield sent.reshape(-1, lanes), far_steps[0][0]
        value = kept.reshape(-1, lanes) + came.astype(FULL)
        value = yield from reduce_chain(value, far_steps[1:])
        value = yield from gather_chain(value.astype(LOW), steps[:0:-1])
        other = yield value, core[0]
        return assemble(odd, value, other, (2 * shape[0], *shape[1:]))

    def in_chain():
        came = yield in_sent, steps[1][0]
        value = in_kept + came.astype(FULL)
        value = yield from reduce_chain(value, steps[2:])
        value = yield from gather_chain(value.astype(LOW), steps[:0:-1])
        other = yield value, core[0]
        return stack(mine, value, other).reshape(-1, middle).astype(FULL)

    chains = Chains()
    mid = mid_chain()
    mid_sent, flips = next(mid)
    came, mid_sent, grad_other, out_sent = tie(sums, mid_sent, grad_other, out_sent)
    chains.begin("out", out_chain(), ())
    chains.begin("mid", mid, (), (mid_sent, flips))
    grad_first, sums_in, in_sent, in_kept = call(
        first_backward,
        [
            (plane, LOW),
            (narrow, FULL),
            ((channels // 4, middle), LOW),
            ((channels // 4, middle), FULL),
        ],
        place,
        sums_first,
        came,
        params,
        first,
        grad_first_pre,
        mask,
        first_other,
        grad_other,
        mask_other,
        features_pair,
        scratch=[pltpu.VMEM((2 * pixels, middle), LOW)],
    )
    chains.slot(held=False)
    chains.begin("in", in_chain(), ())
    grad_features = grad_summed + times_transpose(grad_first, weight_in)
    (grad_features,) = chains.slot(grad_features)
    chains.slot()
    (pooled,) = chains.slot(pooled)
    (pooled,) = chains.slot(sum_rows_axis(pooled))
    pooled = pooled / areas[:, :1]
    for _ in range(0):
        chains.slot()
    while chains.running:
        chains.slot(held=False)
    grad_weight_in, grad_weight_mid, grad_weight_out = (
        chains.results[name] for name in ("in", "mid", "out")
    )
    whole = (images, height, width, channels)
    return (
        result.astype(LOW).reshape(whole),
        pooled,
        grad_features.reshape(whole),
        grad_weight_in,
        sums_in[1],
        sums_in[0],
        grad_weight_mid.reshape(weight_mid.shape),
        sums_mid[1],
        sums_mid[0],
        grad_weight_out,
        sums_out[1],
        sums_out[0],
    )


def solution(mesh):
    images, rows = mesh.devices.shape
    mesh = Mesh(mesh.devices.reshape(images, rows // 2, 2), AXES)
    tiles, single = P("img", ROWS, None, None), P()
    return jax.shard_map(
        per_device,
        mesh=mesh,
        in_specs=(tiles,) + (single,) * 9 + (P("img"), tiles, P("img", None)),
        out_specs=(tiles, P("img", None), tiles) + (single,) * 9,
        check_vma=False,
    )
```

```python
import jax
import jax.numpy as jnp
from jax import lax
from jax.experimental import pallas as pl
from jax.experimental.pallas import tpu as pltpu
from jax.sharding import Mesh
from jax.sharding import PartitionSpec as P

EPSILON = 1e-05
ROWS = ("half", "low")
AXES = ("img", *ROWS)
MIB = 1 << 20
LOW = jnp.bfloat16
FULL = jnp.float32
GROUP = 16
LANES = 128


def swap(value, flips):
    count = lax.axis_size(AXES)
    return lax.ppermute(value, AXES, [(i, i ^ flips[i & 1]) for i in range(count)])


def bits():
    count, found = lax.axis_size(AXES), []
    while (1 << len(found)) < count:
        found.append(1 << len(found))
    return found


def everyone(copies):
    return lax.all_to_all(copies, AXES, 0, 0)


def everyone_wide(sent, kept, low_step):
    mine = lax.all_to_all(kept + swap(sent, low_step[0])[None], AXES[:2], 0, 0)
    return mine, swap(mine, low_step[0])


def tie(*values):
    return lax.optimization_barrier(values)


def flat_index():
    return lax.axis_index("img") * lax.axis_size(ROWS) + lax.axis_index(ROWS)


def plan():
    order = bits()
    steps = [(bit, bit) for bit in order]
    if len(order) >= 3:
        steps[1], steps[2] = (order[1], order[2]), (order[2], order[1])
    index = flat_index()
    low = index % 2
    chosen = []
    for even, odd in steps:
        chosen.append(((even, odd), jnp.where(low == 0, index // even % 2, index // odd % 2)))
    return chosen


def half_of(value, which, axis=0):
    size = value.shape[axis] // 2
    return lax.dynamic_slice_in_dim(value, which * size, size, axis=axis)


def stack(mine, value, other):
    low = mine == 0
    return jnp.stack([jnp.where(low, value, other), jnp.where(low, other, value)])


def scatter_step(value, step):
    _, mine = step
    return half_of(value, 1 - mine).astype(LOW), half_of(value, mine)


def merge(value, other, step):
    return stack(step[1], value, other).reshape((-1,) + value.shape[1:])


def reduce_chain(value, steps):
    for step in steps:
        sent, kept = scatter_step(value, step)
        came = yield sent, step[0]
        value = kept + came.astype(FULL)
    return value


def gather_chain(value, steps):
    for step in steps:
        came = yield value, step[0]
        value = merge(value, came, step)
    return value


class Chains:
    def __init__(self):
        self.running, self.flying, self.results, self.fresh = {}, {}, {}, []

    def begin(self, name, chain, spans, sent=None):
        self.running[name] = (chain, list(spans))
        self.load(name, next(chain) if sent is None else sent)

    def load(self, name, sent):
        spans = self.running[name][1]
        self.flying[name] = [sent, None, spans.pop(0) if spans else 1]

    def slot(self, *extra, held=True):
        due, fresh = [], list(self.fresh)
        for name, flight in self.flying.items():
            if flight[1] is None:
                flight[1] = swap(*flight[0])
            flight[2] -= 1
            if flight[2] <= 0:
                due.append(name)
        done = [self.flying[name][1] for name in due] + list(extra)
        if held:
            done = tie(*done, *(self.results[name] for name in fresh))
            for name, value in zip(fresh, done[len(due) + len(extra) :]):
                self.results[name] = value
            self.fresh = []
        for name, value in zip(due, done):
            try:
                self.load(name, self.running[name][0].send(value))
            except StopIteration as end:
                self.results[name] = end.value
                self.fresh.append(name)
                del self.running[name], self.flying[name]
        return done[len(due) : len(due) + len(extra)]


def sum_rows_axis(value):
    count, bit = lax.axis_size(ROWS), 1
    while bit < count:
        value = value + lax.ppermute(value, ROWS, [(i, i ^ bit) for i in range(count)])
        bit *= 2
    return value


def trade(near, far):
    count = lax.axis_size(ROWS)
    pairs = [(i, i + 1) for i in range(1, count - 1, 2)]
    return (
        lax.ppermute(near, ROWS, [(i, i ^ 1) for i in range(count)]),
        lax.ppermute(far, ROWS, pairs + [(b, a) for a, b in pairs]),
    )


def call(kernel, outs, *args, scratch=(), left=(), limit=60):
    def place(at, arg):
        if at in left:
            return pl.BlockSpec(memory_space=pltpu.HBM)
        return pl.BlockSpec(memory_space=pltpu.SMEM if arg.dtype == jnp.int32 else pltpu.VMEM)

    return pl.pallas_call(
        kernel,
        out_shape=[jax.ShapeDtypeStruct(shape, kind) for shape, kind in outs],
        in_specs=[place(at, arg) for at, arg in enumerate(args)],
        out_specs=[pl.BlockSpec(memory_space=pltpu.VMEM)] * len(outs),
        scratch_shapes=list(scratch),
        compiler_params=pltpu.CompilerParams(vmem_limit_bytes=limit * MIB),
    )(*args)


def logistic(values):
    return 0.5 * jnp.tanh(0.5 * values) + 0.5


def slope(values):
    s = logistic(values)
    return s * (1.0 + values * (1.0 - s))


def shifted(values, by):
    return pltpu.roll(values, (-by) % values.shape[0], 0)


def spread(images, height, width, main, above, below):
    channels = main.shape[-1]
    main = main.reshape(images, height, width, channels)
    above = above.reshape(images, 1, width, channels)
    below = below.reshape(images, 1, width, channels)
    flat = (images * height * width, channels)
    return (
        jnp.concatenate([above, main[:, :-1]], axis=1).reshape(flat),
        main.reshape(flat),
        jnp.concatenate([main[:, 1:], below], axis=1).reshape(flat),
    )


def wide(mask, like):
    return jnp.concatenate([mask] * (like.shape[1] // mask.shape[1]), axis=1)


def edges_of(dims, place, value, near, far):
    images, height, width = dims
    value = value.reshape(images, height, width, -1)
    top = value[:, 0].reshape(images * width, -1)
    bottom = value[:, height - 1].reshape(images * width, -1)
    odd = place[0, 0] % 2 == 1
    near[...] = jnp.where(odd, top, bottom).astype(near.dtype)
    far[...] = jnp.where(odd, bottom, top).astype(far.dtype)


def first_forward(
    dims, place, map_size, gain, bias, gain_mid, bias_mid, features, weight,
    first, near, far, sums, params, params_mid, areas, mask, mask_other, mask_above, mask_below,
    sizes, few, left, right, few_sems, sems,
):
    images, height, width = dims
    lanes = mask.shape[1]
    parts = sems.shape[1]
    deep = left.shape[1] // parts
    small = [pltpu.make_async_copy(map_size, sizes, few_sems.at[0])]
    for k, source in enumerate((gain, bias, gain_mid, bias_mid)):
        small.append(pltpu.make_async_copy(source, few.at[k], few_sems.at[k + 1]))
    for copy in small:
        copy.start()

    def load(k):
        span = pl.ds(k * deep, deep)
        return (
            pltpu.make_async_copy(features.at[:, span], left.at[:, span], sems.at[0, k]),
            pltpu.make_async_copy(weight.at[span, :], right.at[span, :], sems.at[1, k]),
        )

    for k in range(parts):
        for copy in load(k):
            copy.start()
    for copy in small:
        copy.wait()

    def inside(start, count):
        spot = lax.broadcasted_iota(jnp.int32, (count * width, lanes), 0)
        row, column = start + spot // width, spot % width
        parts = []
        for n in range(images):
            size = sizes[0, n]
            here = (row >= 0) & (row < size) & (column < size)
            parts.append(jnp.where(here, 1.0, 0.0))
        return jnp.concatenate(parts, axis=0)

    start = place[0, 0] * height
    kept = inside(start, height)
    mask[...] = kept
    mask_other[...] = inside((place[0, 0] + 1 - 2 * (place[0, 0] % 2)) * height, height)
    mask_above[...] = inside(start - 1, 1)
    mask_below[...] = inside(start + height, 1)
    params[0:1], params[1:2] = few[0], few[1]
    params_mid[0:1], params_mid[1:2] = few[2], few[3]
    spot = lax.broadcasted_iota(jnp.int32, areas.shape, 0)
    area = jnp.zeros(areas.shape, FULL)
    for n in range(images):
        area = jnp.where(spot == n, (sizes[0, n] * sizes[0, n]).astype(FULL), area)
    areas[...] = area
    total = None
    for k in range(parts):
        for copy in load(k):
            copy.wait()
        span = pl.ds(k * deep, deep)
        part = jnp.dot(left[:, span], right[span, :], preferred_element_type=FULL)
        total = part if total is None else total + part
    first[...] = total
    masked = total * wide(kept, total)
    middle = total.shape[1]
    sums[:, 0, 0:middle] = spread_sum(sums, masked)
    sums[:, 1, 0:middle] = spread_sum(sums, masked * total)
    sums[:, 0, middle:] = spread_sum(sums, kept)
    lane = lax.broadcasted_iota(jnp.int32, (1, lanes), 1)
    told = jnp.zeros((1, lanes), FULL)
    for n in range(images):
        told = jnp.where(lane == n, sizes[0, n].astype(FULL), told)
    sums[:, 1, middle:] = jnp.broadcast_to(told, (sums.shape[0], lanes))
    edges_of(dims, place, total, near, far)


def spread_sum(copies, values):
    total = jnp.sum(values, axis=0, keepdims=True)
    return jnp.broadcast_to(total, (copies.shape[0], total.shape[1]))


def fetch(weight, held, sems):
    def load(i, j):
        return pltpu.make_async_copy(weight.at[i, j], held.at[i, j], sems.at[i, j])

    for j in range(3):
        for i in range(3):
            load(i, j).start()

    def tap(i, j):
        load(i, j).wait()
        return held[i, j]

    return tap


def put_sums(dims, place, at, values, others, sent, kept):
    chunk, half = values.shape[1], sent.shape[1]
    span = pl.ds(at % half, chunk)
    mine = (place[0, 0] % 2 == 1) == (at >= half)
    for k, value in enumerate((values, others)):
        total = jnp.sum(value, axis=0, keepdims=True)
        held = jnp.where(mine, total, kept[0, k : k + 1, span])
        kept[:, k, span] = jnp.broadcast_to(held, (kept.shape[0], chunk))
        sent[k : k + 1, span] = jnp.where(mine, sent[k : k + 1, span], total)


def take_sums(place, at, chunk, mine, other):
    half = mine.shape[2]
    span = pl.ds(at % half, chunk)
    here = (place[0, 0] % 2 == 1) == (at >= half)
    return jnp.where(here, jnp.sum(mine[:, :, span], axis=0), jnp.sum(other[:, :, span], axis=0))


def affine(sums, count, gain, bias):
    average = sums[0:1] / count
    inv_std = lax.rsqrt(sums[1:2] / count - average * average + EPSILON)
    scale = inv_std * gain
    return average, inv_std, scale, bias - average * scale


def mid_forward(
    dims, place, came, params, first, near, far, mask, mask_above, mask_below, weight,
    split, second, sums, sums_first, sizes, held, sems,
):
    tap = fetch(weight, held, sems)
    middle = first.shape[1]
    totals = jnp.sum(came[...], axis=0)
    sums_first[...] = totals
    for y in range(2):
        sizes[y : y + 1] = came[place[0, 1] + y * place[0, 2], 1:2, middle:]
    count = totals[0:1, middle : middle + 1]
    _, _, scale, shift = affine(totals[:, 0:middle], count, params[0:1], params[1:2])

    def act(hidden, inside):
        pre = hidden * scale + shift
        return pre * logistic(pre) * wide(inside[...], pre)

    odd = place[0, 0] % 2 == 1
    centre = act(first[...], mask)
    above = act(jnp.where(odd, near[...], far[...]), mask_above)
    below = act(jnp.where(odd, far[...], near[...]), mask_below)
    three = spread(*dims, centre, above, below)
    x3 = [part.astype(LOW) for part in three]
    flat_rows(dims, centre, split)
    total = None
    for j in range(3):
        part = None
        for i in range(3):
            term = jnp.dot(x3[i], tap(i, j), preferred_element_type=FULL)
            part = term if part is None else part + term
        part = shifted(part, j - 1) if j != 1 else part
        total = part if total is None else total + part
    second[...] = total
    masked = total * wide(mask[...], total)
    sums[:, 0] = spread_sum(sums, masked)
    sums[:, 1] = spread_sum(sums, masked * total)


def flat_rows(dims, value, out):
    images, height, width = dims
    value = value.reshape(images, height, width, -1)
    for r in range(height):
        out[r] = value[:, r].reshape(images * width, -1).astype(LOW)


def flat_halves(dims, place, value, sent, kept):
    quarter = value.shape[1] // 4
    odd, high = place[0, 0] % 2 == 1, place[0, 3] == 1
    parts = [value[:, k * quarter : (k + 1) * quarter] for k in range(4)]
    parts[1], parts[2] = jnp.where(odd, parts[2], parts[1]), jnp.where(odd, parts[1], parts[2])
    one, two = jnp.concatenate(parts[:2], axis=1), jnp.concatenate(parts[2:], axis=1)
    flat_rows(dims, jnp.where(high, one, two), sent)
    flat_rows(dims, jnp.where(high, two, one), kept)


def out_forward(
    dims, place, sums_first, came, params_mid, second, mask, weight,
    act, normed_sent, normed_kept, third, sums_sent, sums_kept, sums_second,
):
    middle = second.shape[1]
    totals = jnp.sum(came[...], axis=0)
    sums_second[...] = totals
    count = sums_first[0:1, middle : middle + 1]
    average, inv_std, scale, shift = affine(totals, count, params_mid[0:1], params_mid[1:2])
    hidden = second[...]
    pre = hidden * scale + shift
    inside = wide(mask[...], hidden)
    act[...] = (pre * logistic(pre) * inside).astype(LOW)
    flat_halves(dims, place, (hidden - average) * inv_std, normed_sent, normed_kept)
    for at in range(0, third.shape[1], middle):
        span = pl.ds(at, middle)
        total = jnp.dot(act[...], weight[:, span], preferred_element_type=FULL)
        third[:, span] = total
        masked = total * inside
        put_sums(dims, place, at, masked, masked * total, sums_sent, sums_kept)


def out_result(
    dims, place, sums_first, came, other, params_out, third, features, out_grad, pool_grad, areas, mask,
    result, pooled, grad, sums_sent, sums_kept, sums_third,
):
    images, height, width = dims
    chunk = sums_first.shape[1] - mask.shape[1]
    count = sums_first[0:1, chunk : chunk + 1]
    inside = jnp.concatenate([mask[...]] * (chunk // mask.shape[1]), axis=1)
    area = jnp.concatenate([areas[...]] * (chunk // mask.shape[1]), axis=1)
    for at in range(0, third.shape[1], chunk):
        span = pl.ds(at, chunk)
        totals = take_sums(place, at, chunk, came, other)
        sums_third[:, span] = totals
        average, inv_std, _, _ = affine(totals, count, 1.0, 0.0)
        normed = (third[:, span] - average) * inv_std
        summed = params_out[0:1, span] * normed + params_out[1:2, span] + features[:, span].astype(FULL)
        gate = logistic(summed)
        value = summed * gate * inside
        result[:, span] = value.astype(LOW)
        pooled[:, span] = jnp.sum(value.reshape(images, height * width, chunk), axis=1) / area
        share = (pool_grad[:, span] / area)[:, None]
        total = out_grad[:, span].astype(FULL).reshape(images, height * width, chunk) + share
        total = total.reshape(inside.shape) * inside * (gate * (1.0 + summed * (1.0 - gate)))
        grad[:, span] = total
        put_sums(dims, place, at, total, total * normed, sums_sent, sums_kept)


def out_backward(
    dims, place, sums_first, sums_second, sums_third, came, other, params_mid, params_out, third, grad, second,
    mask, weight, third_sent, third_kept, pre_grad, rows_sent, rows_kept, near, far, sums, sums_out, lows,
):
    chunk = second.shape[1]
    count = sums_first[0:1, chunk : chunk + 1]
    inside = wide(mask[...], second)
    back = None
    for at in range(0, third.shape[1], chunk):
        span = pl.ds(at, chunk)
        average, inv_std, scale, _ = affine(sums_third[:, span], count, params_out[0:1, span], 0.0)
        normed = (third[:, span] - average) * inv_std
        totals = take_sums(place, at, chunk, came, other)
        sums_out[:, span] = totals
        mean = (totals[0:1] + normed * totals[1:2]) / count
        low = (inside * scale * (grad[:, span] - mean)).astype(LOW)
        lows[:, span] = low
        part = lax.dot_general(
            low, weight[:, span], (((1,), (1,)), ((), ())), preferred_element_type=FULL
        )
        back = part if back is None else back + part
    average, inv_std, scale, shift = affine(sums_second[...], count, params_mid[0:1], params_mid[1:2])
    hidden = second[...]
    back = back * inside * slope(hidden * scale + shift)
    pre_grad[...] = back
    flat_halves(dims, place, back, rows_sent, rows_kept)
    odd, half = place[0, 0] % 2 == 1, third.shape[1] // 2
    one, two = lows[:, 0:half], lows[:, half:]
    third_sent[...] = jnp.where(odd, one, two)
    third_kept[...] = jnp.where(odd, two, one)
    sums[:, 0] = spread_sum(sums, back)
    normed = (hidden - average) * inv_std
    sums[:, 1] = spread_sum(sums, back * normed)
    edges_of(dims, place, jnp.concatenate([back, normed], axis=1), near, far)


def mid_weights(
    place, sizes, sums_first, sums_second, sums_grad, params_mid,
    acts_mine, acts_came, normed_mine, normed_came, grads_mine, grads_came, sent, kept, left, right,
):
    groups, _, size, channels = kept.shape
    pixels = acts_mine.shape[2]
    images = sizes.shape[1]
    width = pixels // images
    swapped, high = place[0, 0] == 1, place[0, 3] == 1
    middle = sums_grad.shape[1]
    count = sums_first[0:1, middle : middle + 1]
    span = pl.ds(pl.multiple_of(place[0, 1] * channels, channels), channels)
    average = sums_second[0:1, span] / count
    inv_std = lax.rsqrt(sums_second[1:2, span] / count - average * average + EPSILON)
    scale = inv_std * params_mid[0:1, span]
    mean_grad, mean_gain = sums_grad[0:1, span] / count, sums_grad[1:2, span] / count
    column = lax.broadcasted_iota(jnp.int32, (width, channels), 0)
    for y in range(2):
        for x in range(2):
            for c in range(2):
                spot = jnp.where(swapped, 2 * y + c, 2 * x + c)
                here = jnp.where(swapped, x, y) == place[0, 2]
                four = 2 * x + y if c else 2 * y + x
                own = place[0, 0] == c
                rows = pl.ds(((2 * y + x) * 2 + c) * pixels, pixels)
                for r in range(2):
                    left[r, rows, :] = jnp.where(here, acts_mine[spot, r], acts_came[spot, r])
                    row = (2 * x + c) * 2 + r
                    inside = []
                    for n in range(images):
                        extent = jnp.where(row < sizes[y, n], sizes[y, n], 0)
                        inside.append(jnp.where(column < extent, 1.0, 0.0))
                    value = jnp.where(own, grads_mine[four, r], grads_came[four, r]).astype(FULL)
                    normed = jnp.where(own, normed_mine[four, r], normed_came[four, r])
                    value = value - (mean_grad + normed.astype(FULL) * mean_gain)
                    value = value * scale * jnp.concatenate(inside, axis=0)
                    right[r, rows, 0:channels] = value.astype(LOW)
    for r in range(2):
        grad = right[r, :, 0:channels].astype(FULL)
        right[r, :, channels : 2 * channels] = shifted(grad, 1).astype(LOW)
        right[r, :, 2 * channels :] = shifted(grad, -1).astype(LOW)
    span, image = 3 * pixels, 4 * pixels

    def product(r_left, at_left, r_right, at_right, count):
        return lax.dot_general(
            left[r_left, pl.ds(at_left, count), :],
            right[r_right, pl.ds(at_right, count), :],
            (((0,), (0,)), ((), ())),
            preferred_element_type=FULL,
        )

    def crossed(r_left, r_right, skip_left, skip_right):
        part = product(r_left, 0, r_right, 0, 2 * image)
        for y in range(2):
            part = part + product(
                r_right, y * image + skip_left, r_left, y * image + skip_right, span
            )
        return part

    taps = (
        crossed(0, 1, 0, pixels),
        product(0, 0, 0, 0, 2 * image) + product(1, 0, 1, 0, 2 * image),
        crossed(1, 0, pixels, 0),
    )
    for i in range(3):
        for j, place in ((1, 0), (0, 1), (2, 2)):
            part = taps[i][:, place * channels : (place + 1) * channels]
            one = part[0 : groups * size].reshape(groups, size, channels)
            two = part[groups * size :].reshape(groups, size, channels)
            sent[:, 3 * i + j] = jnp.where(high, one, two).astype(LOW)
            kept[:, 3 * i + j] = jnp.where(high, two, one)


def mid_assemble(odd, mine, other, total):
    quarters, groups, taps, size, lanes = mine.shape
    half = groups * size
    swapped = odd[0, 0] == 1
    for t in range(taps):
        for q, turned in enumerate((0, 2, 1, 3)):
            span = pl.ds(q * lanes, lanes)
            even = jnp.where(swapped, other[q, :, t], mine[q, :, t])
            total[t, 0:half, span] = even.astype(FULL).reshape(half, lanes)
            uneven = jnp.where(swapped, mine[turned, :, t], other[turned, :, t])
            total[t, half:, span] = uneven.astype(FULL).reshape(half, lanes)


def mid_backward(
    dims, place, sums_first, sums_second, came, params, params_mid, grad, near, far,
    second, first, mask, mask_above, mask_below, weight, pre_grad, low_grad, sums, sums_mid, held, sems,
):
    tap = fetch(weight, held, sems)
    middle = first.shape[1]
    count = sums_first[0:1, middle : middle + 1]
    totals = jnp.sum(came[...], axis=0)
    sums_mid[...] = totals
    average, inv_std, scale, shift = affine(sums_second[...], count, params_mid[0:1], params_mid[1:2])
    mean_grad, mean_gain = totals[0:1] / count, totals[1:2] / count

    def normed_grad(value, normed, inside):
        return wide(inside[...], value) * scale * (value - (mean_grad + normed * mean_gain))

    odd = place[0, 0] % 2 == 1

    def beside(one, other, inside):
        value = jnp.where(odd, one[...], other[...]).astype(FULL)
        return normed_grad(value[:, 0:middle], value[:, middle:], inside)

    centre = normed_grad(grad[...], (second[...] - average) * inv_std, mask)
    above = beside(near, far, mask_above)
    below = beside(far, near, mask_below)
    three = spread(*dims, centre, above, below)
    average, inv_std, scale, shift = affine(sums_first[:, 0:middle], count, params[0:1], params[1:2])
    low = [part.astype(LOW) for part in three]
    total = None
    for j in range(3):
        part = None
        for i in range(3):
            term = lax.dot_general(
                low[2 - i], tap(i, j), (((1,), (1,)), ((), ())), preferred_element_type=FULL
            )
            part = term if part is None else part + term
        part = shifted(part, 1 - j) if j != 1 else part
        total = part if total is None else total + part
    hidden = first[...]
    total = total * wide(mask[...], total) * slope(hidden * scale + shift)
    pre_grad[...] = total
    low_grad[...] = total.astype(LOW)
    sums[:, 0] = spread_sum(sums, total)
    sums[:, 1] = spread_sum(sums, total * ((hidden - average) * inv_std))


def contract_in(left, right):
    return lax.dot_general(left, right, (((0,), (0,)), ((), ())), preferred_element_type=FULL)


def put_halves(place, total, sent, kept):
    half = total.shape[0] // 2
    high = place[0, 3] == 1
    one, two = total[0:half], total[half:]
    sent[...] = jnp.where(high, one, two).astype(LOW)
    kept[...] = jnp.where(high, two, one)


def first_backward(
    place, sums_first, came, params, first, grad, mask, first_other, grad_other, mask_other, features,
    low, sums_in, sent, kept, both,
):
    pixels, middle = first.shape
    count = sums_first[0:1, middle : middle + 1]
    totals = jnp.sum(came[...], axis=0)
    sums_in[...] = totals
    average, inv_std, scale, _ = affine(sums_first[:, 0:middle], count, params[0:1], 0.0)
    pairs = ((first, grad, mask), (first_other, grad_other, mask_other))
    for k, (hidden, source, inside) in enumerate(pairs):
        normed = (hidden[...] - average) * inv_std
        value = source[...].astype(FULL) - (totals[0:1] + normed * totals[1:2]) / count
        both[k * pixels : (k + 1) * pixels] = (wide(inside[...], value) * scale * value).astype(LOW)
    low[...] = both[0:pixels]
    put_halves(place, contract_in(features[...], both[...]), sent, kept)


def out_weights(place, act, act_other, third, third_other, sent, kept):
    total = contract_in(act[...], third[...]) + contract_in(act_other[...], third_other[...])
    put_halves(place, total, sent, kept)


def assemble(odd, mine, other, shape):
    groups, taps, size, lanes = shape
    quarters = mine.shape[0] // (groups * taps * size)
    channels = quarters * lanes
    step = 3
    pieces = pl.BlockSpec((quarters, groups, step, size, lanes), lambda t: (0, 0, t, 0, 0))
    return pl.pallas_call(
        mid_assemble,
        grid=(taps // step,),
        out_shape=jax.ShapeDtypeStruct((taps, channels, channels), FULL),
        in_specs=[pl.BlockSpec(memory_space=pltpu.SMEM), pieces, pieces],
        out_specs=pl.BlockSpec((step, channels, channels), lambda t: (t, 0, 0)),
        compiler_params=pltpu.CompilerParams(vmem_limit_bytes=48 * MIB),
    )(
        odd,
        mine.reshape(quarters, groups, taps, size, lanes),
        other.reshape(quarters, groups, taps, size, lanes),
    )


def halves(value, step):
    _, mine = step
    return half_of(value, 1 - mine, 3), half_of(value, mine, 3)


def contract(left, right):
    return lax.dot_general(left, right, (((0,), (0,)), ((), ())), preferred_element_type=FULL)


def times_transpose(left, weights):
    return lax.dot_general(left, weights, (((1,), (1,)), ((), ())), preferred_element_type=FULL)


def per_device(
    features,
    weight_in,
    gain_in,
    bias_in,
    weight_mid,
    gain_mid,
    bias_mid,
    weight_out,
    gain_out,
    bias_out,
    map_size,
    out_grad,
    pool_grad,
):
    images, height, width, channels = features.shape
    middle = weight_mid.shape[3]
    dims = (images, height, width)
    pixels = images * height * width

    count = lax.axis_size(AXES)
    place = lax.axis_index(ROWS).astype(jnp.int32)
    index = flat_index()
    rows_count = lax.axis_size(ROWS)
    base = index - lax.axis_index("img") % 2 * rows_count

    count = lax.axis_size(AXES)
    flat_features = features.reshape(pixels, channels)
    params_out = jnp.stack([gain_out, bias_out])
    steps = plan()
    core, mine, far_steps = steps[0], steps[0][1], steps[3:]
    place = jnp.stack([place, base, jnp.int32(rows_count), steps[1][1]]).astype(jnp.int32)[None]
    plane, narrow, broad, large = (pixels, middle), (2, middle), (2, channels), (pixels, channels)
    edge, split_rows = (images * width, middle), (height, images * width, middle)
    half_broad = (2, channels // 2)
    many_broad = (lax.axis_size(AXES[:2]), *half_broad)
    half_rows = (height, images * width, middle // 2)
    taps = [pltpu.VMEM(weight_mid.shape, LOW), pltpu.SemaphoreType.DMA((3, 3))]

    first, near, far, sums, params, params_mid, areas, mask, mask_other, mask_above, mask_below = call(
        lambda *refs: first_forward(dims, *refs),
        [
            (plane, FULL),
            (edge, FULL),
            (edge, FULL),
            ((count, 2, middle + LANES), FULL),
            (narrow, FULL),
            (narrow, FULL),
            ((images, LANES), FULL),
            ((pixels, LANES), FULL),
            ((pixels, LANES), FULL),
            ((images * width, LANES), FULL),
            ((images * width, LANES), FULL),
        ],
        place,
        map_size[None],
        gain_in[None],
        bias_in[None],
        gain_mid[None],
        bias_mid[None],
        flat_features,
        weight_in,
        scratch=[
            pltpu.SMEM((1, images), jnp.int32),
            pltpu.VMEM((4, 1, middle), FULL),
            pltpu.VMEM((pixels, channels), LOW),
            pltpu.VMEM((channels, middle), LOW),
            pltpu.SemaphoreType.DMA((5,)),
            pltpu.SemaphoreType.DMA((2, 4)),
        ],
        left=(1, 2, 3, 4, 5, 6, 7),
        limit=60,
    )
    near, far = trade(near, far)
    came, near, far = tie(everyone(sums), near, far)
    split, second, sums, sums_first, sizes = call(
        lambda *refs: mid_forward(dims, *refs),
        [
            (split_rows, LOW),
            (plane, FULL),
            ((count, 2, middle), FULL),
            ((2, middle + LANES), FULL),
            ((2, LANES), FULL),
        ],
        place,
        came,
        params,
        first,
        near,
        far,
        mask,
        mask_above,
        mask_below,
        weight_mid,
        scratch=taps,
        left=(9,),
    )
    acts = swap(half_of(split, 1 - mine, 2), core[0])
    came, acts, first_other = tie(everyone(sums), acts, swap(first, core[0]))
    second_act, normed_sent, normed_kept, third, sums_sent, sums_kept, sums_second = call(
        lambda *refs: out_forward(dims, *refs),
        [
            (plane, LOW),
            (half_rows, LOW),
            (half_rows, LOW),
            (large, FULL),
            (half_broad, FULL),
            (many_broad, FULL),
            (narrow, FULL),
        ],
        place,
        sums_first,
        came,
        params_mid,
        second,
        mask,
        weight_out,
    )
    acts = stack(mine, half_of(split, mine, 2), acts)
    features_came = swap(half_of(flat_features, 1 - mine, 1), core[0])
    came, came_other, acts_came, normed_came, act_other, features_came = tie(
        *everyone_wide(sums_sent, sums_kept, core),
        swap(acts, steps[1][0]),
        swap(normed_sent[None], steps[1][0]),
        swap(second_act, core[0]),
        features_came,
    )
    result, pooled, grad_summed, sums_sent, sums_kept, sums_third = call(
        lambda *refs: out_result(dims, *refs),
        [
            (large, LOW),
            ((images, channels), FULL),
            (large, FULL),
            (half_broad, FULL),
            (many_broad, FULL),
            (broad, FULL),
        ],
        place,
        sums_first,
        came,
        came_other,
        params_out,
        third,
        flat_features,
        out_grad.reshape(pixels, channels),
        pool_grad,
        areas,
        mask,
    )

    acts = merge(acts, acts_came, steps[1])
    normed_sent, normed_kept = halves(merge(normed_kept[None], normed_came, steps[1]), steps[2])
    sums_sent, acts, normed_sent = tie(sums_sent, acts, normed_sent)
    features_pair = jnp.concatenate([half_of(flat_features, mine, 1), features_came])
    came, came_other, acts_came, features_pair = tie(
        *everyone_wide(sums_sent, sums_kept, core),
        swap(acts, steps[2][0]),
        features_pair,
    )
    normed_came = swap(normed_sent, steps[2][0])
    third_sent, third_kept, grad_second_pre, grads_sent, grads_kept, near, far, sums, sums_out = call(
        lambda *refs: out_backward(dims, *refs),
        [
            ((pixels, channels // 2), LOW),
            ((pixels, channels // 2), LOW),
            (plane, FULL),
            (half_rows, LOW),
            (half_rows, LOW),
            ((edge[0], 2 * middle), LOW),
            ((edge[0], 2 * middle), LOW),
            ((count, 2, middle), FULL),
            (broad, FULL),
        ],
        place,
        sums_first,
        sums_second,
        sums_third,
        came,
        came_other,
        params_mid,
        params_out,
        third,
        grad_summed,
        second,
        mask,
        weight_out,
        scratch=[pltpu.VMEM(large, LOW)],
    )

    near, far = trade(near, far)
    sums = everyone(sums)
    came = swap(grads_sent[None], steps[1][0])
    sent, kept = halves(merge(grads_kept[None], came, steps[1]), steps[2])
    came = swap(sent, steps[2][0])
    third_came = swap(third_sent, core[0])
    out_sent, out_kept = call(
        out_weights,
        [((middle // 2, channels // 2), LOW), ((middle // 2, channels // 2), FULL)],
        place,
        second_act,
        act_other,
        third_kept,
        third_came,
    )
    sums, came, out_sent, near, far = tie(sums, came, out_sent, near, far)
    grads = merge(kept, came, steps[2])
    grad_first_pre, low_grad, sums, sums_mid = call(
        lambda *refs: mid_backward(dims, *refs),
        [(plane, FULL), (plane, LOW), ((count, 2, middle), FULL), (narrow, FULL)],
        place,
        sums_first,
        sums_second,
        sums,
        params,
        params_mid,
        grad_second_pre,
        near,
        far,
        second,
        first,
        mask,
        mask_above,
        mask_below,
        weight_mid,
        scratch=taps,
        left=(14,),
    )
    sums, normed_came = tie(sums, normed_came)
    normed = merge(normed_kept, normed_came, steps[2])
    sums = everyone(sums)
    grad_other = swap(low_grad, core[0])
    grads_came, normed_came = swap(grads, core[0]), swap(normed, core[0])

    odd = (index % 2).astype(jnp.int32).reshape(1, 1)

    def out_chain():
        came = yield out_sent, steps[1][0]
        value = out_kept + came.astype(FULL)
        value = yield from reduce_chain(value, steps[2:])
        value = yield from gather_chain(value.astype(LOW), steps[:0:-1])
        other = yield value, core[0]
        low = mine == 0
        parts = [jnp.where(low, value, other), jnp.where(low, other, value)]
        return jnp.concatenate(parts, axis=1).astype(FULL)

    def mid_chain():
        high, low = steps[1][1], steps[2][1]
        chunk = jnp.where(index % 2 == 0, 2 * high + low, 2 * low + high)
        lanes, deep = grads.shape[-1], acts.shape[-1]
        span = 2 * acts.shape[0] * images * width
        shape = (deep // GROUP // 2, 9, GROUP, lanes)
        sent, kept = call(
            mid_weights,
            [(shape, LOW), (shape, FULL)],
            jnp.stack([index % 2, chunk, steps[2][1], far_steps[0][1]]).astype(jnp.int32)[None],
            sizes[:, :images].astype(jnp.int32),
            sums_first,
            sums_second,
            sums_mid,
            params_mid,
            acts,
            acts_came,
            normed,
            normed_came,
            grads,
            grads_came,
            scratch=[pltpu.VMEM((2, span, deep), LOW), pltpu.VMEM((2, span, 3 * lanes), LOW)],
        )
        came = yield sent.reshape(-1, lanes), far_steps[0][0]
        value = kept.reshape(-1, lanes) + came.astype(FULL)
        value = yield from reduce_chain(value, far_steps[1:])
        value = yield from gather_chain(value.astype(LOW), steps[:0:-1])
        other = yield value, core[0]
        return assemble(odd, value, other, (2 * shape[0], *shape[1:]))

    def in_chain():
        came = yield in_sent, steps[1][0]
        value = in_kept + came.astype(FULL)
        value = yield from reduce_chain(value, steps[2:])
        value = yield from gather_chain(value.astype(LOW), steps[:0:-1])
        other = yield value, core[0]
        return stack(mine, value, other).reshape(-1, middle).astype(FULL)

    chains = Chains()
    mid = mid_chain()
    mid_sent, flips = next(mid)
    came, mid_sent, grad_other, out_sent = tie(sums, mid_sent, grad_other, out_sent)
    chains.begin("out", out_chain(), ())
    chains.begin("mid", mid, (), (mid_sent, flips))
    grad_first, sums_in, in_sent, in_kept = call(
        first_backward,
        [
            (plane, LOW),
            (narrow, FULL),
            ((channels // 4, middle), LOW),
            ((channels // 4, middle), FULL),
        ],
        place,
        sums_first,
        came,
        params,
        first,
        grad_first_pre,
        mask,
        first_other,
        grad_other,
        mask_other,
        features_pair,
        scratch=[pltpu.VMEM((2 * pixels, middle), LOW)],
    )
    chains.slot(held=False)
    chains.begin("in", in_chain(), ())
    grad_features = grad_summed + times_transpose(grad_first, weight_in)
    (grad_features,) = chains.slot(grad_features)
    chains.slot()
    (pooled,) = chains.slot(pooled)
    (pooled,) = chains.slot(sum_rows_axis(pooled))
    for _ in range(0):
        chains.slot()
    while chains.running:
        chains.slot(held=False)
    grad_weight_in, grad_weight_mid, grad_weight_out = (
        chains.results[name] for name in ("in", "mid", "out")
    )
    whole = (images, height, width, channels)
    return (
        result.astype(LOW).reshape(whole),
        pooled,
        grad_features.reshape(whole),
        grad_weight_in,
        sums_in[1],
        sums_in[0],
        grad_weight_mid.reshape(weight_mid.shape),
        sums_mid[1],
        sums_mid[0],
        grad_weight_out,
        sums_out[1],
        sums_out[0],
    )


def solution(mesh):
    images, rows = mesh.devices.shape
    mesh = Mesh(mesh.devices.reshape(images, rows // 2, 2), AXES)
    tiles, single = P("img", ROWS, None, None), P()
    return jax.shard_map(
        per_device,
        mesh=mesh,
        in_specs=(tiles,) + (single,) * 9 + (P("img"), tiles, P("img", None)),
        out_specs=(tiles, P("img", None), tiles) + (single,) * 9,
        check_vma=False,
    )
```
